32 devices in a mesh: tower: 2 (over x), batch: 4 (over z), tensor: 4 (over y, core).
Axes of the slice: x: 2, y: 2, z: 4, core: 2. Of those that a mesh axis runs over, the one named last changes fastest.
Arguments:
- image_tokens: bfloat16 [9600, 768], P(('tower', 'batch', 'tensor')), may hold values from -6 to 6
- image_gains: float32 [3, 768], replicated, may hold values from 0.25 to 1.75
- image_shifts: float32 [3, 768], replicated, may hold values from -1.8 to 1.8
- image_qkv: bfloat16 [768, 3, 768], P(None, None, 'tensor'), may hold values from -0.21875 to 0.21875
- image_out: bfloat16 [768, 768], P('tensor'), may hold values from -0.875 to 0.875
- image_up: bfloat16 [768, 3072], P(None, 'tensor'), may hold values from -0.21875 to 0.21875
- image_down: bfloat16 [3072, 768], P('tensor'), may hold values from -0.21875 to 0.21875
- image_proj: bfloat16 [768, 512], replicated, may hold values from -0.21875 to 0.21875
- text_tokens: bfloat16 [14784, 512], P(('tower', 'batch', 'tensor')), may hold values from -6 to 6
- text_gains: float32 [3, 512], replicated, may hold values from 0.25 to 1.75
- text_shifts: float32 [3, 512], replicated, may hold values from -1.8 to 1.8
- text_qkv: bfloat16 [512, 3, 512], P(None, None, 'tensor'), may hold values from -0.25 to 0.25
- text_out: bfloat16 [512, 512], P('tensor'), may hold values from -1 to 1
- text_up: bfloat16 [512, 2048], P(None, 'tensor'), may hold values from -0.25 to 0.25
- text_down: bfloat16 [2048, 512], P('tensor'), may hold values from -0.25 to 0.25
- text_proj: bfloat16 [512, 512], replicated, may hold values from -0.25 to 0.25
- caption_lengths: int32 [192], P(('tower', 'batch')), may hold values from 5 to 77, as said below
- logit_scale: float32 [1], replicated, may hold values from 3.3 to 3.9
Outputs:
- image_block: bfloat16 [9600, 768], P(('tower', 'batch', 'tensor'))
- image_input_grad: bfloat16 [9600, 768], P(('tower', 'batch', 'tensor'))
- image_qkv_grad: float32 [768, 3, 768], P(None, None, 'tensor')
- image_out_grad: float32 [768, 768], P('tensor')
- image_up_grad: float32 [768, 3072], P(None, 'tensor')
- image_down_grad: float32 [3072, 768], P('tensor')
- image_gains_grad: float32 [3, 768], replicated
- image_shifts_grad: float32 [3, 768], replicated
- image_proj_grad: float32 [768, 512], replicated
- text_block: bfloat16 [14784, 512], P(('tower', 'batch', 'tensor'))
- text_input_grad: bfloat16 [14784, 512], P(('tower', 'batch', 'tensor'))
- text_qkv_grad: float32 [512, 3, 512], P(None, None, 'tensor')
- text_out_grad: float32 [512, 512], P('tensor')
- text_up_grad: float32 [512, 2048], P(None, 'tensor')
- text_down_grad: float32 [2048, 512], P('tensor')
- text_gains_grad: float32 [3, 512], replicated
- text_shifts_grad: float32 [3, 512], replicated
- text_proj_grad: float32 [512, 512], replicated
- logit_scale_grad: float32 [1], replicated
- loss: float32 [1], replicated
The draws below stay inside these ranges and needn't reach their ends.
Inputs may be any that keep to these rules, and one draw needn't show every extreme that they name: caption_lengths[n] counts the real tokens of caption n; its end-of-text token stands at slot caption_lengths[n] - 1.
All inputs are finite; a program needn't handle non-finite values.
Results may differ from the reference program's by a relative error of at most 0.024.
Values may be sent and summed in bfloat16 or wider, within the bound.
No kernel may reach another device: no remote copies, remote signals or barrier semaphores. Data moves between devices by JAX's collectives and lax.ppermute only.
A program may use at most 192 MiB of HBM per device.

```python
import jax
import jax.numpy as jnp
from jax import lax

D_IMG = 768
FF_IMG = 3072
D_TXT = 512
FF_TXT = 2048
HEAD_DIM = 64
EMBED = 512
PATCHES = 50
CTX = 77
PAIRS_DEV = 24
PAIRS = 192
IMG_ROWS = 9600
CAP_ROWS = 14784


def draw_caption_lengths(key, part):
    key_len, key_spot = jax.random.split(key, 2)
    lengths = jax.random.randint(key_len, (PAIRS,), 5, CTX + 1)
    spots = jax.random.permutation(key_spot, PAIRS)
    places = jnp.arange(PAIRS)
    lengths = jnp.where(places == spots[0], CTX, lengths)
    lengths = jnp.where(places == spots[1], 5, lengths)
    return lengths.astype(jnp.int32)


def block_scale(key, shape, shards, low, top_value):
    def one(position, parts):
        heights = jax.random.uniform(jax.random.fold_in(jax.random.fold_in(key, 6), position), (parts,), jnp.float32, low / len(shards), top_value / len(shards))
        return jnp.repeat(jnp.exp(heights), shape[position] // parts).reshape((-1,) + (1,) * (len(shape) - position - 1))

    factor_of = one(*shards[0])
    for cut in shards[1:]:
        factor_of = factor_of * one(*cut)
    return factor_of


def scatter_about(rng, extent, width, most, cuts=(), held_as=jnp.bfloat16):
    array = jax.random.normal(rng, extent, jnp.float32) * width
    if len(cuts) > 0:
        array = block_scale(rng, extent, cuts, -0.22, 0.18) * array
    return jnp.clip(array, min=-most, max=most).astype(held_as)


def setup_inputs(seed: int = 0) -> dict:
    splits = jax.random.split(jax.random.key(seed), 19)
    image_tokens = scatter_about(splits[0], (IMG_ROWS, D_IMG), 1.0, 6.0, ((0, 32),))
    image_gains = jnp.clip(1.0 + 0.15 * jax.random.normal(splits[1], (3, D_IMG), jnp.float32), 0.25, 1.75)
    image_shifts = scatter_about(splits[2], (3, D_IMG), 0.3, 1.8, (), jnp.float32)
    image_qkv = scatter_about(splits[3], (D_IMG, 3, D_IMG), D_IMG ** -0.5, 0.21875, ((2, 4),))
    image_out = scatter_about(splits[4], (D_IMG, D_IMG), (D_IMG // 16) ** -0.5, 0.875, ((0, 4),))
    image_up = scatter_about(splits[5], (D_IMG, FF_IMG), D_IMG ** -0.5, 0.21875, ((1, 4),))
    image_down = scatter_about(splits[6], (FF_IMG, D_IMG), (FF_IMG // 4) ** -0.5, 0.21875, ((0, 4),))
    image_proj = scatter_about(splits[7], (D_IMG, EMBED), D_IMG ** -0.5, 0.21875)
    text_tokens = scatter_about(splits[8], (CAP_ROWS, D_TXT), 1.0, 6.0, ((0, 32),))
    text_gains = jnp.clip(1.0 + 0.15 * jax.random.normal(splits[9], (3, D_TXT), jnp.float32), 0.25, 1.75)
    text_shifts = scatter_about(splits[10], (3, D_TXT), 0.3, 1.8, (), jnp.float32)
    text_qkv = scatter_about(splits[11], (D_TXT, 3, D_TXT), D_TXT ** -0.5, 0.25, ((2, 4),))
    text_out = scatter_about(splits[12], (D_TXT, D_TXT), (D_TXT // 16) ** -0.5, 1.0, ((0, 4),))
    text_up = scatter_about(splits[13], (D_TXT, FF_TXT), D_TXT ** -0.5, 0.25, ((1, 4),))
    text_down = scatter_about(splits[14], (FF_TXT, D_TXT), (FF_TXT // 4) ** -0.5, 0.25, ((0, 4),))
    text_proj = scatter_about(splits[15], (D_TXT, EMBED), D_TXT ** -0.5, 0.25)
    caption_lengths = draw_caption_lengths(jax.random.fold_in(splits[18], 71), 0)
    logit_scale = jnp.clip(jax.random.uniform(splits[17], (1,), jnp.float32, 3.3, 3.9), 3.3, 3.9)
    return {"image_tokens": image_tokens, "image_gains": image_gains, "image_shifts": image_shifts, "image_qkv": image_qkv, "image_out": image_out, "image_up": image_up, "image_down": image_down, "image_proj": image_proj, "text_tokens": text_tokens, "text_gains": text_gains, "text_shifts": text_shifts, "text_qkv": text_qkv, "text_out": text_out, "text_up": text_up, "text_down": text_down, "text_proj": text_proj, "caption_lengths": caption_lengths, "logit_scale": logit_scale}


@jax.custom_vjp
def low(v):
    return lax.optimization_barrier(v.astype(jnp.bfloat16)).astype(jnp.float32)

@jax.custom_vjp
def low_back(v):
    return v

def low_keep(v):
    return (low(v), None)

def low_pass(kept, grad):
    return (grad,)

def back_keep(v):
    return (v, None)

def back_low(kept, grad):
    return (low(grad),)
low.defvjp(low_keep, low_pass)
low_back.defvjp(back_keep, back_low)
best_precision = lax.Precision.HIGHEST

def layer_norm(values, gain_row, shift_row):
    row_mean = lax.optimization_barrier(jnp.mean(values, axis=-1, keepdims=True))
    centred = values - row_mean
    variance = lax.optimization_barrier(jnp.mean(centred * centred, axis=-1, keepdims=True))
    return centred * lax.rsqrt(variance + 1e-05) * gain_row + shift_row

def block_pass(tokens, allowed, weight_set, length):
    gain_rows, shifts, w_qkv, w_out, w_up, w_down = weight_set
    row_count, feature_width = tokens.shape
    seq_count = row_count // length
    head_count = feature_width // HEAD_DIM
    normed_one = low(layer_norm(tokens, gain_rows[0], shifts[0]))
    qkv_rows = low_back(low(jnp.dot(normed_one, w_qkv.reshape(feature_width, 3 * feature_width), precision=best_precision)))
    split_heads = qkv_rows.reshape(seq_count, length, 3, head_count, HEAD_DIM)
    query_part = split_heads[:, :, 0]
    key_part = split_heads[:, :, 1]
    value_part = split_heads[:, :, 2]
    scores = low_back(jnp.einsum('nqhd,nkhd->nhqk', query_part, key_part, precision=best_precision) * HEAD_DIM ** (-0.5))
    scores = jnp.where(allowed[:, None], scores, -1000000000.0)
    row_top = lax.optimization_barrier(jnp.max(scores, axis=-1, keepdims=True))
    weights = jnp.exp(scores - row_top)
    soft_probs = low(weights / lax.optimization_barrier(jnp.sum(weights, axis=-1, keepdims=True)))
    attn_mix = jnp.einsum('nhqk,nkhd->nqhd', soft_probs, value_part, precision=best_precision)
    attn_mix = low_back(low(attn_mix.reshape(row_count, feature_width)))
    middle = tokens + low_back(jnp.dot(attn_mix, w_out, precision=best_precision))
    normed_two = low(layer_norm(middle, gain_rows[1], shifts[1]))
    pre_act = low_back(jnp.dot(normed_two, w_up, precision=best_precision))
    hidden = low(pre_act * jax.nn.sigmoid(1.702 * pre_act))
    return middle + low_back(jnp.dot(hidden, w_down, precision=best_precision))

def tower_pass(tokens, allowed, weight_set, length):
    groups = tokens.shape[0] // (PAIRS_DEV * length)
    blocks = tokens.reshape(groups, PAIRS_DEV * length, tokens.shape[1])
    group_masks = allowed.reshape(groups, PAIRS_DEV, length, length)

    def group_step(group_pair):
        return block_pass(group_pair[0], group_pair[1], weight_set, length)
    outputs = lax.map(jax.checkpoint(group_step), (blocks, group_masks))
    return outputs.reshape(tokens.shape)

def head_pass(pooled, gain_rows, shifts, proj_weight):
    normed = low(layer_norm(pooled, gain_rows[2], shifts[2]))
    embedding = low_back(jnp.dot(normed, proj_weight, precision=best_precision))
    return low(embedding * lax.rsqrt(lax.optimization_barrier(jnp.sum(embedding * embedding, axis=-1, keepdims=True)) + 1e-06))

def log_total(values, axis):
    row_top = lax.optimization_barrier(jnp.max(values, axis=axis, keepdims=True))
    return jnp.squeeze(row_top, axis) + jnp.log(lax.optimization_barrier(jnp.sum(jnp.exp(values - row_top), axis=axis)))

def reference(image_tokens, image_gains, image_shifts, image_qkv, image_out, image_up, image_down, image_proj, text_tokens, text_gains, text_shifts, text_qkv, text_out, text_up, text_down, text_proj, caption_lengths, logit_scale):
    positions = jnp.arange(CTX, dtype=jnp.int32)
    allowed_text = (positions[None, None, :] <= positions[None, :, None]) & (positions[None, None, :] < caption_lengths[:, None, None])
    allowed_image = jnp.ones((PAIRS, PATCHES, PATCHES), dtype=jnp.bool_)
    end_rows = (jnp.arange(PAIRS, dtype=jnp.int32) * CTX + caption_lengths - 1).astype(jnp.int32)

    def objective(image_x, image_g, image_s, image_q, image_o, image_u, image_d, image_p, text_x, text_g, text_s, text_q, text_o, text_u, text_d, text_p, scale_log):
        image_final = tower_pass(image_x, allowed_image, (image_g, image_s, image_q, image_o, image_u, image_d), PATCHES)
        text_final = tower_pass(text_x, allowed_text, (text_g, text_s, text_q, text_o, text_u, text_d), CTX)
        image_unit = head_pass(image_final[::PATCHES], image_g, image_s, image_p)
        text_unit = head_pass(text_final[end_rows], text_g, text_s, text_p)
        logits = low_back(jnp.exp(scale_log[0]) * jnp.dot(image_unit, text_unit.T, precision=best_precision))
        diag_vals = jnp.diagonal(logits)
        objective_value = 0.5 * jnp.sum(log_total(logits, 1) - diag_vals) + 0.5 * jnp.sum(log_total(logits, 0) - diag_vals)
        return (objective_value, (image_final, text_final))
    floats = tuple((array_in.astype(jnp.float32) for array_in in (image_tokens, image_gains, image_shifts, image_qkv, image_out, image_up, image_down, image_proj, text_tokens, text_gains, text_shifts, text_qkv, text_out, text_up, text_down, text_proj, logit_scale)))
    objective_value, pullback, finals = jax.vjp(objective, *floats, has_aux=True)
    gradients = pullback(jnp.ones_like(objective_value))
    return (finals[0].astype(jnp.bfloat16), gradients[0].astype(jnp.bfloat16), gradients[3], gradients[4], gradients[5], gradients[6], gradients[1], gradients[2], gradients[7], finals[1].astype(jnp.bfloat16), gradients[8].astype(jnp.bfloat16), gradients[11], gradients[12], gradients[13], gradients[14], gradients[9], gradients[10], gradients[15], gradients[16], (objective_value / PAIRS).reshape(1))
```

```python
import jax
import jax.numpy as jnp
from jax import lax
from jax.sharding import Mesh, PartitionSpec as P

HEAD = 64
PATCHES = 50
CTX = 77
EPS = 1e-05
F32 = jnp.float32
BF16 = jnp.bfloat16
HIGH = lax.Precision.HIGHEST
SCALE = HEAD**-0.5
SWAP = [(0, 1), (1, 0)]


def nn(a, b):
    return lax.dot_general(a, b, (((1,), (0,)), ((), ())), preferred_element_type=F32)


def nt(a, b):
    return lax.dot_general(a, b, (((1,), (1,)), ((), ())), preferred_element_type=F32)


def tn(a, b):
    return lax.dot_general(a, b, (((0,), (0,)), ((), ())), preferred_element_type=F32)


def exact_nn(a, b):
    return lax.dot_general(
        a, b, (((1,), (0,)), ((), ())), precision=HIGH, preferred_element_type=F32
    )


def exact_tn(a, b):
    return lax.dot_general(
        a, b, (((0,), (0,)), ((), ())), precision=HIGH, preferred_element_type=F32
    )


def iota(shape, dim):
    return lax.broadcasted_iota(jnp.int32, shape, dim)


def norm_parts(v):
    mean = jnp.mean(v, axis=-1, keepdims=True)
    centred = v - mean
    inv = lax.rsqrt(jnp.mean(centred * centred, axis=-1, keepdims=True) + EPS)
    return centred * inv, inv


def norm_back(o, unit, inv, gain):
    scaled = o * gain
    mean_o = jnp.mean(scaled, axis=-1, keepdims=True)
    mean_u = jnp.mean(scaled * unit, axis=-1, keepdims=True)
    back = inv * (scaled - mean_o - unit * mean_u)
    return back, jnp.sum(o * unit, axis=0, keepdims=True), jnp.sum(o, axis=0, keepdims=True)


def sigmoid(v):
    return 1.0 / (1.0 + jnp.exp(-v))


def into(a, w, flip):
    return nt(a, w) if flip else nn(a, w)


def outof(a, w, flip):
    return nn(a, w) if flip else nt(a, w)


def head_mask(heads):
    shape = (heads * 8, heads * HEAD)
    return iota(shape, 0) // 8 == iota(shape, 1) // HEAD


def seq_mask(lens, heads, length, rows):
    lens_all = jnp.concatenate([lens] * heads, axis=0)
    shape = (heads * 8, rows)
    low = (iota(shape, 0) % 8) * length
    col = iota(shape, 1)
    return (col >= low) & (col < low + lens_all)


def pick_rows(lens, length, rows):
    shape = (8, rows)
    back = lens - 1 if length == CTX else 0
    spot = jnp.where(lens > 0, iota((8, 1), 0) * length + back, -1)
    return iota(shape, 1) == spot


def spread_heads(rows, mask, heads):
    return jnp.where(mask, jnp.concatenate([rows.astype(F32)] * heads, axis=0), 0.0)


def fold_heads(rows, mask, heads):
    kept = jnp.where(mask, rows, 0.0)
    total = kept[:8]
    for h in range(1, heads):
        total = total + kept[8 * h : 8 * h + 8]
    return total


def pooled_front(cfg, tokens, gains, shifts, lens, wq, wk, wv, wo):
    length, heads, flip = cfg
    rows = tokens.shape[0]
    unit, _ = norm_parts(tokens.astype(F32))
    normed = (unit * gains[0:1] + shifts[0:1]).astype(BF16)
    pick = pick_rows(lens, length, rows).astype(BF16)
    middle = nn(pick, tokens)
    normed_pick = nn(pick, normed).astype(BF16)
    allowed = seq_mask(lens, heads, length, rows)
    mask = head_mask(heads)
    keys, values, probs, queries, mixes, y_vals = [], [], [], [], [], []
    for s in range(4):
        key = into(normed, wk[s], flip).astype(BF16)
        value = into(normed, wv[s], flip).astype(BF16)
        query = into(normed_pick, wq[s], flip).astype(BF16)
        scores = nt(spread_heads(query, mask, heads).astype(BF16), key) * SCALE
        scores = jnp.where(allowed, scores, -1e9)
        weights = jnp.where(allowed, jnp.exp(scores - jnp.max(scores, axis=-1, keepdims=True)), 0.0)
        total = jnp.sum(weights, axis=-1, keepdims=True)
        prob = weights / jnp.where(total > 0.0, total, 1.0)
        low = prob.astype(BF16)
        mix = fold_heads(nn(low, value), mask, heads).astype(BF16)
        middle = middle + nn(mix, wo[s])
        y_vals.append(nn(low, normed).astype(BF16))
        keys.append(key)
        values.append(value)
        probs.append(prob)
        queries.append(query)
        mixes.append(mix)
    return middle, normed, normed_pick, keys, values, probs, queries, mixes, y_vals


def bulk(cfg, tokens, gains, shifts, lens, normed, keys, values, wq, wo, up, down):
    length, heads, flip = cfg
    rows = tokens.shape[0]
    seqs = rows // length
    middle = tokens.astype(F32)
    pos = jnp.arange(length)
    allowed = pos[None, None, :] < lens[:seqs, 0][:, None, None]
    if length == CTX:
        allowed = allowed & (pos[None, None, :] <= pos[None, :, None])
    for s in range(4):
        query = into(normed, wq[s], flip).astype(BF16).reshape(seqs, length, heads, HEAD)
        key = keys[s].reshape(seqs, length, heads, HEAD)
        value = values[s].reshape(seqs, length, heads, HEAD)
        scores = jnp.einsum("nqhd,nkhd->nhqk", query, key, preferred_element_type=F32) * SCALE
        scores = jnp.where(allowed[:, None], scores, -1e9)
        weights = jnp.exp(scores - jnp.max(scores, axis=-1, keepdims=True))
        prob = (weights / jnp.sum(weights, axis=-1, keepdims=True)).astype(BF16)
        mix = jnp.einsum("nhqk,nkhd->nqhd", prob, value, preferred_element_type=F32)
        middle = middle + nn(mix.astype(BF16).reshape(rows, heads * HEAD), wo[s])
    unit, _ = norm_parts(middle)
    normed_two = (unit * gains[1:2] + shifts[1:2]).astype(BF16)
    final = middle
    for s in range(4):
        pre = nn(normed_two, up[s])
        final = final + nn((pre * sigmoid(1.702 * pre)).astype(BF16), down[s])
    return final.astype(BF16)


def mlp_head_forward(middle, gains, shifts, up, down, proj):
    unit_two, inv_two = norm_parts(middle)
    normed_two = (unit_two * gains[1:2] + shifts[1:2]).astype(BF16)
    final = middle
    pres, hids = [], []
    for s in range(4):
        pre = nn(normed_two, up[s])
        hid = (pre * sigmoid(1.702 * pre)).astype(BF16)
        final = final + nn(hid, down[s])
        pres.append(pre)
        hids.append(hid)
    unit_head, inv_head = norm_parts(final)
    normed_head = (unit_head * gains[2:3] + shifts[2:3]).astype(BF16)
    embedding = nn(normed_head, proj)
    inv_len = lax.rsqrt(jnp.sum(embedding * embedding, axis=-1, keepdims=True) + 1e-06)
    unit = (embedding * inv_len).astype(BF16)
    return unit, (unit_two, inv_two, normed_two, pres, hids, unit_head, inv_head, normed_head, embedding, inv_len)


def mlp_head_backward(grad_unit, kept, gains, up, down, proj, wo_own, mix_own):
    unit_two, inv_two, normed_two, pres, hids, unit_head, inv_head, normed_head, embedding, inv_len = kept
    along = jnp.sum(embedding * grad_unit, axis=-1, keepdims=True)
    grad_emb = (inv_len * grad_unit - inv_len * inv_len * inv_len * embedding * along).astype(BF16)
    proj_grad = tn(normed_head, grad_emb)
    grad_final, gain_2, shift_2 = norm_back(nt(grad_emb, proj), unit_head, inv_head, gains[2:3])
    grad_mlp = grad_final.astype(BF16)
    grad_two = None
    for s in range(4):
        gate = sigmoid(1.702 * pres[s])
        slope = gate + 1.702 * pres[s] * gate * (1.0 - gate)
        grad_pre = (nt(grad_mlp, down[s]) * slope).astype(BF16)
        part = nt(grad_pre, up[s])
        grad_two = part if grad_two is None else grad_two + part
        if s == 0:
            down_grad = tn(hids[0], grad_mlp)
            up_grad = tn(normed_two, grad_pre)
    back, gain_1, shift_1 = norm_back(grad_two, unit_two, inv_two, gains[1:2])
    grad_middle = grad_final + back
    branch = grad_middle.astype(BF16)
    out_grad = tn(mix_own, branch)
    mixed_own = nt(branch, wo_own).astype(BF16)
    return grad_middle, mixed_own, out_grad, up_grad, down_grad, proj_grad, (gain_1, gain_2), (shift_1, shift_2)


def contrast(image_unit, text_unit, logit_scale):
    factor = jnp.exp(logit_scale)
    logits = factor * nt(image_unit, text_unit)
    count = logits.shape[0]
    row_top = jnp.max(logits, axis=1, keepdims=True)
    row_lse = row_top + jnp.log(jnp.sum(jnp.exp(logits - row_top), axis=1, keepdims=True))
    col_top = jnp.max(logits, axis=0, keepdims=True)
    col_lse = col_top + jnp.log(jnp.sum(jnp.exp(logits - col_top), axis=0, keepdims=True))
    eye = iota(logits.shape, 0) == iota(logits.shape, 1)
    diag = jnp.sum(jnp.where(eye, logits, 0.0))
    loss = (0.5 * (jnp.sum(row_lse) + jnp.sum(col_lse)) - diag) / count
    grad = 0.5 * (jnp.exp(logits - row_lse) + jnp.exp(logits - col_lse))
    grad = jnp.where(eye, grad - 1.0, grad).astype(BF16)
    scale_grad = jnp.sum(grad.astype(F32) * logits)
    grad_image = factor * nn(grad, text_unit)
    grad_text = factor * tn(grad, image_unit)
    return loss, scale_grad, grad_image, grad_text


def attention_back(cfg, tokens, gains, shifts, lens, grad_rows, normed, keys, values, probs, queries, wq, wk, wv, wo):
    length, heads, flip = cfg
    rows = tokens.shape[0]
    unit, inv = norm_parts(tokens.astype(F32))
    mask = head_mask(heads)
    branch = grad_rows.astype(BF16)
    left, right, y_keys, g_queries = [], [], [], []
    query_side = None
    for s in range(4):
        grad_mixed = nt(branch, wo[s]).astype(BF16)
        spread = spread_heads(grad_mixed, mask, heads).astype(BF16)
        grad_probs = nt(spread, values[s])
        prob = probs[s]
        grad_scores = (prob * (grad_probs - jnp.sum(prob * grad_probs, axis=-1, keepdims=True))).astype(BF16)
        grad_query = (fold_heads(nn(grad_scores, keys[s]), mask, heads) * SCALE).astype(BF16)
        part = outof(grad_query, wq[s], flip)
        query_side = part if query_side is None else query_side + part
        wide = (spread_heads(queries[s], mask, heads) * SCALE).astype(BF16)
        left += [grad_scores, prob.astype(BF16)]
        right += [outof(wide, wk[s], flip).astype(BF16), outof(spread, wv[s], flip).astype(BF16)]
        y_keys.append(nn(grad_scores, normed).astype(BF16))
        g_queries.append(grad_query)
    pick = pick_rows(lens, length, rows)
    grad_one = tn(jnp.concatenate(left, axis=0), jnp.concatenate(right, axis=0))
    grad_one = grad_one + tn(pick.astype(BF16), query_side.astype(BF16))
    back, gain_0, shift_0 = norm_back(grad_one, unit, inv, gains[0:1])
    grad_tokens = exact_tn(pick.astype(F32), grad_rows) + back
    return grad_tokens.astype(BF16), gain_0, shift_0, y_keys, g_queries


def per_device(
    image_tokens, image_gains, image_shifts, image_qkv, image_out, image_up, image_down, image_proj,
    text_tokens, text_gains, text_shifts, text_qkv, text_out, text_up, text_down, text_proj,
    caption_lengths, logit_scale,
):
    every = ("x", "zh", "zb", "y", "c")
    devices = lax.axis_size(every)
    groups = devices // 4
    lane = lax.axis_index(("y", "c"))
    seqs = image_tokens.shape[0] // PATCHES
    image_cfg = (PATCHES, image_out.shape[0] // HEAD, True)
    text_cfg = (CTX, text_out.shape[0] // HEAD, False)
    image_lens = jnp.where(iota((8, 1), 0) < seqs, PATCHES, 0)
    own_lens = lax.dynamic_slice(caption_lengths, (lane * seqs,), (seqs,))
    text_lens = jnp.pad(own_lens, (0, 8 - seqs)).reshape(8, 1)

    def gather(w):
        over_y = lax.ppermute(w, "y", SWAP)
        return [w, over_y, lax.ppermute(w, "c", SWAP), lax.ppermute(over_y, "c", SWAP)]

    image_w = gather(jnp.transpose(image_qkv, (1, 2, 0)))
    text_w = gather(jnp.transpose(text_qkv, (1, 0, 2)))
    image_q, image_k, image_v = ([w[i] for w in image_w] for i in range(3))
    text_q, text_k, text_v = ([w[i] for w in text_w] for i in range(3))
    image_o, text_o = gather(image_out), gather(text_out)
    image_u, image_d = gather(image_up), gather(image_down)
    text_u, text_d = gather(text_up), gather(text_down)

    im = pooled_front(image_cfg, image_tokens, image_gains, image_shifts, image_lens, image_q, image_k, image_v, image_o)
    tx = pooled_front(text_cfg, text_tokens, text_gains, text_shifts, text_lens, text_q, text_k, text_v, text_o)

    def everywhere(v):
        wide = jnp.broadcast_to(v[None], (devices,) + v.shape)
        return lax.all_to_all(wide, every, split_axis=0, concat_axis=0, tiled=True)

    def to_lanes(slots):
        order = jnp.arange(4) ^ lane
        slot_of = order // 2 % 2 + order % 2 * 2
        v = jnp.take(jnp.stack(slots), slot_of, axis=0)
        wide = jnp.broadcast_to(v[None], (groups,) + v.shape).reshape((devices,) + v.shape[1:])
        return lax.all_to_all(wide, every, split_axis=0, concat_axis=0, tiled=True)

    def compact(v):
        return v[:, :seqs].reshape(devices * seqs, v.shape[-1])

    width = image_tokens.shape[1]
    mids = everywhere(jnp.concatenate([im[0], tx[0]], axis=1))
    image_mid, text_mid = compact(mids[:, :, :width]), compact(mids[:, :, width:])
    image_mix, text_mix = compact(to_lanes(im[7])), compact(to_lanes(tx[7]))
    image_first, text_first = compact(everywhere(im[2])), compact(everywhere(tx[2]))

    def by_head(y, heads):
        y = y.reshape(devices, heads, 8, y.shape[-1])[:, :, :seqs]
        return jnp.swapaxes(y, 0, 1).reshape(heads, devices * seqs, y.shape[-1])

    image_yv, text_yv = by_head(to_lanes(im[8]), image_cfg[1]), by_head(to_lanes(tx[8]), text_cfg[1])

    image_block = bulk(image_cfg, image_tokens, image_gains, image_shifts, image_lens, im[1], im[3], im[4], image_q, image_o, image_u, image_d)
    text_block = bulk(text_cfg, text_tokens, text_gains, text_shifts, text_lens, tx[1], tx[3], tx[4], text_q, text_o, text_u, text_d)

    image_unit, image_kept = mlp_head_forward(image_mid, image_gains, image_shifts, image_u, image_d, image_proj)
    text_unit, text_kept = mlp_head_forward(text_mid, text_gains, text_shifts, text_u, text_d, text_proj)
    loss, scale_grad, grad_image, grad_text = contrast(image_unit, text_unit, logit_scale[0])
    ib = mlp_head_backward(grad_image, image_kept, image_gains, image_u, image_d, image_proj, image_out, image_mix)
    tb = mlp_head_backward(grad_text, text_kept, text_gains, text_u, text_d, text_proj, text_out, text_mix)

    me = lax.axis_index(every)

    def own_rows(v):
        return jnp.pad(lax.dynamic_slice(v, (me * seqs, 0), (seqs, v.shape[1])), ((0, 8 - seqs), (0, 0)))

    ia = attention_back(image_cfg, image_tokens, image_gains, image_shifts, image_lens, own_rows(ib[0]), im[1], im[3], im[4], im[5], im[6], image_q, image_k, image_v, image_o)
    ta = attention_back(text_cfg, text_tokens, text_gains, text_shifts, text_lens, own_rows(tb[0]), tx[1], tx[3], tx[4], tx[5], tx[6], text_q, text_k, text_v, text_o)
    image_yk, text_yk = by_head(to_lanes(ia[3]), image_cfg[1]), by_head(to_lanes(ta[3]), text_cfg[1])
    image_gq, text_gq = compact(to_lanes(ia[4])), compact(to_lanes(ta[4]))
    sums = lax.psum((ia[1], ia[2], ta[1], ta[2]), every)

    def qkv_grads(cfg, first, wq, gq, yk, yv, mixed):
        heads, flip = cfg[1], cfg[2]
        pair = (lambda left, right: tn(right, left)) if flip else tn
        queries = (into(first, wq, flip).astype(BF16).astype(F32) * SCALE).astype(BF16)
        q_part = pair(first, gq)
        axis = 0 if flip else 1
        k_part = jnp.concatenate([pair(yk[h], queries[:, h * HEAD : (h + 1) * HEAD]) for h in range(heads)], axis=axis)
        v_part = jnp.concatenate([pair(yv[h], mixed[:, h * HEAD : (h + 1) * HEAD]) for h in range(heads)], axis=axis)
        return jnp.stack([q_part, k_part, v_part])

    image_qkv_grad = jnp.transpose(qkv_grads(image_cfg, image_first, image_q[0], image_gq, image_yk, image_yv, ib[1]), (2, 0, 1))
    text_qkv_grad = jnp.transpose(qkv_grads(text_cfg, text_first, text_q[0], text_gq, text_yk, text_yv, tb[1]), (1, 0, 2))
    return (
        image_block, ia[0], image_qkv_grad, ib[2], ib[3], ib[4],
        jnp.concatenate([sums[0], ib[6][0], ib[6][1]], axis=0),
        jnp.concatenate([sums[1], ib[7][0], ib[7][1]], axis=0),
        ib[5],
        text_block, ta[0], text_qkv_grad, tb[2], tb[3], tb[4],
        jnp.concatenate([sums[2], tb[6][0], tb[6][1]], axis=0),
        jnp.concatenate([sums[3], tb[7][0], tb[7][1]], axis=0),
        tb[5],
        scale_grad.reshape(1), loss.reshape(1),
    )


def solution(mesh):
    towers, batches, tensors = (mesh.shape[a] for a in ("tower", "batch", "tensor"))
    fine = Mesh(mesh.devices.reshape(towers, batches // 2, 2, tensors // 2, 2), ("x", "zh", "zb", "y", "c"))
    rows = P(("x", "zh", "zb", "y", "c"), None)
    lanes = ("y", "c")
    weights = (P(None, None, lanes), P(lanes, None), P(None, lanes), P(lanes, None))
    tower_in = (rows, P(), P()) + weights + (P(),)
    tower_out = (rows, rows) + weights + (P(), P(), P())
    return jax.shard_map(
        per_device,
        mesh=fine,
        in_specs=tower_in + tower_in + (P(("x", "zh", "zb")), P()),
        out_specs=tower_out + tower_out + (P(), P()),
        check_vma=False,
    )
```

```python
import jax
import jax.numpy as jnp
from jax import lax
from jax.experimental import pallas as pl
from jax.experimental.pallas import tpu as pltpu
from jax.sharding import Mesh, PartitionSpec as P

HEAD = 64
PATCHES = 50
CTX = 77
EPS = 1e-05
F32 = jnp.float32
BF16 = jnp.bfloat16
HIGH = lax.Precision.HIGHEST
SCALE = HEAD**-0.5
SWAP = [(0, 1), (1, 0)]
ONE_KERNEL_ROWS = 256
SLOT_LANES = (0, 2, 1, 3)
VMEM_BYTES = 60 * 1024 * 1024


def nn(a, b):
    return lax.dot_general(a, b, (((1,), (0,)), ((), ())), preferred_element_type=F32)


def nt(a, b):
    return lax.dot_general(a, b, (((1,), (1,)), ((), ())), preferred_element_type=F32)


def tn(a, b):
    return lax.dot_general(a, b, (((0,), (0,)), ((), ())), preferred_element_type=F32)


def exact_nn(a, b):
    return lax.dot_general(
        a, b, (((1,), (0,)), ((), ())), precision=HIGH, preferred_element_type=F32
    )


def exact_tn(a, b):
    return lax.dot_general(
        a, b, (((0,), (0,)), ((), ())), precision=HIGH, preferred_element_type=F32
    )


def iota(shape, dim):
    return lax.broadcasted_iota(jnp.int32, shape, dim)


def norm_parts(v):
    mean = jnp.mean(v, axis=-1, keepdims=True)
    centred = v - mean
    inv = lax.rsqrt(jnp.mean(centred * centred, axis=-1, keepdims=True) + EPS)
    return centred * inv, inv


def norm_back(o, unit, inv, gain):
    scaled = o * gain
    mean_o = jnp.mean(scaled, axis=-1, keepdims=True)
    mean_u = jnp.mean(scaled * unit, axis=-1, keepdims=True)
    back = inv * (scaled - mean_o - unit * mean_u)
    return back, jnp.sum(o * unit, axis=0, keepdims=True), jnp.sum(o, axis=0, keepdims=True)


def sigmoid(v):
    return 1.0 / (1.0 + jnp.exp(-v))


def shape_of(shape, dtype):
    return jax.ShapeDtypeStruct(shape, dtype)


def call(name, body, out_types, args, flops, smem=()):
    flat, tree = jax.tree.flatten(args)
    count = len(flat)

    def kernel(*refs):
        body(jax.tree.unflatten(tree, refs[:count]), refs[count:])

    moved = sum(v.size * v.dtype.itemsize for v in flat)
    spaces = [pltpu.SMEM if any(v is t for t in smem) else pltpu.VMEM for v in flat]
    return pl.pallas_call(
        kernel,
        out_shape=out_types,
        in_specs=[pl.BlockSpec(memory_space=space) for space in spaces],
        compiler_params=pltpu.CompilerParams(vmem_limit_bytes=VMEM_BYTES),
        cost_estimate=pl.CostEstimate(flops=flops, bytes_accessed=moved, transcendentals=0),
        name=name,
    )(*flat)


def fused(name, fn, out_types, args, flops, smem=()):
    def body(ins, outs):
        for ref, value in zip(outs, fn(*ins), strict=True):
            ref[...] = value

    return call(name, body, out_types, args, flops, smem)


def as_ones(mask):
    return jnp.where(mask, 1.0, 0.0)


def head_mask(heads):
    shape = (heads * 8, heads * HEAD)
    return (iota(shape, 0) >> 3) == (iota(shape, 1) >> 6)


def seq_mask(lens, heads, length, rows):
    lens_all = jnp.concatenate([lens[...]] * heads, axis=0)
    shape = (heads * 8, rows)
    low = (iota(shape, 0) & 7) * length
    col = iota(shape, 1)
    return (col >= low) & (col < low + lens_all)


def pick_rows(lens, length, rows):
    shape = (8, rows)
    held = lens[...]
    back = held - 1 if length == CTX else 0
    spot = jnp.where(held > 0, iota((8, 1), 0) * length + back, -1)
    return as_ones(iota(shape, 1) == spot)


def spread_heads(rows, mask, heads):
    return jnp.where(mask, jnp.concatenate([rows.astype(F32)] * heads, axis=0), 0.0)


def fold_heads(rows, mask, heads):
    kept = jnp.where(mask, rows, 0.0)
    total = kept[:8]
    for h in range(1, heads):
        total = total + kept[8 * h : 8 * h + 8]
    return total


class Tower:
    def __init__(self, length, heads, width, rows, seqs, flip):
        self.length, self.heads, self.width, self.rows, self.seqs, self.flip = length, heads, width, rows, seqs, flip
        self.part = heads * HEAD
        self.padded = -(-rows // 16) * 16
        self.piece = -(-self.part // 128) * 128
        self.per_row = width // self.piece

    def into(self, a, w):
        return nt(a, w) if self.flip else nn(a, w)

    def outof(self, a, w):
        return nn(a, w) if self.flip else nt(a, w)

    def through(self, a, w):
        return nn(a, w) if self.flip else nt(a, w)

    def through_back(self, a, w):
        return nt(a, w) if self.flip else nn(a, w)


def lane_rows(tower, small):
    shape = (tower.part, tower.piece)
    wide = nn(small, as_ones(iota(shape, 0) == iota(shape, 1)).astype(BF16))
    empty = jnp.zeros((1, tower.piece), F32)
    rows = []
    for first in (0, tower.per_row):
        ends = range(first, first + tower.per_row)
        rows.append(jnp.concatenate([wide[n : n + 1] if n < tower.seqs else empty for n in ends], axis=1))
    return rows


def fill_spare(rows, spare):
    row = iota(rows.shape, 0)
    for place, value in spare:
        rows = jnp.where(row == place, value, rows)
    return rows


def front_body(tower, groups, ins, outs):
    tokens, gains, shifts, lens, lane, slots = ins
    middle_out, normed_out, key_out, value_out, prob_out, query_out, early_out = outs
    heads = tower.heads
    low_tokens = tokens[...]
    unit, _ = norm_parts(low_tokens.astype(F32))
    normed = (unit * gains[0:1, :] + shifts[0:1, :]).astype(BF16)
    normed_out[...] = normed
    pick = pick_rows(lens, tower.length, tower.padded).astype(BF16)
    middle = nn(pick, low_tokens)
    normed_pick = nn(pick, normed).astype(BF16)
    allowed = seq_mask(lens, heads, tower.length, tower.padded)
    mask = head_mask(heads)
    for s in range(4):
        key = tower.into(normed, slots[s][1]).astype(BF16)
        value = tower.into(normed, slots[s][2]).astype(BF16)
        query = tower.into(normed_pick, slots[s][0]).astype(BF16)
        key_out[s] = key
        value_out[s] = value
        query_out[s] = query
        scores = nt(spread_heads(query, mask, heads).astype(BF16), key) * SCALE
        scores = jnp.where(allowed, scores, -1e9)
        weights = jnp.where(allowed, jnp.exp(scores - jnp.max(scores, axis=-1, keepdims=True)), 0.0)
        total = jnp.sum(weights, axis=-1, keepdims=True)
        prob = weights / jnp.where(total > 0.0, total, 1.0)
        prob_out[s] = prob
        low = prob.astype(BF16)
        mix = fold_heads(nn(low, value), mask, heads).astype(BF16)
        middle = middle + tower.through(mix, slots[s][3])
        halves = lane_rows(tower, mix)
        y = fill_spare(nn(low, normed), ((14, halves[0]), (15, halves[1])))
        block = jnp.concatenate([y, normed_pick.astype(F32)], axis=0).astype(BF16)
        early_out[:, lane[0] ^ SLOT_LANES[s]] = jnp.broadcast_to(block[None], (groups,) + block.shape)
    middle_out[...] = middle.astype(BF16)


def front_types(tower, groups):
    return (
        shape_of((8, tower.width), BF16),
        shape_of((tower.padded, tower.width), BF16),
        shape_of((4, tower.padded, tower.part), BF16),
        shape_of((4, tower.padded, tower.part), BF16),
        shape_of((4, tower.heads * 8, tower.padded), F32),
        shape_of((4, 8, tower.part), BF16),
        shape_of((groups, 4, tower.heads * 8 + 8, tower.width), BF16),
    )


def window(first, last, tower):
    low = first // tower.length * tower.length // 16 * 16
    high = -(-(((last - 1) // tower.length + 1) * tower.length) // 16) * 16
    return low, min(high, tower.padded)


def mix_body(tower, ins, outs):
    tokens, gains, shifts, lens, normed, keys, values, slots = ins
    middle_out, normed_out = outs
    length, heads, rows = tower.length, tower.heads, tower.padded
    tile = 160 if length == CTX else 112
    row = iota((rows, 1), 0)
    low = jnp.zeros((rows, 1), jnp.int32)
    high = jnp.zeros((rows, 1), jnp.int32)
    for n in range(tower.seqs):
        here = (row >= n * length) & (row < (n + 1) * length)
        low = jnp.where(here, n * length, low)
        end = n * length + lens[n : n + 1, :]
        if length == CTX:
            end = jnp.minimum(end, row + 1)
        high = jnp.where(here, end, high)
    spans = [(first, min(first + tile, rows)) for first in range(0, rows, tile)]
    allowed = []
    for first, last in spans:
        start, stop = window(first, last, tower)
        col = iota((last - first, stop - start), 1) + start
        allowed.append((col >= low[first:last]) & (col < high[first:last]))
    held = normed[...]
    middle = tokens[...].astype(F32)
    lane_head = iota((1, tower.part), 1) >> 6
    for s in range(4):
        query = tower.into(held, slots[s][0]).astype(BF16)
        mixes = []
        for (first, last), mask in zip(spans, allowed, strict=True):
            start, stop = window(first, last, tower)
            mine = query[first:last].astype(F32)
            mix = None
            for h in range(heads):
                one = jnp.where(lane_head == h, mine, 0.0).astype(BF16)
                scores = nt(one, keys[s, start:stop, :]) * SCALE
                scores = jnp.where(mask, scores, -1e9)
                weights = jnp.exp(scores - jnp.max(scores, axis=-1, keepdims=True))
                prob = (weights / jnp.sum(weights, axis=-1, keepdims=True)).astype(BF16)
                part = jnp.where(lane_head == h, nn(prob, values[s, start:stop, :]), 0.0)
                mix = part if mix is None else mix + part
            mixes.append(mix)
        middle = middle + tower.through(jnp.concatenate(mixes, axis=0).astype(BF16), slots[s][3])
    middle_out[...] = middle
    unit, _ = norm_parts(middle)
    normed_out[...] = (unit * gains[1:2, :] + shifts[1:2, :]).astype(BF16)


def mlp_body(tower, ins, outs):
    middle, normed, after, slots = ins
    final = middle[...]
    held = normed[...]
    width = tower.width
    for s in range(4):
        pre = nn(held, slots[s][:width, :])
        final = final + nn((pre * sigmoid(1.702 * pre)).astype(BF16), slots[s][width:, :])
    outs[0][...] = final[: tower.rows].astype(BF16)


def mlp_head_forward(tower, middle, gains, shifts, slots, proj):
    width = tower.width
    unit_two, inv_two = norm_parts(middle)
    normed_two = (unit_two * gains[1:2, :] + shifts[1:2, :]).astype(BF16)
    final = middle
    pres, hids = [], []
    for s in range(4):
        pre = nn(normed_two, slots[s][:width, :])
        hid = (pre * sigmoid(1.702 * pre)).astype(BF16)
        final = final + nn(hid, slots[s][width:, :])
        pres.append(pre)
        hids.append(hid)
    unit_head, inv_head = norm_parts(final)
    normed_head = (unit_head * gains[2:3, :] + shifts[2:3, :]).astype(BF16)
    embedding = nn(normed_head, proj[...])
    inv_len = lax.rsqrt(jnp.sum(embedding * embedding, axis=-1, keepdims=True) + 1e-06)
    unit = (embedding * inv_len).astype(BF16)
    return unit, (unit_two, inv_two, normed_two, pres, hids[0], unit_head, inv_head, normed_head, embedding, inv_len)


def mlp_head_backward(tower, grad_unit, kept, gains, slots, proj):
    unit_two, inv_two, normed_two, pres, hid, unit_head, inv_head, normed_head, embedding, inv_len = kept
    width = tower.width
    along = jnp.sum(embedding * grad_unit, axis=-1, keepdims=True)
    grad_emb = (inv_len * grad_unit - inv_len * inv_len * inv_len * embedding * along).astype(BF16)
    proj_grad = tn(normed_head, grad_emb)
    grad_final, gain_2, shift_2 = norm_back(nt(grad_emb, proj[...]), unit_head, inv_head, gains[2:3, :])
    grad_mlp = grad_final.astype(BF16)
    grad_two = None
    for s in range(4):
        gate = sigmoid(1.702 * pres[s])
        slope = gate + 1.702 * pres[s] * gate * (1.0 - gate)
        grad_pre = (nt(grad_mlp, slots[s][width:, :]) * slope).astype(BF16)
        part = nt(grad_pre, slots[s][:width, :])
        grad_two = part if grad_two is None else grad_two + part
        if s == 0:
            down_grad = tn(hid, grad_mlp)
            up_grad = tn(normed_two, grad_pre)
    back, gain_1, shift_1 = norm_back(grad_two, unit_two, inv_two, gains[1:2, :])
    grad_middle = grad_final + back
    gains_grad = jnp.concatenate([gain_1, gain_2], axis=0)
    shifts_grad = jnp.concatenate([shift_1, shift_2], axis=0)
    return grad_middle, up_grad, down_grad, proj_grad, gains_grad, shifts_grad


def total(v):
    return jnp.sum(jnp.sum(v, axis=1, keepdims=True), axis=0, keepdims=True)


def contrast(image_unit, text_unit, logit_scale):
    factor = jnp.exp(logit_scale[...])
    logits = factor * nt(image_unit, text_unit)
    count = logits.shape[0]
    row_top = jnp.max(logits, axis=1, keepdims=True)
    row_lse = row_top + jnp.log(jnp.sum(jnp.exp(logits - row_top), axis=1, keepdims=True))
    col_top = jnp.max(logits, axis=0, keepdims=True)
    col_lse = col_top + jnp.log(jnp.sum(jnp.exp(logits - col_top), axis=0, keepdims=True))
    eye = iota(logits.shape, 0) == iota(logits.shape, 1)
    diag = total(jnp.where(eye, logits, 0.0))
    loss = (0.5 * (total(row_lse) + total(col_lse)) - diag) / count
    grad = 0.5 * (jnp.exp(logits - row_lse) + jnp.exp(logits - col_lse))
    low = jnp.where(eye, grad - 1.0, grad).astype(BF16)
    scale_grad = total(low.astype(F32) * logits)
    grad_image = factor * nn(low, text_unit)
    grad_text = factor * tn(low, image_unit)
    return loss, scale_grad, grad_image, grad_text


def pooled_back(towers, devices, one_hot, place, mids, image, text, logit_scale):
    seqs = towers[0].seqs
    pairs, spread, half = devices * seqs, devices * 8, devices * 4
    own_mids, other_mids = mids
    core = place[0] & 1
    if one_hot:
        pair = iota((pairs, 1), 0)
        device = ((2 * pair + 1) * (65536 // (2 * seqs) + 1)) >> 16
        spot = (device >> 1) * 8 + (pair - device * seqs)
        spot = jnp.where((device & 1) == core, spot, spot + half)
        pick = as_ones(iota((pairs, spread), 1) == spot).astype(BF16)
        split = towers[0].width
        rows = [
            nn(pick, jnp.concatenate([own_mids[:, cut], other_mids[:, cut]], axis=0))
            for cut in (slice(0, split), slice(split, split + towers[1].width))
        ]
        back_shape = (spread, pairs)
        place_back = as_ones(iota(back_shape, 0) == widen(pairs, seqs))
        own_shape = (8, pairs)
        own_row = iota((8, 1), 0)
        pick_mine = as_ones(iota(own_shape, 1) == jnp.where(own_row < seqs, place[0] * seqs + own_row, -1))
    else:
        both = jnp.stack([own_mids, other_mids]).reshape(2, devices // 2, 8, own_mids.shape[-1])
        both = jnp.where(core == 0, both, both[::-1])
        rows = jnp.swapaxes(both, 0, 1).reshape(devices, 8, -1)[:, :seqs].reshape(pairs, -1).astype(F32)
        rows = [rows[:, : towers[0].width], rows[:, towers[0].width :]]
    units, kept = [], []
    for tower, middle, (gains, shifts, slots, proj) in zip(towers, rows, (image, text), strict=True):
        unit, state = mlp_head_forward(tower, middle, gains, shifts, slots, proj)
        units.append(unit)
        kept.append(state)
    loss, scale_grad, grad_image, grad_text = contrast(units[0], units[1], logit_scale)
    results = ()
    for tower, grad, state, (gains, shifts, slots, proj) in zip(towers, (grad_image, grad_text), kept, (image, text), strict=True):
        grad_middle, *rest = mlp_head_backward(tower, grad, state, gains, slots, proj)
        low = grad_middle.astype(BF16)
        if one_hot:
            branch = nn(place_back.astype(BF16), low).astype(BF16)
            own = exact_nn(pick_mine, grad_middle)
        else:
            branch = jnp.pad(low.reshape(devices, seqs, -1), ((0, 0), (0, 8 - seqs), (0, 0))).reshape(spread, -1)
            own = jnp.pad(lax.dynamic_slice(grad_middle, (place[0] * seqs, 0), (seqs, tower.width)), ((0, 8 - seqs), (0, 0)))
        results += (own, branch) + tuple(rest)
    return results + (loss, scale_grad)


def widen(pairs, seqs):
    pair = iota((1, pairs), 1)
    device = ((2 * pair + 1) * (65536 // (2 * seqs) + 1)) >> 16
    return device * 8 + (pair - device * seqs)


def pooled_types(tower, spread, slots, proj):
    width = tower.width
    return (
        shape_of((8, width), F32),
        shape_of((spread, width), BF16),
        shape_of((width, slots[0].shape[0] - width), F32),
        shape_of((slots[0].shape[0] - width, width), F32),
        shape_of(proj.shape, F32),
        shape_of((2, width), F32),
        shape_of((2, width), F32),
    )


def back_body(tower, groups, ins, outs):
    tokens, gains, lens, lane, grad_rows, normed, keys, values, probs, queries, slots = ins
    grad_out, late_out = outs
    heads = tower.heads
    unit, inv = norm_parts(tokens[...].astype(F32))
    mask = head_mask(heads)
    held = normed[...]
    grad_rows = grad_rows[...]
    branch = grad_rows.astype(BF16)
    left, right, y_keys, g_queries = [], [], [], []
    query_side = None
    for s in range(4):
        grad_mixed = tower.through_back(branch, slots[s][3]).astype(BF16)
        spread = spread_heads(grad_mixed, mask, heads).astype(BF16)
        grad_probs = nt(spread, values[s])
        prob = probs[s]
        grad_scores = (prob * (grad_probs - jnp.sum(prob * grad_probs, axis=-1, keepdims=True))).astype(BF16)
        grad_query = (fold_heads(nn(grad_scores, keys[s]), mask, heads) * SCALE).astype(BF16)
        part = tower.outof(grad_query, slots[s][0])
        query_side = part if query_side is None else query_side + part
        wide = (spread_heads(queries[s], mask, heads) * SCALE).astype(BF16)
        left += [grad_scores, prob.astype(BF16)]
        right += [tower.outof(wide, slots[s][1]).astype(BF16), tower.outof(spread, slots[s][2]).astype(BF16)]
        y_keys.append(nn(grad_scores, held))
        g_queries.append(grad_query)
    pick = pick_rows(lens, tower.length, tower.padded)
    grad_one = tn(jnp.concatenate(left, axis=0), jnp.concatenate(right, axis=0))
    grad_one = grad_one + tn(pick.astype(BF16), query_side.astype(BF16))
    back, gain_0, shift_0 = norm_back(grad_one, unit, inv, gains[0:1, :])
    grad_tokens = exact_tn(pick, grad_rows) + back
    grad_out[...] = grad_tokens[: tower.rows].astype(BF16)
    for s in range(4):
        halves = lane_rows(tower, g_queries[s])
        block = fill_spare(y_keys[s], ((6, gain_0), (7, shift_0), (14, halves[0]), (15, halves[1]))).astype(BF16)
        late_out[:, lane[0] ^ SLOT_LANES[s]] = jnp.broadcast_to(block[None], (groups,) + block.shape)


def back_types(tower, groups):
    return (
        shape_of((tower.rows, tower.width), BF16),
        shape_of((groups, 4, tower.heads * 8, tower.width), BF16),
    )


def last_step(tower, devices, one_hot, branch, wq, wo, early, late, gains, shifts):
    heads, part, piece = tower.heads, tower.part, tower.piece
    spread = devices * 8
    lane_head = iota((1, 1, 1, part), 3) >> 6

    def block_rows(block, per, first):
        if not one_hot:
            return block.reshape(devices, per, -1)[:, first : first + 8].reshape(spread, -1)
        shape = (spread, devices * per)
        row = iota((spread, 1), 0)
        return nn(as_ones(iota(shape, 1) == (row >> 3) * per + first + (row & 7)).astype(BF16), block).astype(BF16)

    def spare_rows(block, per, place):
        if not one_hot:
            return block.reshape(devices, per, -1)[:, place]
        shape = (devices, devices * per)
        return nn(as_ones(iota(shape, 1) == iota((devices, 1), 0) * per + place).astype(BF16), block).astype(BF16)

    def sum_rows(block, per, place):
        if not one_hot:
            return jnp.sum(block.reshape(devices, per, -1)[:, place].astype(F32), axis=0, keepdims=True)
        return jnp.sum(spare_rows(block, per, place).astype(F32), axis=0, keepdims=True)

    def small_rows(block, per):
        halves = (spare_rows(block, per, 14), spare_rows(block, per, 15))
        if not one_hot:
            both = jnp.concatenate(halves, axis=1).reshape(devices, -1, piece)[:, :8, :part]
            both = jnp.pad(both[:, : tower.seqs], ((0, 0), (0, 8 - tower.seqs), (0, 0)))
            return both.reshape(spread, part)
        row, col = iota((spread, devices), 0), iota((spread, devices), 1)
        rows = None
        for n in range(tower.seqs):
            here = n % tower.per_row * piece
            one = nn(as_ones((row >> 3 == col) & ((row & 7) == n)).astype(BF16), halves[n // tower.per_row][:, here : here + part])
            rows = one if rows is None else rows + one
        return rows.astype(BF16)

    def by_head(rows, per):
        blocks = per // 8
        wide = jnp.broadcast_to(rows.reshape(devices, 1, 8, part), (devices, blocks, 8, part))
        number = iota((1, blocks, 1, 1), 1)
        return jnp.where(lane_head == number, wide, 0.0).reshape(devices * per, part).astype(BF16)

    def pair(left, right):
        return tn(right, left) if tower.flip else tn(left, right)

    early_per, late_per = heads * 8 + 8, heads * 8
    branch, early, late = branch[...], early[...], late[...]
    first = block_rows(early, early_per, heads * 8)
    queries = tower.into(first, wq[...]).astype(BF16).astype(F32) * SCALE
    grad_mixed = nt(branch, wo[...]).astype(BF16).astype(F32)
    mixes = small_rows(early, early_per)
    grad_queries = small_rows(late, late_per)
    q_part = pair(first, grad_queries)
    k_part = pair(late, by_head(queries, late_per))
    v_part = pair(early, by_head(grad_mixed, early_per))
    out_grad = tn(mixes, branch)
    gains_grad = jnp.concatenate([sum_rows(late, late_per, 6), gains[...]], axis=0)
    shifts_grad = jnp.concatenate([sum_rows(late, late_per, 7), shifts[...]], axis=0)
    return q_part, k_part, v_part, out_grad, gains_grad, shifts_grad


def per_device(
    image_tokens, image_gains, image_shifts, image_qkv, image_out, image_up, image_down, image_proj,
    text_tokens, text_gains, text_shifts, text_qkv, text_out, text_up, text_down, text_proj,
    caption_lengths, logit_scale,
):
    every = ("x", "zh", "zb", "y", "c")
    devices = lax.axis_size(every)
    groups = devices // 4
    lane = lax.axis_index(("y", "c")).astype(jnp.int32).reshape(1)
    me = lax.axis_index(every).astype(jnp.int32).reshape(1)
    seqs = image_tokens.shape[0] // PATCHES
    towers = (
        Tower(PATCHES, image_out.shape[0] // HEAD, image_tokens.shape[1], image_tokens.shape[0], seqs, True),
        Tower(CTX, text_out.shape[0] // HEAD, text_tokens.shape[1], text_tokens.shape[0], seqs, False),
    )
    small = devices * seqs <= ONE_KERNEL_ROWS
    image_lens = jnp.where(iota((8, 1), 0) < seqs, PATCHES, 0)
    own_lens = lax.dynamic_slice(caption_lengths, (lane[0] * seqs,), (seqs,))
    lens = (image_lens, jnp.pad(own_lens, (0, 8 - seqs)).reshape(8, 1))
    gains, shifts = (image_gains, text_gains), (image_shifts, text_shifts)
    tokens = tuple(jnp.pad(v, ((0, t.padded - t.rows), (0, 0))) for t, v in zip(towers, (image_tokens, text_tokens)))

    corner = lax.axis_index(("x", "zb"))

    def gather(quarters):
        mine = lax.dynamic_index_in_dim(quarters, corner, 0, keepdims=False)
        over = lax.ppermute(mine, "y", SWAP)
        wide = jnp.broadcast_to(over[None], quarters.shape)
        across = lax.all_to_all(wide, ("x", "zb"), split_axis=0, concat_axis=0, tiled=True)
        return [quarters, across, lax.ppermute(quarters, "c", SWAP), lax.ppermute(across, "c", SWAP)]

    text_attn = gather(jnp.concatenate([jnp.transpose(text_qkv, (1, 0, 2)), text_out.T[None]], axis=0))
    image_attn = gather(jnp.concatenate([jnp.transpose(image_qkv, (1, 2, 0)), image_out[None]], axis=0))

    def quarter(up, down):
        both = jnp.concatenate([up, down], axis=0)
        return both.reshape(4, both.shape[0] // 4, both.shape[1])

    def joined(slots):
        return [w.reshape(-1, w.shape[-1]) for w in slots]

    image_mlp = joined(gather(quarter(image_up, image_down)))
    text_mlp = joined(gather(quarter(text_up, text_down)))
    attn, mlp = (image_attn, text_attn), (image_mlp, text_mlp)
    names = ("image", "text")

    fronts = [None, None]
    for i in (1, 0):
        fronts[i] = call(
            "front_" + names[i],
            lambda ins, outs, tower=towers[i]: front_body(tower, groups, ins, outs),
            front_types(towers[i], groups),
            (tokens[i], gains[i], shifts[i], lens[i], lane, attn[i]),
            2 * 10**9,
            smem=(lane,),
        )

    def same_core(v):
        wide = jnp.broadcast_to(v[None], (devices // 2,) + v.shape)
        got = lax.all_to_all(wide, ("x", "zh", "zb", "y"), split_axis=0, concat_axis=0, tiled=True)
        got = got.reshape(devices * 4, v.shape[-1])
        return got, lax.ppermute(got, "c", SWAP)

    def swap_all(v):
        got = lax.all_to_all(v.reshape((devices,) + v.shape[2:]), every, split_axis=0, concat_axis=0, tiled=True)
        return got.reshape(-1, v.shape[-1])

    mids = same_core(jnp.concatenate([fronts[0][0], fronts[1][0]], axis=1))
    early = [swap_all(f[6]) for f in fronts]

    mixed = []
    for i in range(2):
        types = (shape_of(tokens[i].shape, F32), shape_of(tokens[i].shape, BF16))
        front = fronts[i]
        args = (tokens[i], gains[i], shifts[i], lens[i], front[1], front[2], front[3], attn[i])
        mixed.append(call("mix_" + names[i], lambda ins, outs, tower=towers[i]: mix_body(tower, ins, outs), types, args, 4 * 10**9))

    projs = (image_proj, text_proj)
    pools = [(gains[i], shifts[i], mlp[i], projs[i]) for i in range(2)]
    scale = logit_scale.reshape(1, 1)
    args = (me, mids, pools[0], pools[1], scale)
    if small:
        types = ()
        for i in range(2):
            types += pooled_types(towers[i], devices * 8, mlp[i], projs[i])
        types += (shape_of((1, 1), F32),) * 2
        pooled = fused("pooled", lambda *v: pooled_back(towers, devices, True, *v), types, args, 10**10, smem=(me,))
    else:
        pooled = pooled_back(towers, devices, False, *args)
    pools = (pooled[:7], pooled[7:14])
    loss, scale_grad = pooled[14:]

    backs, late = [], []
    for i in range(2):
        front = fronts[i]
        args = (tokens[i], gains[i], lens[i], lane, pools[i][0], front[1], front[2], front[3], front[4], front[5], attn[i])
        backs.append(call(
            "back_" + names[i],
            lambda ins, outs, tower=towers[i]: back_body(tower, groups, ins, outs),
            back_types(towers[i], groups), args, 10**9, smem=(lane,),
        ))
        late.append(swap_all(backs[i][1]))

    blocks = []
    for i in range(2):
        types = (shape_of((towers[i].rows, towers[i].width), BF16),)
        after = backs[1][0][:8, :128]
        args = (mixed[i][0], mixed[i][1], after, mlp[i])
        blocks.append(call("mlp_" + names[i], lambda ins, outs, tower=towers[i]: mlp_body(tower, ins, outs), types, args, 8 * 10**9)[0])

    ends = []
    own_q = (image_attn[0][0], text_attn[0][0])
    for i, wo in enumerate((image_out, text_out)):
        tower = towers[i]
        args = (pools[i][1], own_q[i], wo, early[i], late[i], pools[i][5], pools[i][6])
        if small:
            types = (shape_of(own_q[i].shape, F32),) * 3 + (shape_of(wo.shape, F32),) + (shape_of((3, tower.width), F32),) * 2
            ends.append(fused("last_" + names[i], lambda *v, tower=tower: last_step(tower, devices, True, *v), types, args, 10**9))
        else:
            ends.append(last_step(tower, devices, False, *args))

    image_qkv_grad = jnp.transpose(jnp.stack(ends[0][:3]), (2, 0, 1))
    text_qkv_grad = jnp.transpose(jnp.stack(ends[1][:3]), (1, 0, 2))
    results = ()
    for i, qkv_grad in enumerate((image_qkv_grad, text_qkv_grad)):
        own, branch, up_grad, down_grad, proj_grad, _, _ = pools[i]
        results += (blocks[i], backs[i][0], qkv_grad, ends[i][3], up_grad, down_grad, ends[i][4], ends[i][5], proj_grad)
    return results + (scale_grad.reshape(1), loss.reshape(1))


def solution(mesh):
    towers, batches, tensors = (mesh.shape[a] for a in ("tower", "batch", "tensor"))
    fine = Mesh(mesh.devices.reshape(towers, batches // 2, 2, tensors // 2, 2), ("x", "zh", "zb", "y", "c"))
    rows = P(("x", "zh", "zb", "y", "c"), None)
    lanes = ("y", "c")
    weights = (P(None, None, lanes), P(lanes, None), P(None, lanes), P(lanes, None))
    tower_in = (rows, P(), P()) + weights + (P(),)
    tower_out = (rows, rows) + weights + (P(), P(), P())
    return jax.shard_map(
        per_device,
        mesh=fine,
        in_specs=tower_in + tower_in + (P(("x", "zh", "zb")), P()),
        out_specs=tower_out + tower_out + (P(), P()),
        check_vma=False,
    )
```

```python
import jax
import jax.numpy as jnp
from jax import lax
from jax.experimental import pallas as pl
from jax.experimental.pallas import tpu as pltpu
from jax.sharding import Mesh, PartitionSpec as P

HEAD = 64
PATCHES = 50
CTX = 77
EPS = 1e-05
F32 = jnp.float32
BF16 = jnp.bfloat16
HIGH = lax.Precision.HIGHEST
SCALE = HEAD**-0.5
SWAP = [(0, 1), (1, 0)]
ONE_KERNEL_ROWS = 256
SLOT_LANES = (0, 2, 1, 3)
VMEM_BYTES = 60 * 1024 * 1024


def nn(a, b):
    return lax.dot_general(a, b, (((1,), (0,)), ((), ())), preferred_element_type=F32)


def nt(a, b):
    return lax.dot_general(a, b, (((1,), (1,)), ((), ())), preferred_element_type=F32)


def tn(a, b):
    return lax.dot_general(a, b, (((0,), (0,)), ((), ())), preferred_element_type=F32)


def exact_nn(a, b):
    return lax.dot_general(
        a, b, (((1,), (0,)), ((), ())), precision=HIGH, preferred_element_type=F32
    )


def exact_tn(a, b):
    return lax.dot_general(
        a, b, (((0,), (0,)), ((), ())), precision=HIGH, preferred_element_type=F32
    )


def iota(shape, dim):
    return lax.broadcasted_iota(jnp.int32, shape, dim)


def norm_parts(v):
    mean = jnp.mean(v, axis=-1, keepdims=True)
    centred = v - mean
    inv = lax.rsqrt(jnp.mean(centred * centred, axis=-1, keepdims=True) + EPS)
    return centred * inv, inv


def norm_back(o, unit, inv, gain):
    scaled = o * gain
    mean_o = jnp.mean(scaled, axis=-1, keepdims=True)
    mean_u = jnp.mean(scaled * unit, axis=-1, keepdims=True)
    back = inv * (scaled - mean_o - unit * mean_u)
    return back, jnp.sum(o * unit, axis=0, keepdims=True), jnp.sum(o, axis=0, keepdims=True)


def sigmoid(v):
    return 1.0 / (1.0 + jnp.exp(-v))


def shape_of(shape, dtype):
    return jax.ShapeDtypeStruct(shape, dtype)


def call(name, body, out_types, args, flops, smem=(), scratch=()):
    flat, tree = jax.tree.flatten(args)
    count, total_outs = len(flat), len(out_types)

    def kernel(*refs):
        outs, held = refs[count : count + total_outs], refs[count + total_outs :]
        body(jax.tree.unflatten(tree, refs[:count]), outs, *held)

    moved = sum(v.size * v.dtype.itemsize for v in flat)
    spaces = [pltpu.SMEM if any(v is t for t in smem) else pltpu.VMEM for v in flat]
    return pl.pallas_call(
        kernel,
        out_shape=out_types,
        in_specs=[pl.BlockSpec(memory_space=space) for space in spaces],
        scratch_shapes=scratch,
        compiler_params=pltpu.CompilerParams(vmem_limit_bytes=VMEM_BYTES),
        cost_estimate=pl.CostEstimate(flops=flops, bytes_accessed=moved, transcendentals=0),
        name=name,
    )(*flat)


def fused(name, fn, out_types, args, flops, smem=(), scratch=()):
    def body(ins, outs, *held):
        for ref, value in zip(outs, fn(*ins, *held), strict=True):
            if isinstance(value, list):
                for i, part in enumerate(value):
                    ref[i] = part
            else:
                ref[...] = value

    return call(name, body, out_types, args, flops, smem, scratch)


def as_ones(mask):
    return jnp.where(mask, 1.0, 0.0)


def head_mask(heads):
    shape = (heads * 8, heads * HEAD)
    return (iota(shape, 0) >> 3) == (iota(shape, 1) >> 6)


def seq_mask(lens, heads, length, rows):
    lens_all = jnp.concatenate([lens[...]] * heads, axis=0)
    shape = (heads * 8, rows)
    low = (iota(shape, 0) & 7) * length
    col = iota(shape, 1)
    return (col >= low) & (col < low + lens_all)


def pick_rows(lens, length, rows):
    shape = (8, rows)
    held = lens[...]
    back = held - 1 if length == CTX else 0
    spot = jnp.where(held > 0, iota((8, 1), 0) * length + back, -1)
    return as_ones(iota(shape, 1) == spot)


def spread_heads(rows, mask, heads):
    return jnp.where(mask, jnp.concatenate([rows.astype(F32)] * heads, axis=0), 0.0)


def fold_heads(rows, mask, heads):
    kept = jnp.where(mask, rows, 0.0)
    total = kept[:8]
    for h in range(1, heads):
        total = total + kept[8 * h : 8 * h + 8]
    return total


class Tower:
    def __init__(self, length, heads, width, rows, seqs, flip):
        self.length, self.heads, self.width, self.rows, self.seqs, self.flip = length, heads, width, rows, seqs, flip
        self.part = heads * HEAD
        self.padded = -(-rows // 16) * 16
        self.piece = -(-self.part // 128) * 128
        self.per_row = width // self.piece

    def into(self, a, w):
        return nt(a, w) if self.flip else nn(a, w)

    def outof(self, a, w):
        return nn(a, w) if self.flip else nt(a, w)

    def through(self, a, w):
        return nn(a, w) if self.flip else nt(a, w)

    def through_back(self, a, w):
        return nt(a, w) if self.flip else nn(a, w)


def lane_rows(tower, small):
    shape = (tower.part, tower.piece)
    wide = nn(small, as_ones(iota(shape, 0) == iota(shape, 1)).astype(BF16))
    empty = jnp.zeros((1, tower.piece), F32)
    rows = []
    for first in (0, tower.per_row):
        ends = range(first, first + tower.per_row)
        rows.append(jnp.concatenate([wide[n : n + 1] if n < tower.seqs else empty for n in ends], axis=1))
    return rows


def fill_spare(rows, spare):
    row = iota(rows.shape, 0)
    for place, value in spare:
        rows = jnp.where(row == place, value, rows)
    return rows


def front_body(tower, groups, ins, outs):
    tokens, gains, shifts, lens, lane, slots = ins
    middle_out, normed_out, key_out, value_out, prob_out, query_out, early_out = outs
    heads = tower.heads
    low_tokens = tokens[...]
    unit, _ = norm_parts(low_tokens.astype(F32))
    normed = (unit * gains[0:1, :] + shifts[0:1, :]).astype(BF16)
    normed_out[...] = normed
    pick = pick_rows(lens, tower.length, tower.padded).astype(BF16)
    middle = nn(pick, low_tokens)
    normed_pick = nn(pick, normed).astype(BF16)
    allowed = seq_mask(lens, heads, tower.length, tower.padded)
    mask = head_mask(heads)
    for s in range(4):
        key = tower.into(normed, slots[s][1]).astype(BF16)
        value = tower.into(normed, slots[s][2]).astype(BF16)
        query = tower.into(normed_pick, slots[s][0]).astype(BF16)
        key_out[s] = key
        value_out[s] = value
        query_out[s] = query
        scores = nt(spread_heads(query, mask, heads).astype(BF16), key) * SCALE
        scores = jnp.where(allowed, scores, -1e9)
        weights = jnp.where(allowed, jnp.exp(scores - jnp.max(scores, axis=-1, keepdims=True)), 0.0)
        total = jnp.sum(weights, axis=-1, keepdims=True)
        prob = weights / jnp.where(total > 0.0, total, 1.0)
        prob_out[s] = prob
        low = prob.astype(BF16)
        mix = fold_heads(nn(low, value), mask, heads).astype(BF16)
        middle = middle + tower.through(mix, slots[s][3])
        halves = lane_rows(tower, mix)
        block = fill_spare(nn(low, normed), ((14, halves[0]), (15, halves[1]))).astype(BF16)
        early_out[:, lane[0] ^ SLOT_LANES[s]] = jnp.broadcast_to(block[None], (groups,) + block.shape)
    middle_out[...] = jnp.concatenate([middle, normed_pick.astype(F32)], axis=0).astype(BF16)


def front_types(tower, groups):
    return (
        shape_of((16, tower.width), BF16),
        shape_of((tower.padded, tower.width), BF16),
        shape_of((4, tower.padded, tower.part), BF16),
        shape_of((4, tower.padded, tower.part), BF16),
        shape_of((4, tower.heads * 8, tower.padded), F32),
        shape_of((4, 8, tower.part), BF16),
        shape_of((groups, 4, tower.heads * 8, tower.width), BF16),
    )


def window(first, last, tower):
    low = first // tower.length * tower.length // 16 * 16
    high = -(-(((last - 1) // tower.length + 1) * tower.length) // 16) * 16
    return low, min(high, tower.padded)


def mix_body(tower, ins, outs):
    tokens, gains, shifts, lens, normed, keys, values, slots = ins
    middle_out, normed_out = outs
    length, heads, rows = tower.length, tower.heads, tower.padded
    tile = 160 if length == CTX else 112
    row = iota((rows, 1), 0)
    low = jnp.zeros((rows, 1), jnp.int32)
    high = jnp.zeros((rows, 1), jnp.int32)
    for n in range(tower.seqs):
        here = (row >= n * length) & (row < (n + 1) * length)
        low = jnp.where(here, n * length, low)
        end = n * length + lens[n : n + 1, :]
        if length == CTX:
            end = jnp.minimum(end, row + 1)
        high = jnp.where(here, end, high)
    spans = [(first, min(first + tile, rows)) for first in range(0, rows, tile)]
    allowed = []
    for first, last in spans:
        start, stop = window(first, last, tower)
        col = iota((last - first, stop - start), 1) + start
        allowed.append((col >= low[first:last]) & (col < high[first:last]))
    held = normed[...]
    middle = tokens[...].astype(F32)
    lane_head = iota((1, tower.part), 1) >> 6
    for s in range(4):
        query = tower.into(held, slots[s][0]).astype(BF16)
        mixes = []
        for (first, last), mask in zip(spans, allowed, strict=True):
            start, stop = window(first, last, tower)
            mine = query[first:last].astype(F32)
            mix = None
            for h in range(heads):
                one = jnp.where(lane_head == h, mine, 0.0).astype(BF16)
                scores = nt(one, keys[s, start:stop, :]) * SCALE
                scores = jnp.where(mask, scores, -1e9)
                weights = jnp.exp(scores - jnp.max(scores, axis=-1, keepdims=True))
                prob = (weights / jnp.sum(weights, axis=-1, keepdims=True)).astype(BF16)
                part = jnp.where(lane_head == h, nn(prob, values[s, start:stop, :]), 0.0)
                mix = part if mix is None else mix + part
            mixes.append(mix)
        middle = middle + tower.through(jnp.concatenate(mixes, axis=0).astype(BF16), slots[s][3])
    middle_out[...] = middle
    unit, _ = norm_parts(middle)
    normed_out[...] = (unit * gains[1:2, :] + shifts[1:2, :]).astype(BF16)


def mlp_body(tower, ins, outs):
    middle, normed, after, slots = ins
    final = middle[...]
    held = normed[...]
    for slot in slots:
        pre = nt(held, slot[0])
        final = final + nn((pre * sigmoid(1.702 * pre)).astype(BF16), slot[1])
    outs[0][...] = final[: tower.rows].astype(BF16)


def mlp_head_forward(tower, middle, gains, shifts, slots, proj, keep):
    unit_two, inv_two = norm_parts(middle)
    normed_two = (unit_two * gains[1:2, :] + shifts[1:2, :]).astype(BF16)
    final = middle
    pres, hids = [], []
    for slot in slots:
        pre = nt(normed_two, slot[0])
        hid = (pre * sigmoid(1.702 * pre)).astype(BF16)
        final = final + nn(hid, slot[1])
        pres.append(pre if keep else None)
        hids.append(hid)
    unit_head, inv_head = norm_parts(final)
    normed_head = (unit_head * gains[2:3, :] + shifts[2:3, :]).astype(BF16)
    embedding = nn(normed_head, proj[...])
    inv_len = lax.rsqrt(jnp.sum(embedding * embedding, axis=-1, keepdims=True) + 1e-06)
    unit = (embedding * inv_len).astype(BF16)
    return unit, (unit_two, inv_two, normed_two, pres, hids[0], unit_head, inv_head, normed_head, embedding, inv_len)


def mlp_head_backward(tower, grad_unit, kept, gains, slots, proj):
    unit_two, inv_two, normed_two, pres, hid, unit_head, inv_head, normed_head, embedding, inv_len = kept
    along = jnp.sum(embedding * grad_unit, axis=-1, keepdims=True)
    grad_emb = (inv_len * grad_unit - inv_len * inv_len * inv_len * embedding * along).astype(BF16)
    proj_grad = tn(normed_head, grad_emb)
    grad_final, gain_2, shift_2 = norm_back(nt(grad_emb, proj[...]), unit_head, inv_head, gains[2:3, :])
    grad_mlp = grad_final.astype(BF16)
    grad_two = None
    again = normed_two if pres[0] is not None else lax.optimization_barrier((normed_two, grad_mlp))[0]
    for slot, pre in zip(slots, pres, strict=True):
        if pre is None:
            pre = nt(again, slot[0])
        gate = sigmoid(1.702 * pre)
        slope = gate + 1.702 * pre * gate * (1.0 - gate)
        grad_pre = (nt(grad_mlp, slot[1]) * slope).astype(BF16)
        part = nn(grad_pre, slot[0])
        grad_two = part if grad_two is None else grad_two + part
        if slot is slots[0]:
            down_grad = tn(hid, grad_mlp)
            up_grad = tn(normed_two, grad_pre)
    back, gain_1, shift_1 = norm_back(grad_two, unit_two, inv_two, gains[1:2, :])
    grad_middle = grad_final + back
    gains_grad = jnp.concatenate([gain_1, gain_2], axis=0)
    shifts_grad = jnp.concatenate([shift_1, shift_2], axis=0)
    return grad_middle, up_grad, down_grad, proj_grad, gains_grad, shifts_grad


def total(v):
    return jnp.sum(jnp.sum(v, axis=1, keepdims=True), axis=0, keepdims=True)


def contrast(image_unit, text_unit, logit_scale):
    factor = jnp.exp(logit_scale[...])
    logits = factor * nt(image_unit, text_unit)
    count = logits.shape[0]
    row_top = jnp.max(logits, axis=1, keepdims=True)
    row_lse = row_top + jnp.log(jnp.sum(jnp.exp(logits - row_top), axis=1, keepdims=True))
    col_top = jnp.max(logits, axis=0, keepdims=True)
    col_lse = col_top + jnp.log(jnp.sum(jnp.exp(logits - col_top), axis=0, keepdims=True))
    eye = iota(logits.shape, 0) == iota(logits.shape, 1)
    diag = total(jnp.where(eye, logits, 0.0))
    loss = (0.5 * (total(row_lse) + total(col_lse)) - diag) / count
    grad = 0.5 * (jnp.exp(logits - row_lse) + jnp.exp(logits - col_lse))
    low = jnp.where(eye, grad - 1.0, grad).astype(BF16)
    scale_grad = total(low.astype(F32) * logits)
    grad_image = factor * nn(low, text_unit)
    grad_text = factor * tn(low, image_unit)
    return loss, scale_grad, grad_image, grad_text


def pooled_back(towers, devices, one_hot, place, mids, after, image, text, logit_scale, *held):
    seqs = towers[0].seqs
    pairs, spread = devices * seqs, devices * 8
    own_mids, other_mids = mids
    core = place[0] & 1
    if one_hot:
        pair = iota((pairs, 1), 0)
        device = ((2 * pair + 1) * (65536 // (2 * seqs) + 1)) >> 16
        spot = (device >> 1) * 16 + (pair - device * seqs)
        spot = jnp.where((device & 1) == core, spot, spot + spread)
        pick = as_ones(iota((pairs, 2 * spread), 1) == spot).astype(BF16)
        row = iota((spread, 1), 0)
        spot = (row >> 4) * 16 + 8 + (row & 7)
        spot = jnp.where(((row >> 3) & 1) == core, spot, spot + spread)
        pick_first = as_ones(iota((spread, 2 * spread), 1) == spot).astype(BF16)
        split = towers[0].width
        both = [
            jnp.concatenate([own_mids[:, cut], other_mids[:, cut]], axis=0)
            for cut in (slice(0, split), slice(split, split + towers[1].width))
        ]
        rows = []
        for ref, v in zip(held, both, strict=True):
            ref[...] = jnp.maximum(nn(pick, v), -3.0e38)
            rows.append(ref[...])
        firsts = [nn(pick_first, v).astype(BF16) for v in both]
        back_shape = (spread, pairs)
        place_back = as_ones(iota(back_shape, 0) == widen(pairs, seqs))
        own_shape = (8, pairs)
        own_row = iota((8, 1), 0)
        pick_mine = as_ones(iota(own_shape, 1) == jnp.where(own_row < seqs, place[0] * seqs + own_row, -1))
    else:
        both = jnp.stack([own_mids, other_mids]).reshape(2, devices // 2, 16, own_mids.shape[-1])
        both = jnp.where(core == 0, both, both[::-1])
        both = jnp.swapaxes(both, 0, 1).reshape(devices, 16, -1)
        rows = both[:, :seqs].reshape(pairs, -1).astype(F32)
        rows = [rows[:, : towers[0].width], rows[:, towers[0].width :]]
        firsts = both[:, 8:].reshape(spread, -1)
        firsts = [firsts[:, : towers[0].width], firsts[:, towers[0].width :]]
    units, kept = [], []
    for tower, middle, (gains, shifts, slots, proj) in zip(towers, rows, (image, text), strict=True):
        unit, state = mlp_head_forward(tower, middle, gains, shifts, slots, proj, one_hot)
        units.append(unit)
        kept.append(state)
    loss, scale_grad, grad_image, grad_text = contrast(units[0], units[1], logit_scale)
    results = ()
    for tower, grad, state, first, (gains, shifts, slots, proj) in zip(towers, (grad_image, grad_text), kept, firsts, (image, text), strict=True):
        grad_middle, *rest = mlp_head_backward(tower, grad, state, gains, slots, proj)
        low = grad_middle.astype(BF16)
        if one_hot:
            branch = nn(place_back.astype(BF16), low).astype(BF16)
            own = exact_nn(pick_mine, grad_middle)
        else:
            branch = jnp.pad(low.reshape(devices, seqs, -1), ((0, 0), (0, 8 - seqs), (0, 0))).reshape(spread, -1)
            own = jnp.pad(lax.dynamic_slice(grad_middle, (place[0] * seqs, 0), (seqs, tower.width)), ((0, 8 - seqs), (0, 0)))
        results += (own, branch, first) + tuple(rest)
    return results + (loss, scale_grad)


def widen(pairs, seqs):
    pair = iota((1, pairs), 1)
    device = ((2 * pair + 1) * (65536 // (2 * seqs) + 1)) >> 16
    return device * 8 + (pair - device * seqs)


def pooled_types(tower, spread, slots, proj):
    width = tower.width
    return (
        shape_of((8, width), F32),
        shape_of((spread, width), BF16),
        shape_of((spread, width), BF16),
        shape_of((width, slots[0].shape[1]), F32),
        shape_of((slots[0].shape[1], width), F32),
        shape_of(proj.shape, F32),
        shape_of((2, width), F32),
        shape_of((2, width), F32),
    )


def back_body(tower, groups, ins, outs):
    tokens, gains, lens, lane, grad_rows, normed, keys, values, probs, queries, slots = ins
    grad_out, late_out = outs
    heads = tower.heads
    unit, inv = norm_parts(tokens[...].astype(F32))
    mask = head_mask(heads)
    held = normed[...]
    grad_rows = grad_rows[...]
    branch = grad_rows.astype(BF16)
    left, right, y_keys, g_queries = [], [], [], []
    query_side = None
    for s in range(4):
        grad_mixed = tower.through_back(branch, slots[s][3]).astype(BF16)
        spread = spread_heads(grad_mixed, mask, heads).astype(BF16)
        grad_probs = nt(spread, values[s])
        prob = probs[s]
        grad_scores = (prob * (grad_probs - jnp.sum(prob * grad_probs, axis=-1, keepdims=True))).astype(BF16)
        grad_query = (fold_heads(nn(grad_scores, keys[s]), mask, heads) * SCALE).astype(BF16)
        part = tower.outof(grad_query, slots[s][0])
        query_side = part if query_side is None else query_side + part
        wide = (spread_heads(queries[s], mask, heads) * SCALE).astype(BF16)
        left += [grad_scores, prob.astype(BF16)]
        right += [tower.outof(wide, slots[s][1]).astype(BF16), tower.outof(spread, slots[s][2]).astype(BF16)]
        y_keys.append(nn(grad_scores, held))
        g_queries.append(grad_query)
    pick = pick_rows(lens, tower.length, tower.padded)
    grad_one = tn(jnp.concatenate(left, axis=0), jnp.concatenate(right, axis=0))
    grad_one = grad_one + tn(pick.astype(BF16), query_side.astype(BF16))
    back, gain_0, shift_0 = norm_back(grad_one, unit, inv, gains[0:1, :])
    grad_tokens = exact_tn(pick, grad_rows) + back
    grad_out[...] = grad_tokens[: tower.rows].astype(BF16)
    for s in range(4):
        halves = lane_rows(tower, g_queries[s])
        block = fill_spare(y_keys[s], ((6, gain_0), (7, shift_0), (14, halves[0]), (15, halves[1]))).astype(BF16)
        late_out[:, lane[0] ^ SLOT_LANES[s]] = jnp.broadcast_to(block[None], (groups,) + block.shape)


def back_types(tower, groups):
    return (
        shape_of((tower.rows, tower.width), BF16),
        shape_of((groups, 4, tower.heads * 8, tower.width), BF16),
    )


def last_step(tower, devices, one_hot, branch, first, wq, wo, early, late, gains, shifts):
    heads, part, piece = tower.heads, tower.part, tower.piece
    spread = devices * 8
    lane_head = iota((1, 1, 1, part), 3) >> 6

    def spare_rows(block, per, place):
        if not one_hot:
            return block.reshape(devices, per, -1)[:, place]
        shape = (devices, devices * per)
        return nn(as_ones(iota(shape, 1) == iota((devices, 1), 0) * per + place).astype(BF16), block).astype(BF16)

    def sum_rows(block, per, place):
        if not one_hot:
            return jnp.sum(block.reshape(devices, per, -1)[:, place].astype(F32), axis=0, keepdims=True)
        return jnp.sum(spare_rows(block, per, place).astype(F32), axis=0, keepdims=True)

    def small_rows(block, per):
        halves = (spare_rows(block, per, 14), spare_rows(block, per, 15))
        if not one_hot:
            both = jnp.concatenate(halves, axis=1).reshape(devices, -1, piece)[:, :8, :part]
            both = jnp.pad(both[:, : tower.seqs], ((0, 0), (0, 8 - tower.seqs), (0, 0)))
            return both.reshape(spread, part)
        row, col = iota((spread, devices), 0), iota((spread, devices), 1)
        rows = None
        for n in range(tower.seqs):
            here = n % tower.per_row * piece
            one = nn(as_ones((row >> 3 == col) & ((row & 7) == n)).astype(BF16), halves[n // tower.per_row][:, here : here + part])
            rows = one if rows is None else rows + one
        return rows.astype(BF16)

    def by_head(rows, per):
        blocks = per // 8
        wide = jnp.broadcast_to(rows.reshape(devices, 1, 8, part), (devices, blocks, 8, part))
        number = iota((1, blocks, 1, 1), 1)
        return jnp.where(lane_head == number, wide, 0.0).reshape(devices * per, part).astype(BF16)

    def pair(left, right):
        return tn(right, left) if tower.flip else tn(left, right)

    per = heads * 8
    branch, first, early, late = branch[...], first[...], early[...], late[...]
    queries = tower.into(first, wq[...]).astype(BF16).astype(F32) * SCALE
    grad_mixed = nt(branch, wo[...]).astype(BF16).astype(F32)
    mixes = small_rows(early, per)
    grad_queries = small_rows(late, per)
    q_part = pair(first, grad_queries)
    k_part = pair(late, by_head(queries, per))
    v_part = pair(early, by_head(grad_mixed, per))
    out_grad = tn(mixes, branch)
    gains_grad = jnp.concatenate([sum_rows(late, per, 6), gains[...]], axis=0)
    shifts_grad = jnp.concatenate([sum_rows(late, per, 7), shifts[...]], axis=0)
    return [q_part, k_part, v_part], out_grad, gains_grad, shifts_grad


def per_device(
    image_tokens, image_gains, image_shifts, image_qkv, image_out, image_up, image_down, image_proj,
    text_tokens, text_gains, text_shifts, text_qkv, text_out, text_up, text_down, text_proj,
    caption_lengths, logit_scale,
):
    every = ("x", "zh", "zb", "y", "c")
    devices = lax.axis_size(every)
    groups = devices // 4
    lane = lax.axis_index(("y", "c")).astype(jnp.int32).reshape(1)
    me = lax.axis_index(every).astype(jnp.int32).reshape(1)
    seqs = image_tokens.shape[0] // PATCHES
    towers = (
        Tower(PATCHES, image_out.shape[0] // HEAD, image_tokens.shape[1], image_tokens.shape[0], seqs, True),
        Tower(CTX, text_out.shape[0] // HEAD, text_tokens.shape[1], text_tokens.shape[0], seqs, False),
    )
    small = devices * seqs <= ONE_KERNEL_ROWS
    image_lens = jnp.where(iota((8, 1), 0) < seqs, PATCHES, 0)
    own_lens = lax.dynamic_slice(caption_lengths, (lane[0] * seqs,), (seqs,))
    lens = (image_lens, jnp.pad(own_lens, (0, 8 - seqs)).reshape(8, 1))
    gains, shifts = (image_gains, text_gains), (image_shifts, text_shifts)
    tokens = tuple(jnp.pad(v, ((0, t.padded - t.rows), (0, 0))) for t, v in zip(towers, (image_tokens, text_tokens)))

    corner = lax.axis_index(("x", "zb"))

    def then(v, *before):
        return lax.optimization_barrier((v,) + before)[0]

    def quarter_over_y(quarters):
        return lax.ppermute(lax.dynamic_index_in_dim(quarters, corner, 0, keepdims=False), "y", SWAP)

    def gather(quarters, over, before, late):
        wide = jnp.broadcast_to(then(over, *before)[None], quarters.shape)
        across = lax.all_to_all(wide, ("x", "zb"), split_axis=0, concat_axis=0, tiled=True)
        across = then(across, *late)
        return [quarters, across, lax.ppermute(quarters, "c", SWAP), lax.ppermute(across, "c", SWAP)]

    def pair_of(up, down):
        return jnp.stack([up.T, down])

    text_quarters = jnp.concatenate([jnp.transpose(text_qkv, (1, 0, 2)), text_out.T[None]], axis=0)
    image_quarters = jnp.concatenate([jnp.transpose(image_qkv, (1, 2, 0)), image_out[None]], axis=0)
    image_pair, text_pair = pair_of(image_up, image_down), pair_of(text_up, text_down)
    def with_core(slots):
        return slots + [lax.ppermute(v, "c", SWAP) for v in slots]

    fourths = image_pair.reshape(2, 4, image_pair.shape[1] // 4, image_pair.shape[2])
    fourth = lax.dynamic_index_in_dim(fourths, corner, 1, keepdims=False)
    image_over = quarter_over_y(image_quarters)
    text_over = lax.ppermute(then(text_quarters, image_over), "y", SWAP)
    pair_over = lax.ppermute(then(fourth, image_over), "y", SWAP)
    text_across = lax.ppermute(then(text_pair, pair_over), "y", SWAP)
    image_attn = gather(image_quarters, image_over, (text_pair, fourth) + tokens, (pair_over,))
    beside_x, beside_z = lax.ppermute(pair_over, "x", SWAP), lax.ppermute(pair_over, "zb", SWAP)
    beside_xz = lax.ppermute(pair_over, ("x", "zb"), [(i, i ^ 3) for i in range(4)])
    text_core = lax.ppermute(text_quarters, "c", SWAP)
    image_mlp = with_core([image_pair, pair_over, beside_x, beside_z, beside_xz])
    text_mlp = with_core([text_pair, text_across])
    attn, mlp = [image_attn, None], (image_mlp, text_mlp)
    names = ("image", "text")

    fronts = [None, None]
    for i in (0, 1):
        if i == 1:
            attn[1] = [text_quarters, text_over, text_core, lax.ppermute(then(text_over, fronts[0][0]), "c", SWAP)]
            tokens = (tokens[0], then(tokens[1], beside_x, beside_z))
        fronts[i] = call(
            "front_" + names[i],
            lambda ins, outs, tower=towers[i]: front_body(tower, groups, ins, outs),
            front_types(towers[i], groups),
            (tokens[i], gains[i], shifts[i], lens[i], lane, attn[i]),
            2 * 10**9,
            smem=(lane,),
        )

    def same_core(v):
        wide = jnp.broadcast_to(v[None], (devices // 2,) + v.shape)
        got = lax.all_to_all(wide, ("x", "zh", "zb", "y"), split_axis=0, concat_axis=0, tiled=True)
        return got.reshape(-1, v.shape[-1])

    def swap_all(v):
        got = lax.all_to_all(v.reshape((devices,) + v.shape[2:]), every, split_axis=0, concat_axis=0, tiled=True)
        return got.reshape(-1, v.shape[-1])

    mids = same_core(then(jnp.concatenate([fronts[0][0], fronts[1][0]], axis=1), beside_xz))
    mixed = []
    for i in range(2):
        types = (shape_of(tokens[i].shape, F32), shape_of(tokens[i].shape, BF16))
        front = fronts[i]
        held = then(front[1], text_across)
        args = (tokens[i], gains[i], shifts[i], lens[i], held, front[2], front[3], attn[i])
        mixed.append(call("mix_" + names[i], lambda ins, outs, tower=towers[i]: mix_body(tower, ins, outs), types, args, 4 * 10**9))

    mids = then(mids, mixed[1][1])
    mids = (mids, lax.ppermute(mids, "c", SWAP))
    early_image = swap_all(then(fronts[0][6], mids[0]))

    projs = (image_proj, text_proj)
    pools = [(gains[i], shifts[i], mlp[i], projs[i]) for i in range(2)]
    scale = logit_scale.reshape(1, 1)
    after = (mixed[1][1],) if small else ()
    args = (me, mids, after, pools[0], pools[1], scale)
    if small:
        types = ()
        for i in range(2):
            types += pooled_types(towers[i], devices * 8, mlp[i], projs[i])
        types += (shape_of((1, 1), F32),) * 2
        pooled = fused("pooled", lambda *v: pooled_back(towers, devices, True, *v), types, args, 10**10, (me,), tuple(pltpu.VMEM((devices * seqs, t.width), F32) for t in towers))
    else:
        pooled = pooled_back(towers, devices, False, *args)
    pools = (pooled[:8], pooled[8:16])
    loss, scale_grad = pooled[16:]

    early = [early_image, swap_all(then(fronts[1][6], early_image, pools[0][0]))]
    backs, late = [], []
    for i in range(2):
        front = fronts[i]
        args = (tokens[i], gains[i], lens[i], lane, pools[i][0], front[1], front[2], front[3], front[4], front[5], attn[i])
        backs.append(call(
            "back_" + names[i],
            lambda ins, outs, tower=towers[i]: back_body(tower, groups, ins, outs),
            back_types(towers[i], groups), args, 10**9, smem=(lane,),
        ))
        late.append(swap_all(then(backs[i][1], early[1], *late)))

    blocks = []
    for i in range(2):
        types = (shape_of((towers[i].rows, towers[i].width), BF16),)
        after = backs[1][0]
        args = (mixed[i][0], mixed[i][1], after, mlp[i])
        blocks.append(call("mlp_" + names[i], lambda ins, outs, tower=towers[i]: mlp_body(tower, ins, outs), types, args, 8 * 10**9)[0])

    ends = []
    own_q = (attn[0][0][0], attn[1][0][0])
    for i, wo in enumerate((image_out, text_out)):
        tower = towers[i]
        args = (pools[i][1], pools[i][2], own_q[i], wo, early[i], late[i], pools[i][6], pools[i][7])
        if small:
            types = (shape_of((3,) + own_q[i].shape, F32), shape_of(wo.shape, F32)) + (shape_of((3, tower.width), F32),) * 2
            ends.append(fused("last_" + names[i], lambda *v, tower=tower: last_step(tower, devices, True, *v), types, args, 10**9))
        else:
            grads, *rest = last_step(tower, devices, False, *args)
            ends.append((jnp.stack(grads), *rest))

    image_qkv_grad = jnp.transpose(jnp.asarray(ends[0][0]), (2, 0, 1))
    text_qkv_grad = jnp.transpose(jnp.asarray(ends[1][0]), (1, 0, 2))
    results = ()
    for i, qkv_grad in enumerate((image_qkv_grad, text_qkv_grad)):
        own, branch, first, up_grad, down_grad, proj_grad, _, _ = pools[i]
        results += (blocks[i], backs[i][0], qkv_grad, ends[i][1], up_grad, down_grad, ends[i][2], ends[i][3], proj_grad)
    return results + (scale_grad.reshape(1), loss.reshape(1))


def solution(mesh):
    towers, batches, tensors = (mesh.shape[a] for a in ("tower", "batch", "tensor"))
    fine = Mesh(mesh.devices.reshape(towers, batches // 2, 2, tensors // 2, 2), ("x", "zh", "zb", "y", "c"))
    rows = P(("x", "zh", "zb", "y", "c"), None)
    lanes = ("y", "c")
    weights = (P(None, None, lanes), P(lanes, None), P(None, lanes), P(lanes, None))
    tower_in = (rows, P(), P()) + weights + (P(),)
    tower_out = (rows, rows) + weights + (P(), P(), P())
    return jax.shard_map(
        per_device,
        mesh=fine,
        in_specs=tower_in + tower_in + (P(("x", "zh", "zb")), P()),
        out_specs=tower_out + tower_out + (P(), P()),
        check_vma=False,
    )
```

```python
import jax
import jax.numpy as jnp
from jax import lax
from jax.experimental import pallas as pl
from jax.experimental.pallas import tpu as pltpu
from jax.sharding import Mesh, PartitionSpec as P

HEAD = 64
PATCHES = 50
CTX = 77
EPS = 1e-05
F32 = jnp.float32
BF16 = jnp.bfloat16
HIGH = lax.Precision.HIGHEST
SCALE = HEAD**-0.5
SWAP = [(0, 1), (1, 0)]
ONE_KERNEL_ROWS = 256
SLOT_LANES = (0, 2, 1, 3)
VMEM_BYTES = 60 * 1024 * 1024


def nn(a, b):
    return lax.dot_general(a, b, (((1,), (0,)), ((), ())), preferred_element_type=F32)


def nt(a, b):
    return lax.dot_general(a, b, (((1,), (1,)), ((), ())), preferred_element_type=F32)


def tn(a, b):
    return lax.dot_general(a, b, (((0,), (0,)), ((), ())), preferred_element_type=F32)


def exact_nn(a, b):
    return lax.dot_general(
        a, b, (((1,), (0,)), ((), ())), precision=HIGH, preferred_element_type=F32
    )


def exact_tn(a, b):
    return lax.dot_general(
        a, b, (((0,), (0,)), ((), ())), precision=HIGH, preferred_element_type=F32
    )


def iota(shape, dim):
    return lax.broadcasted_iota(jnp.int32, shape, dim)


def norm_parts(v):
    mean = jnp.mean(v, axis=-1, keepdims=True)
    centred = v - mean
    inv = lax.rsqrt(jnp.mean(centred * centred, axis=-1, keepdims=True) + EPS)
    return centred * inv, inv


def norm_back(o, unit, inv, gain):
    scaled = o * gain
    mean_o = jnp.mean(scaled, axis=-1, keepdims=True)
    mean_u = jnp.mean(scaled * unit, axis=-1, keepdims=True)
    back = inv * (scaled - mean_o - unit * mean_u)
    return back, jnp.sum(o * unit, axis=0, keepdims=True), jnp.sum(o, axis=0, keepdims=True)


def sigmoid(v):
    return 0.5 + 0.5 * jnp.tanh(0.5 * v)


def shape_of(shape, dtype):
    return jax.ShapeDtypeStruct(shape, dtype)


class Streamed:
    def __init__(self, source, held, done):
        self.held, self.waiting = held, pltpu.make_async_copy(source, held, done)
        self.waiting.start()

    @property
    def shape(self):
        return self.held.shape

    def __getitem__(self, index):
        if self.waiting is not None:
            self.waiting.wait()
            self.waiting = None
        return self.held[index]


def call(name, body, out_types, args, flops, smem=(), scratch=(), stream=(), idle=()):
    flat, tree = jax.tree.flatten(args)
    count, total_outs = len(flat), len(out_types)
    moving = [i for i, v in enumerate(flat) if any(v is t for t in stream)]
    buffers = tuple(pltpu.VMEM(flat[i].shape, flat[i].dtype) for i in moving)

    def kernel(*refs):
        ins, outs, held = list(refs[:count]), refs[count : count + total_outs], refs[count + total_outs :]
        if moving:
            done = held[-1]
            for slot, i in enumerate(moving):
                ins[i] = Streamed(ins[i], held[slot], done.at[slot])
        body(jax.tree.unflatten(tree, ins), outs, *held[len(moving) : len(moving) + len(scratch)])

    moved = sum(v.size * v.dtype.itemsize for v in flat)
    spaces = [pltpu.SMEM if any(v is t for t in smem) else pltpu.VMEM for v in flat]
    for i, v in enumerate(flat):
        if i in moving or any(v is t for t in idle):
            spaces[i] = pl.ANY
    last = (pltpu.SemaphoreType.DMA((len(moving),)),) if moving else ()
    return pl.pallas_call(
        kernel,
        out_shape=out_types,
        in_specs=[pl.BlockSpec(memory_space=space) for space in spaces],
        scratch_shapes=buffers + tuple(scratch) + last,
        compiler_params=pltpu.CompilerParams(vmem_limit_bytes=VMEM_BYTES),
        cost_estimate=pl.CostEstimate(flops=flops, bytes_accessed=moved, transcendentals=0),
        name=name,
    )(*flat)


def fused(name, fn, out_types, args, flops, smem=(), scratch=(), stream=(), idle=()):
    def body(ins, outs, *held):
        for ref, value in zip(outs, fn(*ins, *held), strict=True):
            if isinstance(value, list):
                for i, part in enumerate(value):
                    ref[i] = part
            else:
                ref[...] = value

    return call(name, body, out_types, args, flops, smem, scratch, stream, idle)


def as_ones(mask):
    return jnp.where(mask, 1.0, 0.0)


def head_mask(heads):
    shape = (heads * 8, heads * HEAD)
    return (iota(shape, 0) >> 3) == (iota(shape, 1) >> 6)


def seq_mask(lens, heads, length, rows):
    lens_all = jnp.concatenate([lens[...]] * heads, axis=0)
    shape = (heads * 8, rows)
    low = (iota(shape, 0) & 7) * length
    col = iota(shape, 1)
    return (col >= low) & (col < low + lens_all)


def pick_rows(lens, length, rows):
    shape = (8, rows)
    held = lens[...]
    back = held - 1 if length == CTX else 0
    spot = jnp.where(held > 0, iota((8, 1), 0) * length + back, -1)
    return as_ones(iota(shape, 1) == spot)


def spread_heads(rows, mask, heads):
    return jnp.where(mask, jnp.concatenate([rows.astype(F32)] * heads, axis=0), 0.0)


def fold_heads(rows, mask, heads):
    kept = jnp.where(mask, rows, 0.0)
    total = kept[:8]
    for h in range(1, heads):
        total = total + kept[8 * h : 8 * h + 8]
    return total


class Tower:
    def __init__(self, length, heads, width, rows, seqs, flip):
        self.length, self.heads, self.width, self.rows, self.seqs, self.flip = length, heads, width, rows, seqs, flip
        self.part = heads * HEAD
        self.padded = -(-rows // 16) * 16
        self.piece = -(-self.part // 128) * 128
        self.per_row = width // self.piece

    def into(self, a, w):
        return nt(a, w) if self.flip else nn(a, w)

    def outof(self, a, w):
        return nn(a, w) if self.flip else nt(a, w)

    def through(self, a, w):
        return nn(a, w) if self.flip else nt(a, w)

    def through_back(self, a, w):
        return nt(a, w) if self.flip else nn(a, w)


def lane_rows(tower, small):
    shape = (tower.part, tower.piece)
    wide = nn(small, as_ones(iota(shape, 0) == iota(shape, 1)).astype(BF16))
    empty = jnp.zeros((1, tower.piece), F32)
    rows = []
    for first in (0, tower.per_row):
        ends = range(first, first + tower.per_row)
        rows.append(jnp.concatenate([wide[n : n + 1] if n < tower.seqs else empty for n in ends], axis=1))
    return rows


def fill_spare(rows, spare):
    row = iota(rows.shape, 0)
    for place, value in spare:
        rows = jnp.where(row == place, value, rows)
    return rows


def front_body(tower, groups, ins, outs):
    tokens, gains, shifts, lens, lane, slots = ins
    middle_out, normed_out, key_out, value_out, prob_out, query_out, early_out = outs
    heads = tower.heads
    low_tokens = tokens[...]
    unit, _ = norm_parts(low_tokens.astype(F32))
    normed = (unit * gains[0:1, :] + shifts[0:1, :]).astype(BF16)
    normed_out[...] = normed
    pick = pick_rows(lens, tower.length, tower.padded).astype(BF16)
    middle = nn(pick, low_tokens)
    normed_pick = nn(pick, normed).astype(BF16)
    allowed = seq_mask(lens, heads, tower.length, tower.padded)
    mask = head_mask(heads)
    for s in range(4):
        key = tower.into(normed, slots[s][1]).astype(BF16)
        value = tower.into(normed, slots[s][2]).astype(BF16)
        query = tower.into(normed_pick, slots[s][0]).astype(BF16)
        key_out[s] = key
        value_out[s] = value
        query_out[s] = query
        scores = nt(spread_heads(query, mask, heads).astype(BF16), key) * SCALE
        scores = jnp.where(allowed, scores, -1e9)
        weights = jnp.where(allowed, jnp.exp(scores - jnp.max(scores, axis=-1, keepdims=True)), 0.0)
        total = jnp.sum(weights, axis=-1, keepdims=True)
        prob = weights * (1.0 / jnp.where(total > 0.0, total, 1.0))
        prob_out[s] = prob
        low = prob.astype(BF16)
        mix = fold_heads(nn(low, value), mask, heads).astype(BF16)
        middle = middle + tower.through(mix, slots[s][3])
        halves = lane_rows(tower, mix)
        block = fill_spare(nn(low, normed), ((14, halves[0]), (15, halves[1]))).astype(BF16)
        early_out[:, lane[0] ^ SLOT_LANES[s]] = jnp.broadcast_to(block[None], (groups,) + block.shape)
    middle_out[...] = jnp.concatenate([middle, normed_pick.astype(F32)], axis=0).astype(BF16)


def front_types(tower, groups):
    return (
        shape_of((16, tower.width), BF16),
        shape_of((tower.padded, tower.width), BF16),
        shape_of((4, tower.padded, tower.part), BF16),
        shape_of((4, tower.padded, tower.part), BF16),
        shape_of((4, tower.heads * 8, tower.padded), F32),
        shape_of((4, 8, tower.part), BF16),
        shape_of((groups, 4, tower.heads * 8, tower.width), BF16),
    )


def window(first, last, tower):
    low = first // tower.length * tower.length // 16 * 16
    high = -(-(((last - 1) // tower.length + 1) * tower.length) // 16) * 16
    return low, min(high, tower.padded)


def mix_body(tower, ins, outs):
    tokens, gains, shifts, lens, normed, keys, values, slots = ins
    middle_out, normed_out = outs
    length, heads, rows = tower.length, tower.heads, tower.padded
    tile = 160 if length == CTX else 112
    row = iota((rows, 1), 0)
    low = jnp.zeros((rows, 1), jnp.int32)
    high = jnp.zeros((rows, 1), jnp.int32)
    for n in range(tower.seqs):
        here = (row >= n * length) & (row < (n + 1) * length)
        low = jnp.where(here, n * length, low)
        end = n * length + lens[n : n + 1, :]
        if length == CTX:
            end = jnp.minimum(end, row + 1)
        high = jnp.where(here, end, high)
    spans = [(first, min(first + tile, rows)) for first in range(0, rows, tile)]
    allowed = []
    for first, last in spans:
        start, stop = window(first, last, tower)
        col = iota((heads * (last - first), stop - start), 1) + start
        lows, highs = (jnp.concatenate([v[first:last]] * heads, axis=0) for v in (low, high))
        allowed.append((col >= lows) & (col < highs))
    held = normed[...]
    middle = tokens[...].astype(F32)
    lane_head = iota((1, tower.part), 1) >> 6
    for s in range(4):
        query = tower.into(held, slots[s][0]).astype(BF16)
        mixes = []
        for (first, last), mask in zip(spans, allowed, strict=True):
            start, stop = window(first, last, tower)
            mine = query[first:last].astype(F32) * SCALE
            stacked = jnp.concatenate([jnp.where(lane_head == h, mine, 0.0) for h in range(heads)], axis=0).astype(BF16)
            scores = jnp.where(mask, nt(stacked, keys[s, start:stop, :]), -1e9)
            weights = jnp.exp(scores - jnp.max(scores, axis=-1, keepdims=True))
            prob = (weights * (1.0 / jnp.sum(weights, axis=-1, keepdims=True))).astype(BF16)
            every = nn(prob, values[s, start:stop, :])
            size = last - first
            mix = jnp.where(lane_head == 0, every[:size], 0.0)
            for h in range(1, heads):
                mix = mix + jnp.where(lane_head == h, every[h * size : (h + 1) * size], 0.0)
            mixes.append(mix)
        middle = middle + tower.through(jnp.concatenate(mixes, axis=0).astype(BF16), slots[s][3])
    middle_out[...] = middle
    unit, _ = norm_parts(middle)
    normed_out[...] = (unit * gains[1:2, :] + shifts[1:2, :]).astype(BF16)


def mlp_body(tower, ins, outs):
    middle, normed, after, slots = ins
    final = middle[...]
    held = normed[...]
    for slot in slots:
        pre = nt(held, slot[0])
        final = final + nn((pre * sigmoid(1.702 * pre)).astype(BF16), slot[1])
    outs[0][...] = final[: tower.rows].astype(BF16)


def mlp_head_forward(tower, middle, gains, shifts, slots, proj, keep):
    unit_two, inv_two = norm_parts(middle)
    normed_two = (unit_two * gains[1:2, :] + shifts[1:2, :]).astype(BF16)
    final = middle
    pres, hids = [], []
    for slot in slots:
        pre = nt(normed_two, slot[0])
        hid = (pre * sigmoid(1.702 * pre)).astype(BF16)
        final = final + nn(hid, slot[1])
        pres.append(pre if keep else None)
        hids.append(hid)
    unit_head, inv_head = norm_parts(final)
    normed_head = (unit_head * gains[2:3, :] + shifts[2:3, :]).astype(BF16)
    embedding = nn(normed_head, proj[...])
    inv_len = lax.rsqrt(jnp.sum(embedding * embedding, axis=-1, keepdims=True) + 1e-06)
    unit = (embedding * inv_len).astype(BF16)
    return unit, (unit_two, inv_two, normed_two, pres, hids[0], unit_head, inv_head, normed_head, embedding, inv_len)


def mlp_head_backward(tower, grad_unit, kept, gains, slots, proj):
    unit_two, inv_two, normed_two, pres, hid, unit_head, inv_head, normed_head, embedding, inv_len = kept
    along = jnp.sum(embedding * grad_unit, axis=-1, keepdims=True)
    grad_emb = (inv_len * grad_unit - inv_len * inv_len * inv_len * embedding * along).astype(BF16)
    proj_grad = tn(normed_head, grad_emb)
    grad_final, gain_2, shift_2 = norm_back(nt(grad_emb, proj[...]), unit_head, inv_head, gains[2:3, :])
    grad_mlp = grad_final.astype(BF16)
    grad_two = None
    again = normed_two if pres[0] is not None else lax.optimization_barrier((normed_two, grad_mlp))[0]
    for slot, pre in zip(slots, pres, strict=True):
        if pre is None:
            pre = nt(again, slot[0])
        gate = sigmoid(1.702 * pre)
        slope = gate + 1.702 * pre * gate * (1.0 - gate)
        grad_pre = (nt(grad_mlp, slot[1]) * slope).astype(BF16)
        part = nn(grad_pre, slot[0])
        grad_two = part if grad_two is None else grad_two + part
        if slot is slots[0]:
            down_grad = tn(hid, grad_mlp)
            up_grad = tn(normed_two, grad_pre)
    back, gain_1, shift_1 = norm_back(grad_two, unit_two, inv_two, gains[1:2, :])
    grad_middle = grad_final + back
    gains_grad = jnp.concatenate([gain_1, gain_2], axis=0)
    shifts_grad = jnp.concatenate([shift_1, shift_2], axis=0)
    return grad_middle, up_grad, down_grad, proj_grad, gains_grad, shifts_grad


def total(v):
    return jnp.sum(jnp.sum(v, axis=1, keepdims=True), axis=0, keepdims=True)


def contrast(image_unit, text_unit, logit_scale):
    factor = jnp.exp(logit_scale[...])
    logits = factor * nt(image_unit, text_unit)
    count = logits.shape[0]
    row_top = jnp.max(logits, axis=1, keepdims=True)
    row_lse = row_top + jnp.log(jnp.sum(jnp.exp(logits - row_top), axis=1, keepdims=True))
    col_top = jnp.max(logits, axis=0, keepdims=True)
    col_lse = col_top + jnp.log(jnp.sum(jnp.exp(logits - col_top), axis=0, keepdims=True))
    eye = iota(logits.shape, 0) == iota(logits.shape, 1)
    diag = total(jnp.where(eye, logits, 0.0))
    loss = (0.5 * (total(row_lse) + total(col_lse)) - diag) / count
    grad = 0.5 * (jnp.exp(logits - row_lse) + jnp.exp(logits - col_lse))
    low = jnp.where(eye, grad - 1.0, grad).astype(BF16)
    scale_grad = total(low.astype(F32) * logits)
    grad_image = factor * nn(low, text_unit)
    grad_text = factor * tn(low, image_unit)
    return loss, scale_grad, grad_image, grad_text


def pooled_back(towers, devices, one_hot, place, mids, after, image, text, logit_scale, *held):
    seqs = towers[0].seqs
    pairs, spread = devices * seqs, devices * 8
    own_mids, other_mids = mids
    core = place[0] & 1
    if one_hot:
        pair = iota((pairs, 1), 0)
        device = ((2 * pair + 1) * (65536 // (2 * seqs) + 1)) >> 16
        spot = (device >> 1) * 16 + (pair - device * seqs)
        spot = jnp.where((device & 1) == core, spot, spot + spread)
        pick = as_ones(iota((pairs, 2 * spread), 1) == spot).astype(BF16)
        row = iota((spread, 1), 0)
        true_row = row + place[1] * (spread // 2)
        true_row = jnp.where(true_row >= spread, true_row - spread, true_row)
        spot = (true_row >> 4) * 16 + 8 + (row & 7)
        spot = jnp.where(((true_row >> 3) & 1) == core, spot, spot + spread)
        pick_first = as_ones(iota((spread, 2 * spread), 1) == spot).astype(BF16)
        split = towers[0].width
        both = [
            jnp.concatenate([own_mids[:, cut], other_mids[:, cut]], axis=0)
            for cut in (slice(0, split), slice(split, split + towers[1].width))
        ]
        rows = []
        for ref, v in zip(held, both, strict=True):
            ref[...] = jnp.maximum(nn(pick, v), -3.0e38)
            rows.append(ref[...])
        firsts = [nn(pick_first, v).astype(BF16) for v in both]
        back_shape = (spread, pairs)
        place_back = as_ones(iota(back_shape, 0) == widen(pairs, seqs, place[1]))
        own_shape = (8, pairs)
        own_row = iota((8, 1), 0)
        pick_mine = as_ones(iota(own_shape, 1) == jnp.where(own_row < seqs, place[0] * seqs + own_row, -1))
    else:
        both = jnp.stack([own_mids, other_mids]).reshape(2, devices // 2, 16, own_mids.shape[-1])
        both = jnp.where(core == 0, both, both[::-1])
        both = jnp.swapaxes(both, 0, 1).reshape(devices, 16, -1)
        rows = both[:, :seqs].reshape(pairs, -1).astype(F32)
        rows = [rows[:, : towers[0].width], rows[:, towers[0].width :]]
        firsts = own_half_first(both[:, 8:].reshape(spread, -1), place[1])
        firsts = [firsts[:, : towers[0].width], firsts[:, towers[0].width :]]
    units, kept = [], []
    for tower, middle, (gains, shifts, slots, proj) in zip(towers, rows, (image, text), strict=True):
        unit, state = mlp_head_forward(tower, middle, gains, shifts, slots, proj, one_hot)
        units.append(unit)
        kept.append(state)
    loss, scale_grad, grad_image, grad_text = contrast(units[0], units[1], logit_scale)
    results = ()
    for tower, grad, state, first, (gains, shifts, slots, proj) in zip(towers, (grad_image, grad_text), kept, firsts, (image, text), strict=True):
        grad_middle, *rest = mlp_head_backward(tower, grad, state, gains, slots, proj)
        low = grad_middle.astype(BF16)
        if one_hot:
            branch = nn(place_back.astype(BF16), low).astype(BF16)
            own = exact_nn(pick_mine, grad_middle)
        else:
            branch = jnp.pad(low.reshape(devices, seqs, -1), ((0, 0), (0, 8 - seqs), (0, 0))).reshape(spread, -1)
            branch = own_half_first(branch, place[1])
            own = jnp.pad(lax.dynamic_slice(grad_middle, (place[0] * seqs, 0), (seqs, tower.width)), ((0, 8 - seqs), (0, 0)))
        results += (own, branch, first) + tuple(rest)
    return results + (loss, scale_grad)


def own_half_first(rows, turn):
    half = rows.shape[0] // 2
    return jnp.where(turn == 0, rows, jnp.concatenate([rows[half:], rows[:half]], axis=0))


def widen(pairs, seqs, turn):
    pair = iota((1, pairs), 1)
    device = ((2 * pair + 1) * (65536 // (2 * seqs) + 1)) >> 16
    spread = pairs // seqs * 8
    row = device * 8 + (pair - device * seqs) + turn * (spread // 2)
    return jnp.where(row >= spread, row - spread, row)


def pooled_types(tower, spread, slots, proj):
    width = tower.width
    return (
        shape_of((8, width), F32),
        shape_of((spread, width), BF16),
        shape_of((spread, width), BF16),
        shape_of((width, slots[0].shape[1]), F32),
        shape_of((slots[0].shape[1], width), F32),
        shape_of(proj.shape, F32),
        shape_of((2, width), F32),
        shape_of((2, width), F32),
    )


def back_body(tower, groups, ins, outs):
    tokens, gains, lens, lane, grad_rows, normed, keys, values, probs, queries, slots = ins
    grad_out, late_out = outs
    heads = tower.heads
    unit, inv = norm_parts(tokens[...].astype(F32))
    mask = head_mask(heads)
    held = normed[...]
    grad_rows = grad_rows[...]
    branch = grad_rows.astype(BF16)
    left, right, y_keys, g_queries = [], [], [], []
    query_side = None
    for s in range(4):
        grad_mixed = tower.through_back(branch, slots[s][3]).astype(BF16)
        spread = spread_heads(grad_mixed, mask, heads).astype(BF16)
        grad_probs = nt(spread, values[s])
        prob = probs[s]
        grad_scores = (prob * (grad_probs - jnp.sum(prob * grad_probs, axis=-1, keepdims=True))).astype(BF16)
        grad_query = (fold_heads(nn(grad_scores, keys[s]), mask, heads) * SCALE).astype(BF16)
        part = tower.outof(grad_query, slots[s][0])
        query_side = part if query_side is None else query_side + part
        wide = (spread_heads(queries[s], mask, heads) * SCALE).astype(BF16)
        left += [grad_scores, prob.astype(BF16)]
        right += [tower.outof(wide, slots[s][1]).astype(BF16), tower.outof(spread, slots[s][2]).astype(BF16)]
        y_keys.append(nn(grad_scores, held))
        g_queries.append(grad_query)
    pick = pick_rows(lens, tower.length, tower.padded)
    grad_one = tn(jnp.concatenate(left, axis=0), jnp.concatenate(right, axis=0))
    grad_one = grad_one + tn(pick.astype(BF16), query_side.astype(BF16))
    back, gain_0, shift_0 = norm_back(grad_one, unit, inv, gains[0:1, :])
    grad_tokens = exact_tn(pick, grad_rows) + back
    grad_out[...] = grad_tokens[: tower.rows].astype(BF16)
    for s in range(4):
        halves = lane_rows(tower, g_queries[s])
        block = fill_spare(y_keys[s], ((6, gain_0), (7, shift_0), (14, halves[0]), (15, halves[1]))).astype(BF16)
        late_out[:, lane[0] ^ SLOT_LANES[s]] = jnp.broadcast_to(block[None], (groups,) + block.shape)


def back_types(tower, groups):
    return (
        shape_of((tower.rows, tower.width), BF16),
        shape_of((groups, 4, tower.heads * 8, tower.width), BF16),
    )


def last_step(tower, devices, one_hot, branch, first, wq, wo, early, late, gains, shifts):
    heads, part, piece = tower.heads, tower.part, tower.piece
    spread = devices * 8
    lane_head = iota((1, 1, 1, part), 3) >> 6

    def spare_rows(block, per, place):
        if not one_hot:
            return block.reshape(devices, per, -1)[:, place]
        shape = (devices, devices * per)
        return nn(as_ones(iota(shape, 1) == iota((devices, 1), 0) * per + place).astype(BF16), block).astype(BF16)

    def sum_rows(block, per, place):
        if not one_hot:
            return jnp.sum(block.reshape(devices, per, -1)[:, place].astype(F32), axis=0, keepdims=True)
        return jnp.sum(spare_rows(block, per, place).astype(F32), axis=0, keepdims=True)

    def small_rows(block, per):
        halves = (spare_rows(block, per, 14), spare_rows(block, per, 15))
        if not one_hot:
            both = jnp.concatenate(halves, axis=1).reshape(devices, -1, piece)[:, :8, :part]
            both = jnp.pad(both[:, : tower.seqs], ((0, 0), (0, 8 - tower.seqs), (0, 0)))
            return both.reshape(spread, part)
        row, col = iota((spread, devices), 0), iota((spread, devices), 1)
        rows = None
        for n in range(tower.seqs):
            here = n % tower.per_row * piece
            one = nn(as_ones((row >> 3 == col) & ((row & 7) == n)).astype(BF16), halves[n // tower.per_row][:, here : here + part])
            rows = one if rows is None else rows + one
        return rows.astype(BF16)

    def by_head(rows, per):
        blocks = per // 8
        wide = jnp.broadcast_to(rows.reshape(devices, 1, 8, part), (devices, blocks, 8, part))
        number = iota((1, blocks, 1, 1), 1)
        return jnp.where(lane_head == number, wide, 0.0).reshape(devices * per, part).astype(BF16)

    def pair(left, right):
        return tn(right, left) if tower.flip else tn(left, right)

    per = heads * 8
    branch, first = branch[...], first[...]
    early, late = (jnp.concatenate([v[0][...], v[1][...]], axis=0) for v in (early, late))
    queries = tower.into(first, wq[...]).astype(BF16).astype(F32) * SCALE
    grad_mixed = nt(branch, wo[...]).astype(BF16).astype(F32)
    mixes = small_rows(early, per)
    grad_queries = small_rows(late, per)
    q_part = pair(first, grad_queries)
    k_part = pair(late, by_head(queries, per))
    v_part = pair(early, by_head(grad_mixed, per))
    out_grad = tn(mixes, branch)
    gains_grad = jnp.concatenate([sum_rows(late, per, 6), gains[...]], axis=0)
    shifts_grad = jnp.concatenate([sum_rows(late, per, 7), shifts[...]], axis=0)
    return [q_part, k_part, v_part], out_grad, gains_grad, shifts_grad


def per_device(
    image_tokens, image_gains, image_shifts, image_qkv, image_out, image_up, image_down, image_proj,
    text_tokens, text_gains, text_shifts, text_qkv, text_out, text_up, text_down, text_proj,
    caption_lengths, logit_scale,
):
    every = ("x", "zh", "zb", "y", "c")
    devices = lax.axis_size(every)
    groups = devices // 8
    lane = lax.axis_index(("y", "c")).astype(jnp.int32).reshape(1)
    me = jnp.stack([lax.axis_index(every), lax.axis_index("x")]).astype(jnp.int32)
    seqs = image_tokens.shape[0] // PATCHES
    towers = (
        Tower(PATCHES, image_out.shape[0] // HEAD, image_tokens.shape[1], image_tokens.shape[0], seqs, True),
        Tower(CTX, text_out.shape[0] // HEAD, text_tokens.shape[1], text_tokens.shape[0], seqs, False),
    )
    small = devices * seqs <= ONE_KERNEL_ROWS
    image_lens = jnp.where(iota((8, 1), 0) < seqs, PATCHES, 0)
    own_lens = lax.dynamic_slice(caption_lengths, (lane[0] * seqs,), (seqs,))
    lens = (image_lens, jnp.pad(own_lens, (0, 8 - seqs)).reshape(8, 1))
    gains, shifts = (image_gains, text_gains), (image_shifts, text_shifts)
    tokens = tuple(jnp.pad(v, ((0, t.padded - t.rows), (0, 0))) for t, v in zip(towers, (image_tokens, text_tokens)))

    corner = lax.axis_index(("x", "zb"))

    def then(v, *before):
        return lax.optimization_barrier((v,) + before)[0]

    def quarter_over_y(quarters):
        return lax.ppermute(lax.dynamic_index_in_dim(quarters, corner, 0, keepdims=False), "y", SWAP)

    def gather(quarters, over, before, late):
        wide = jnp.broadcast_to(then(over, *before)[None], quarters.shape)
        across = lax.all_to_all(wide, ("x", "zb"), split_axis=0, concat_axis=0, tiled=True)
        across = then(across, *late)
        return [quarters, across, lax.ppermute(quarters, "c", SWAP), lax.ppermute(across, "c", SWAP)]

    def pair_of(up, down):
        return jnp.stack([up.T, down])

    text_quarters = jnp.concatenate([jnp.transpose(text_qkv, (1, 0, 2)), text_out.T[None]], axis=0)
    image_quarters = jnp.concatenate([jnp.transpose(image_qkv, (1, 2, 0)), image_out[None]], axis=0)
    image_pair, text_pair = pair_of(image_up, image_down), pair_of(text_up, text_down)
    def with_core(slots):
        return slots + [lax.ppermute(v, "c", SWAP) for v in slots]

    fourths = image_pair.reshape(2, 4, image_pair.shape[1] // 4, image_pair.shape[2])
    fourth = lax.dynamic_index_in_dim(fourths, corner, 1, keepdims=False)
    image_over = quarter_over_y(image_quarters)
    text_over = lax.ppermute(then(text_quarters, image_over), "y", SWAP)
    pair_over = lax.ppermute(then(fourth, image_over), "y", SWAP)
    text_across = lax.ppermute(then(text_pair, pair_over), "y", SWAP)
    image_attn = gather(image_quarters, image_over, (text_pair, fourth) + tokens, (pair_over,))
    beside_x, beside_z = lax.ppermute(pair_over, "x", SWAP), lax.ppermute(pair_over, "zb", SWAP)
    beside_xz = lax.ppermute(pair_over, ("x", "zb"), [(i, i ^ 3) for i in range(4)])
    text_core = lax.ppermute(text_quarters, "c", SWAP)
    image_mlp = with_core([image_pair, pair_over, beside_x, beside_z, beside_xz])
    text_mlp = with_core([text_pair, text_across])
    attn, mlp = [image_attn, None], (image_mlp, text_mlp)
    names = ("image", "text")

    fronts = [None, None]
    for i in (0, 1):
        if i == 1:
            attn[1] = [text_quarters, text_over, text_core, lax.ppermute(then(text_over, fronts[0][0]), "c", SWAP)]
            tokens = (tokens[0], then(tokens[1], beside_x, beside_z))
        fronts[i] = call(
            "front_" + names[i],
            lambda ins, outs, tower=towers[i]: front_body(tower, groups, ins, outs),
            front_types(towers[i], groups),
            (tokens[i], gains[i], shifts[i], lens[i], lane, attn[i]),
            2 * 10**9,
            smem=(lane,),
            stream=attn[i],
        )

    def same_core(v):
        wide = jnp.broadcast_to(v[None], (devices // 2,) + v.shape)
        got = lax.all_to_all(wide, ("x", "zh", "zb", "y"), split_axis=0, concat_axis=0, tiled=True)
        return got.reshape(-1, v.shape[-1])

    def swap_all(v):
        flat = v.reshape((devices // 2,) + v.shape[2:])
        got = lax.all_to_all(flat, ("zh", "zb", "y", "c"), split_axis=0, concat_axis=0, tiled=True)
        got = got.reshape(-1, v.shape[-1])
        return got, lax.ppermute(got, "x", SWAP)

    mids = same_core(then(jnp.concatenate([fronts[0][0], fronts[1][0]], axis=1), beside_xz))
    def mix(i, *before):
        types = (shape_of(tokens[i].shape, F32), shape_of(tokens[i].shape, BF16))
        front = fronts[i]
        args = (tokens[i], gains[i], shifts[i], lens[i], then(front[1], *before), front[2], front[3], attn[i])
        return call("mix_" + names[i], lambda ins, outs: mix_body(towers[i], ins, outs), types, args, 4 * 10**9, stream=attn[i])

    mixed = [None, mix(1, text_across)]
    mids = then(mids, mixed[1][1], *image_mlp[5:], *text_mlp[2:])
    mids = (mids, lax.ppermute(mids, "c", SWAP))
    early_image = swap_all(then(fronts[0][6], mids[0]))

    projs = (image_proj, text_proj)
    pools = [(gains[i], shifts[i], mlp[i], projs[i]) for i in range(2)]
    scale = logit_scale.reshape(1, 1)
    after = (mixed[1][1],) if small else ()
    args = (me, mids, after, pools[0], pools[1], scale)
    if small:
        types = ()
        for i in range(2):
            types += pooled_types(towers[i], devices * 8, mlp[i], projs[i])
        types += (shape_of((1, 1), F32),) * 2
        pooled = fused("pooled", lambda *v: pooled_back(towers, devices, True, *v), types, args, 10**10, (me,), tuple(pltpu.VMEM((devices * seqs, t.width), F32) for t in towers), mlp[0] + mlp[1] + list(projs), after)
    else:
        pooled = pooled_back(towers, devices, False, *args)
    pools = (pooled[:8], pooled[8:16])
    loss, scale_grad = pooled[16:]

    early = [early_image, swap_all(then(fronts[1][6], early_image[0], pools[0][0]))]
    backs, late = [], []
    for i in range(2):
        front = fronts[i]
        ahead = pools[i][0] if i == 0 else then(pools[i][0], backs[0][0])
        args = (tokens[i], gains[i], lens[i], lane, ahead, front[1], front[2], front[3], front[4], front[5], attn[i])
        backs.append(call(
            "back_" + names[i],
            lambda ins, outs, tower=towers[i]: back_body(tower, groups, ins, outs),
            back_types(towers[i], groups), args, 10**9, smem=(lane,), stream=attn[i],
        ))
        late.append(swap_all(then(backs[i][1], early[1][0], *(v[0] for v in late))))

    mixed[0] = mix(0, backs[1][0])
    blocks = [None, None]
    for i in (1, 0):
        types = (shape_of((towers[i].rows, towers[i].width), BF16),)
        after = mixed[0][1] if i == 1 else late[1][0]
        middle = then(mixed[i][0], early[0][1], early[1][1]) if i == 1 else mixed[i][0]
        args = (middle, mixed[i][1], after, mlp[i])
        blocks[i] = call("mlp_" + names[i], lambda ins, outs, tower=towers[i]: mlp_body(tower, ins, outs), types, args, 8 * 10**9, stream=mlp[i], idle=(after,))[0]

    ends = []
    own_q = (attn[0][0][0], attn[1][0][0])
    for i, wo in enumerate((image_out, text_out)):
        tower = towers[i]
        args = (pools[i][1], pools[i][2], own_q[i], wo, early[i], late[i], pools[i][6], pools[i][7])
        if small:
            types = (shape_of((3,) + own_q[i].shape, F32), shape_of(wo.shape, F32)) + (shape_of((3, tower.width), F32),) * 2
            ends.append(fused("last_" + names[i], lambda *v, tower=tower: last_step(tower, devices, True, *v), types, args, 10**9))
        else:
            grads, *rest = last_step(tower, devices, False, *args)
            ends.append((jnp.stack(grads), *rest))

    image_qkv_grad = jnp.transpose(jnp.asarray(ends[0][0]), (2, 0, 1))
    text_qkv_grad = jnp.transpose(jnp.asarray(ends[1][0]), (1, 0, 2))
    results = ()
    for i, qkv_grad in enumerate((image_qkv_grad, text_qkv_grad)):
        own, branch, first, up_grad, down_grad, proj_grad, _, _ = pools[i]
        results += (blocks[i], backs[i][0], qkv_grad, ends[i][1], up_grad, down_grad, ends[i][2], ends[i][3], proj_grad)
    return results + (scale_grad.reshape(1), loss.reshape(1))


def solution(mesh):
    towers, batches, tensors = (mesh.shape[a] for a in ("tower", "batch", "tensor"))
    fine = Mesh(mesh.devices.reshape(towers, batches // 2, 2, tensors // 2, 2), ("x", "zh", "zb", "y", "c"))
    rows = P(("x", "zh", "zb", "y", "c"), None)
    lanes = ("y", "c")
    weights = (P(None, None, lanes), P(lanes, None), P(None, lanes), P(lanes, None))
    tower_in = (rows, P(), P()) + weights + (P(),)
    tower_out = (rows, rows) + weights + (P(), P(), P())
    return jax.shard_map(
        per_device,
        mesh=fine,
        in_specs=tower_in + tower_in + (P(("x", "zh", "zb")), P()),
        out_specs=tower_out + tower_out + (P(), P()),
        check_vma=False,
    )
```

```python
import jax
import jax.numpy as jnp
from jax import lax
from jax.experimental import pallas as pl
from jax.experimental.pallas import tpu as pltpu
from jax.sharding import Mesh, PartitionSpec as P

HEAD = 64
PATCHES = 50
CTX = 77
EPS = 1e-05
F32 = jnp.float32
BF16 = jnp.bfloat16
HIGH = lax.Precision.HIGHEST
SCALE = HEAD**-0.5
SWAP = [(0, 1), (1, 0)]
ONE_KERNEL_ROWS = 256
SLOT_LANES = (0, 2, 1, 3)
VMEM_BYTES = 60 * 1024 * 1024


def nn(a, b):
    return lax.dot_general(a, b, (((1,), (0,)), ((), ())), preferred_element_type=F32)


def nt(a, b):
    return lax.dot_general(a, b, (((1,), (1,)), ((), ())), preferred_element_type=F32)


def tn(a, b):
    return lax.dot_general(a, b, (((0,), (0,)), ((), ())), preferred_element_type=F32)


def exact_nn(a, b):
    return lax.dot_general(
        a, b, (((1,), (0,)), ((), ())), precision=HIGH, preferred_element_type=F32
    )


def exact_tn(a, b):
    return lax.dot_general(
        a, b, (((0,), (0,)), ((), ())), precision=HIGH, preferred_element_type=F32
    )


def iota(shape, dim):
    return lax.broadcasted_iota(jnp.int32, shape, dim)


def norm_parts(v):
    mean = jnp.mean(v, axis=-1, keepdims=True)
    centred = v - mean
    inv = lax.rsqrt(jnp.mean(centred * centred, axis=-1, keepdims=True) + EPS)
    return centred * inv, inv


def norm_back(o, unit, inv, gain):
    scaled = o * gain
    mean_o = jnp.mean(scaled, axis=-1, keepdims=True)
    mean_u = jnp.mean(scaled * unit, axis=-1, keepdims=True)
    back = inv * (scaled - mean_o - unit * mean_u)
    return back, jnp.sum(o * unit, axis=0, keepdims=True), jnp.sum(o, axis=0, keepdims=True)


def sigmoid(v):
    return 0.5 + 0.5 * jnp.tanh(0.5 * v)


def shape_of(shape, dtype):
    return jax.ShapeDtypeStruct(shape, dtype)


class Streamed:
    def __init__(self, source, held, done):
        self.held, self.waiting = held, pltpu.make_async_copy(source, held, done)
        self.waiting.start()

    @property
    def shape(self):
        return self.held.shape

    def __getitem__(self, index):
        if self.waiting is not None:
            self.waiting.wait()
            self.waiting = None
        return self.held[index]


def call(name, body, out_types, args, flops, smem=(), scratch=(), stream=(), idle=()):
    flat, tree = jax.tree.flatten(args)
    count, total_outs = len(flat), len(out_types)
    moving = [i for i, v in enumerate(flat) if any(v is t for t in stream)]
    buffers = tuple(pltpu.VMEM(flat[i].shape, flat[i].dtype) for i in moving)

    def kernel(*refs):
        ins, outs, held = list(refs[:count]), refs[count : count + total_outs], refs[count + total_outs :]
        if moving:
            done = held[-1]
            for slot, i in enumerate(moving):
                ins[i] = Streamed(ins[i], held[slot], done.at[slot])
        body(jax.tree.unflatten(tree, ins), outs, *held[len(moving) : len(moving) + len(scratch)])

    moved = sum(v.size * v.dtype.itemsize for v in flat)
    spaces = [pltpu.SMEM if any(v is t for t in smem) else pltpu.VMEM for v in flat]
    for i, v in enumerate(flat):
        if i in moving or any(v is t for t in idle):
            spaces[i] = pl.ANY
    last = (pltpu.SemaphoreType.DMA((len(moving),)),) if moving else ()
    return pl.pallas_call(
        kernel,
        out_shape=out_types,
        in_specs=[pl.BlockSpec(memory_space=space) for space in spaces],
        scratch_shapes=buffers + tuple(scratch) + last,
        compiler_params=pltpu.CompilerParams(vmem_limit_bytes=VMEM_BYTES),
        cost_estimate=pl.CostEstimate(flops=flops, bytes_accessed=moved, transcendentals=0),
        name=name,
    )(*flat)


def fused(name, fn, out_types, args, flops, smem=(), scratch=(), stream=(), idle=()):
    def body(ins, outs, *held):
        for ref, value in zip(outs, fn(*ins, *held), strict=True):
            if isinstance(value, list):
                for i, part in enumerate(value):
                    ref[i] = part
            else:
                ref[...] = value

    return call(name, body, out_types, args, flops, smem, scratch, stream, idle)


def as_ones(mask):
    return jnp.where(mask, 1.0, 0.0)


def head_mask(heads):
    shape = (heads * 8, heads * HEAD)
    return (iota(shape, 0) >> 3) == (iota(shape, 1) >> 6)


def seq_mask(lens, heads, length, rows):
    lens_all = jnp.concatenate([lens[...]] * heads, axis=0)
    shape = (heads * 8, rows)
    low = (iota(shape, 0) & 7) * length
    col = iota(shape, 1)
    return (col >= low) & (col < low + lens_all)


def pick_rows(lens, length, rows):
    shape = (8, rows)
    held = lens[...]
    back = held - 1 if length == CTX else 0
    spot = jnp.where(held > 0, iota((8, 1), 0) * length + back, -1)
    return as_ones(iota(shape, 1) == spot)


def spread_heads(rows, mask, heads):
    return jnp.where(mask, jnp.concatenate([rows.astype(F32)] * heads, axis=0), 0.0)


def fold_heads(rows, mask, heads):
    kept = jnp.where(mask, rows, 0.0)
    total = kept[:8]
    for h in range(1, heads):
        total = total + kept[8 * h : 8 * h + 8]
    return total


class Tower:
    def __init__(self, length, heads, width, rows, seqs, flip):
        self.length, self.heads, self.width, self.rows, self.seqs, self.flip = length, heads, width, rows, seqs, flip
        self.part = heads * HEAD
        self.padded = -(-rows // 16) * 16
        self.piece = -(-self.part // 128) * 128
        self.per_row = width // self.piece

    def into(self, a, w):
        return nt(a, w) if self.flip else nn(a, w)

    def outof(self, a, w):
        return nn(a, w) if self.flip else nt(a, w)

    def through(self, a, w):
        return nn(a, w) if self.flip else nt(a, w)

    def through_back(self, a, w):
        return nt(a, w) if self.flip else nn(a, w)


def lane_rows(tower, small):
    shape = (tower.part, tower.piece)
    wide = nn(small, as_ones(iota(shape, 0) == iota(shape, 1)).astype(BF16))
    empty = jnp.zeros((1, tower.piece), F32)
    rows = []
    for first in (0, tower.per_row):
        ends = range(first, first + tower.per_row)
        rows.append(jnp.concatenate([wide[n : n + 1] if n < tower.seqs else empty for n in ends], axis=1))
    return rows


def fill_spare(rows, spare):
    row = iota(rows.shape, 0)
    for place, value in spare:
        rows = jnp.where(row == place, value, rows)
    return rows


def front_body(tower, groups, ins, outs):
    tokens, gains, shifts, lens, lane, slots = ins
    middle_out, normed_out, key_out, value_out, prob_out, query_out, early_out = outs
    heads = tower.heads
    low_tokens = tokens[...]
    unit, _ = norm_parts(low_tokens.astype(F32))
    normed = (unit * gains[0:1, :] + shifts[0:1, :]).astype(BF16)
    normed_out[...] = normed
    pick = pick_rows(lens, tower.length, tower.padded).astype(BF16)
    middle = nn(pick, low_tokens)
    normed_pick = nn(pick, normed).astype(BF16)
    allowed = seq_mask(lens, heads, tower.length, tower.padded)
    mask = head_mask(heads)
    for s in range(4):
        key = tower.into(normed, slots[s][1]).astype(BF16)
        value = tower.into(normed, slots[s][2]).astype(BF16)
        query = tower.into(normed_pick, slots[s][0]).astype(BF16)
        key_out[s] = key
        value_out[s] = value
        query_out[s] = query
        scores = nt(spread_heads(query, mask, heads).astype(BF16), key) * SCALE
        scores = jnp.where(allowed, scores, -1e9)
        weights = jnp.where(allowed, jnp.exp(scores - jnp.max(scores, axis=-1, keepdims=True)), 0.0)
        total = jnp.sum(weights, axis=-1, keepdims=True)
        prob = weights * (1.0 / jnp.where(total > 0.0, total, 1.0))
        prob_out[s] = prob
        low = prob.astype(BF16)
        mix = fold_heads(nn(low, value), mask, heads).astype(BF16)
        middle = middle + tower.through(mix, slots[s][3])
        halves = lane_rows(tower, mix)
        block = fill_spare(nn(low, normed), ((14, halves[0]), (15, halves[1]))).astype(BF16)
        early_out[:, lane[0] ^ SLOT_LANES[s]] = jnp.broadcast_to(block[None], (groups,) + block.shape)
    middle_out[...] = jnp.concatenate([middle, normed_pick.astype(F32)], axis=0).astype(BF16)


def front_types(tower, groups):
    return (
        shape_of((16, tower.width), BF16),
        shape_of((tower.padded, tower.width), BF16),
        shape_of((4, tower.padded, tower.part), BF16),
        shape_of((4, tower.padded, tower.part), BF16),
        shape_of((4, tower.heads * 8, tower.padded), F32),
        shape_of((4, 8, tower.part), BF16),
        shape_of((groups, 4, tower.heads * 8, tower.width), BF16),
    )


def window(first, last, tower):
    low = first // tower.length * tower.length // 16 * 16
    high = -(-(((last - 1) // tower.length + 1) * tower.length) // 16) * 16
    return low, min(high, tower.padded)


def mix_body(tower, ins, outs):
    tokens, gains, shifts, lens, normed, keys, values, slots = ins
    middle_out, normed_out = outs
    length, heads, rows = tower.length, tower.heads, tower.padded
    tile = 160 if length == CTX else 112
    row = iota((rows, 1), 0)
    low = jnp.zeros((rows, 1), jnp.int32)
    high = jnp.zeros((rows, 1), jnp.int32)
    for n in range(tower.seqs):
        here = (row >= n * length) & (row < (n + 1) * length)
        low = jnp.where(here, n * length, low)
        end = n * length + lens[n : n + 1, :]
        if length == CTX:
            end = jnp.minimum(end, row + 1)
        high = jnp.where(here, end, high)
    spans = [(first, min(first + tile, rows)) for first in range(0, rows, tile)]
    allowed = []
    for first, last in spans:
        start, stop = window(first, last, tower)
        col = iota((heads * (last - first), stop - start), 1) + start
        lows, highs = (jnp.concatenate([v[first:last]] * heads, axis=0) for v in (low, high))
        allowed.append((col >= lows) & (col < highs))
    held = normed[...]
    middle = tokens[...].astype(F32)
    lane_head = iota((1, tower.part), 1) >> 6
    for s in range(4):
        query = tower.into(held, slots[s][0]).astype(BF16)
        mixes = []
        for (first, last), mask in zip(spans, allowed, strict=True):
            start, stop = window(first, last, tower)
            mine = query[first:last].astype(F32) * SCALE
            stacked = jnp.concatenate([jnp.where(lane_head == h, mine, 0.0) for h in range(heads)], axis=0).astype(BF16)
            scores = jnp.where(mask, nt(stacked, keys[s, start:stop, :]), -1e9)
            weights = jnp.exp(scores - jnp.max(scores, axis=-1, keepdims=True))
            prob = (weights * (1.0 / jnp.sum(weights, axis=-1, keepdims=True))).astype(BF16)
            every = nn(prob, values[s, start:stop, :])
            size = last - first
            mix = jnp.where(lane_head == 0, every[:size], 0.0)
            for h in range(1, heads):
                mix = mix + jnp.where(lane_head == h, every[h * size : (h + 1) * size], 0.0)
            mixes.append(mix)
        middle = middle + tower.through(jnp.concatenate(mixes, axis=0).astype(BF16), slots[s][3])
    middle_out[...] = middle
    unit, _ = norm_parts(middle)
    normed_out[...] = (unit * gains[1:2, :] + shifts[1:2, :]).astype(BF16)


def mlp_body(tower, ins, outs):
    middle, normed, after, slots = ins
    final = middle[...]
    held = normed[...]
    for slot in slots:
        pre = nt(held, slot[0])
        final = final + nn((pre * sigmoid(1.702 * pre)).astype(BF16), slot[1])
    outs[0][...] = final[: tower.rows].astype(BF16)


def mlp_head_forward(tower, middle, gains, shifts, slots, proj, keep):
    unit_two, inv_two = norm_parts(middle)
    normed_two = (unit_two * gains[1:2, :] + shifts[1:2, :]).astype(BF16)
    final = middle
    pres, hids = [], []
    for slot in slots:
        pre = nt(normed_two, slot[0])
        hid = (pre * sigmoid(1.702 * pre)).astype(BF16)
        final = final + nn(hid, slot[1])
        pres.append(pre if keep else None)
        hids.append(hid)
    unit_head, inv_head = norm_parts(final)
    normed_head = (unit_head * gains[2:3, :] + shifts[2:3, :]).astype(BF16)
    embedding = nn(normed_head, proj[...])
    inv_len = lax.rsqrt(jnp.sum(embedding * embedding, axis=-1, keepdims=True) + 1e-06)
    unit = (embedding * inv_len).astype(BF16)
    return unit, (unit_two, inv_two, normed_two, pres, hids[0], unit_head, inv_head, normed_head, embedding, inv_len)


def mlp_head_backward(tower, grad_unit, kept, gains, slots, proj):
    unit_two, inv_two, normed_two, pres, hid, unit_head, inv_head, normed_head, embedding, inv_len = kept
    along = jnp.sum(embedding * grad_unit, axis=-1, keepdims=True)
    grad_emb = (inv_len * grad_unit - inv_len * inv_len * inv_len * embedding * along).astype(BF16)
    proj_grad = tn(normed_head, grad_emb)
    grad_final, gain_2, shift_2 = norm_back(nt(grad_emb, proj[...]), unit_head, inv_head, gains[2:3, :])
    grad_mlp = grad_final.astype(BF16)
    grad_two = None
    again = normed_two if pres[0] is not None else lax.optimization_barrier((normed_two, grad_mlp))[0]
    for slot, pre in zip(slots, pres, strict=True):
        if pre is None:
            pre = nt(again, slot[0])
        gate = sigmoid(1.702 * pre)
        slope = gate + 1.702 * pre * gate * (1.0 - gate)
        grad_pre = (nt(grad_mlp, slot[1]) * slope).astype(BF16)
        part = nn(grad_pre, slot[0])
        grad_two = part if grad_two is None else grad_two + part
        if slot is slots[0]:
            down_grad = tn(hid, grad_mlp)
            up_grad = tn(normed_two, grad_pre)
    back, gain_1, shift_1 = norm_back(grad_two, unit_two, inv_two, gains[1:2, :])
    grad_middle = grad_final + back
    gains_grad = jnp.concatenate([gain_1, gain_2], axis=0)
    shifts_grad = jnp.concatenate([shift_1, shift_2], axis=0)
    return grad_middle, up_grad, down_grad, proj_grad, gains_grad, shifts_grad


def total(v):
    return jnp.sum(jnp.sum(v, axis=1, keepdims=True), axis=0, keepdims=True)


def contrast(image_unit, text_unit, logit_scale):
    factor = jnp.exp(logit_scale[...])
    logits = factor * nt(image_unit, text_unit)
    count = logits.shape[0]
    row_top = jnp.max(logits, axis=1, keepdims=True)
    row_lse = row_top + jnp.log(jnp.sum(jnp.exp(logits - row_top), axis=1, keepdims=True))
    col_top = jnp.max(logits, axis=0, keepdims=True)
    col_lse = col_top + jnp.log(jnp.sum(jnp.exp(logits - col_top), axis=0, keepdims=True))
    eye = iota(logits.shape, 0) == iota(logits.shape, 1)
    diag = total(jnp.where(eye, logits, 0.0))
    loss = (0.5 * (total(row_lse) + total(col_lse)) - diag) / count
    grad = 0.5 * (jnp.exp(logits - row_lse) + jnp.exp(logits - col_lse))
    low = jnp.where(eye, grad - 1.0, grad).astype(BF16)
    scale_grad = total(low.astype(F32) * logits)
    grad_image = factor * nn(low, text_unit)
    grad_text = factor * tn(low, image_unit)
    return loss, scale_grad, grad_image, grad_text


def pooled_back(towers, devices, one_hot, place, mids, after, image, text, logit_scale, *held):
    seqs = towers[0].seqs
    pairs, spread = devices * seqs, devices * 8
    own_mids, other_mids = mids
    core = place[0] & 1
    if one_hot:
        pair = iota((pairs, 1), 0)
        device = ((2 * pair + 1) * (65536 // (2 * seqs) + 1)) >> 16
        spot = (device >> 1) * 16 + (pair - device * seqs)
        spot = jnp.where((device & 1) == core, spot, spot + spread)
        pick = as_ones(iota((pairs, 2 * spread), 1) == spot).astype(BF16)
        row = iota((spread, 1), 0)
        true_row = row + place[1] * (spread // 2)
        true_row = jnp.where(true_row >= spread, true_row - spread, true_row)
        spot = (true_row >> 4) * 16 + 8 + (row & 7)
        spot = jnp.where(((true_row >> 3) & 1) == core, spot, spot + spread)
        pick_first = as_ones(iota((spread, 2 * spread), 1) == spot).astype(BF16)
        split = towers[0].width
        both = [
            jnp.concatenate([own_mids[:, cut], other_mids[:, cut]], axis=0)
            for cut in (slice(0, split), slice(split, split + towers[1].width))
        ]
        rows = []
        for ref, v in zip(held, both, strict=True):
            ref[...] = jnp.maximum(nn(pick, v), -3.0e38)
            rows.append(ref[...])
        firsts = [nn(pick_first, v).astype(BF16) for v in both]
        back_shape = (spread, pairs)
        place_back = as_ones(iota(back_shape, 0) == widen(pairs, seqs, place[1]))
        own_shape = (8, pairs)
        own_row = iota((8, 1), 0)
        pick_mine = as_ones(iota(own_shape, 1) == jnp.where(own_row < seqs, place[0] * seqs + own_row, -1))
    else:
        both = jnp.stack([own_mids, other_mids]).reshape(2, devices // 2, 16, own_mids.shape[-1])
        both = jnp.where(core == 0, both, both[::-1])
        both = jnp.swapaxes(both, 0, 1).reshape(devices, 16, -1)
        rows = both[:, :seqs].reshape(pairs, -1).astype(F32)
        rows = [rows[:, : towers[0].width], rows[:, towers[0].width :]]
        firsts = own_half_first(both[:, 8:].reshape(spread, -1), place[1])
        firsts = [firsts[:, : towers[0].width], firsts[:, towers[0].width :]]
    units, kept = [], []
    for tower, middle, (gains, shifts, slots, proj) in zip(towers, rows, (image, text), strict=True):
        unit, state = mlp_head_forward(tower, middle, gains, shifts, slots, proj, one_hot)
        units.append(unit)
        kept.append(state)
    loss, scale_grad, grad_image, grad_text = contrast(units[0], units[1], logit_scale)
    results = ()
    for tower, grad, state, first, (gains, shifts, slots, proj) in zip(towers, (grad_image, grad_text), kept, firsts, (image, text), strict=True):
        grad_middle, *rest = mlp_head_backward(tower, grad, state, gains, slots, proj)
        low = grad_middle.astype(BF16)
        if one_hot:
            branch = nn(place_back.astype(BF16), low).astype(BF16)
            own = exact_nn(pick_mine, grad_middle)
        else:
            branch = jnp.pad(low.reshape(devices, seqs, -1), ((0, 0), (0, 8 - seqs), (0, 0))).reshape(spread, -1)
            branch = own_half_first(branch, place[1])
            own = jnp.pad(lax.dynamic_slice(grad_middle, (place[0] * seqs, 0), (seqs, tower.width)), ((0, 8 - seqs), (0, 0)))
        results += (own, branch, first) + tuple(rest)
    return results + (loss, scale_grad)


def own_half_first(rows, turn):
    half = rows.shape[0] // 2
    return jnp.where(turn == 0, rows, jnp.concatenate([rows[half:], rows[:half]], axis=0))


def widen(pairs, seqs, turn):
    pair = iota((1, pairs), 1)
    device = ((2 * pair + 1) * (65536 // (2 * seqs) + 1)) >> 16
    spread = pairs // seqs * 8
    row = device * 8 + (pair - device * seqs) + turn * (spread // 2)
    return jnp.where(row >= spread, row - spread, row)


def pooled_types(tower, spread, slots, proj):
    width = tower.width
    return (
        shape_of((8, width), F32),
        shape_of((spread, width), BF16),
        shape_of((spread, width), BF16),
        shape_of((width, slots[0].shape[1]), F32),
        shape_of((slots[0].shape[1], width), F32),
        shape_of(proj.shape, F32),
        shape_of((2, width), F32),
        shape_of((2, width), F32),
    )


def back_body(tower, groups, ins, outs):
    tokens, gains, lens, lane, grad_rows, normed, keys, values, probs, queries, slots = ins
    grad_out, late_out = outs
    heads = tower.heads
    unit, inv = norm_parts(tokens[...].astype(F32))
    mask = head_mask(heads)
    held = normed[...]
    grad_rows = grad_rows[...]
    branch = grad_rows.astype(BF16)
    left, right, y_keys, g_queries = [], [], [], []
    query_side = None
    for s in range(4):
        grad_mixed = tower.through_back(branch, slots[s][3]).astype(BF16)
        spread = spread_heads(grad_mixed, mask, heads).astype(BF16)
        grad_probs = nt(spread, values[s])
        prob = probs[s]
        grad_scores = (prob * (grad_probs - jnp.sum(prob * grad_probs, axis=-1, keepdims=True))).astype(BF16)
        grad_query = (fold_heads(nn(grad_scores, keys[s]), mask, heads) * SCALE).astype(BF16)
        part = tower.outof(grad_query, slots[s][0])
        query_side = part if query_side is None else query_side + part
        wide = (spread_heads(queries[s], mask, heads) * SCALE).astype(BF16)
        left += [grad_scores, prob.astype(BF16)]
        right += [tower.outof(wide, slots[s][1]).astype(BF16), tower.outof(spread, slots[s][2]).astype(BF16)]
        y_keys.append(nn(grad_scores, held))
        g_queries.append(grad_query)
    pick = pick_rows(lens, tower.length, tower.padded)
    grad_one = tn(jnp.concatenate(left, axis=0), jnp.concatenate(right, axis=0))
    grad_one = grad_one + tn(pick.astype(BF16), query_side.astype(BF16))
    back, gain_0, shift_0 = norm_back(grad_one, unit, inv, gains[0:1, :])
    grad_tokens = exact_tn(pick, grad_rows) + back
    grad_out[...] = grad_tokens[: tower.rows].astype(BF16)
    for s in range(4):
        halves = lane_rows(tower, g_queries[s])
        block = fill_spare(y_keys[s], ((6, gain_0), (7, shift_0), (14, halves[0]), (15, halves[1]))).astype(BF16)
        late_out[:, lane[0] ^ SLOT_LANES[s]] = jnp.broadcast_to(block[None], (groups,) + block.shape)


def back_types(tower, groups):
    return (
        shape_of((tower.rows, tower.width), BF16),
        shape_of((groups, 4, tower.heads * 8, tower.width), BF16),
    )


def last_step(tower, devices, one_hot, branch, first, wq, wo, early, late, gains, shifts):
    heads, part, piece = tower.heads, tower.part, tower.piece
    spread = devices * 8
    lane_head = iota((1, 1, 1, part), 3) >> 6

    def spare_rows(block, per, place):
        if not one_hot:
            return block.reshape(devices, per, -1)[:, place]
        shape = (devices, devices * per)
        return nn(as_ones(iota(shape, 1) == iota((devices, 1), 0) * per + place).astype(BF16), block).astype(BF16)

    def sum_rows(block, per, place):
        if not one_hot:
            return jnp.sum(block.reshape(devices, per, -1)[:, place].astype(F32), axis=0, keepdims=True)
        return jnp.sum(spare_rows(block, per, place).astype(F32), axis=0, keepdims=True)

    def small_rows(block, per):
        halves = (spare_rows(block, per, 14), spare_rows(block, per, 15))
        if not one_hot:
            both = jnp.concatenate(halves, axis=1).reshape(devices, -1, piece)[:, :8, :part]
            both = jnp.pad(both[:, : tower.seqs], ((0, 0), (0, 8 - tower.seqs), (0, 0)))
            return both.reshape(spread, part)
        row, col = iota((spread, devices), 0), iota((spread, devices), 1)
        rows = None
        for n in range(tower.seqs):
            here = n % tower.per_row * piece
            one = nn(as_ones((row >> 3 == col) & ((row & 7) == n)).astype(BF16), halves[n // tower.per_row][:, here : here + part])
            rows = one if rows is None else rows + one
        return rows.astype(BF16)

    def by_head(rows, per):
        blocks = per // 8
        wide = jnp.broadcast_to(rows.reshape(devices, 1, 8, part), (devices, blocks, 8, part))
        number = iota((1, blocks, 1, 1), 1)
        return jnp.where(lane_head == number, wide, 0.0).reshape(devices * per, part).astype(BF16)

    def pair(left, right):
        return tn(right, left) if tower.flip else tn(left, right)

    per = heads * 8
    branch, first = branch[...], first[...]
    early, late = (jnp.concatenate([v[0][...], v[1][...]], axis=0) for v in (early, late))
    queries = tower.into(first, wq[0]).astype(BF16).astype(F32) * SCALE
    grad_mixed = nt(branch, wo[...]).astype(BF16).astype(F32)
    mixes = small_rows(early, per)
    grad_queries = small_rows(late, per)
    q_part = pair(first, grad_queries)
    k_part = pair(late, by_head(queries, per))
    v_part = pair(early, by_head(grad_mixed, per))
    out_grad = tn(mixes, branch)
    gains_grad = jnp.concatenate([sum_rows(late, per, 6), gains[...]], axis=0)
    shifts_grad = jnp.concatenate([sum_rows(late, per, 7), shifts[...]], axis=0)
    return [q_part, k_part, v_part], out_grad, gains_grad, shifts_grad


def per_device(
    image_tokens, image_gains, image_shifts, image_qkv, image_out, image_up, image_down, image_proj,
    text_tokens, text_gains, text_shifts, text_qkv, text_out, text_up, text_down, text_proj,
    caption_lengths, logit_scale,
):
    every = ("x", "zh", "zb", "y", "c")
    devices = lax.axis_size(every)
    groups = devices // 8
    lane = lax.axis_index(("y", "c")).astype(jnp.int32).reshape(1)
    me = jnp.stack([lax.axis_index(every), lax.axis_index("x")]).astype(jnp.int32)
    seqs = image_tokens.shape[0] // PATCHES
    towers = (
        Tower(PATCHES, image_out.shape[0] // HEAD, image_tokens.shape[1], image_tokens.shape[0], seqs, True),
        Tower(CTX, text_out.shape[0] // HEAD, text_tokens.shape[1], text_tokens.shape[0], seqs, False),
    )
    small = devices * seqs <= ONE_KERNEL_ROWS
    image_lens = jnp.where(iota((8, 1), 0) < seqs, PATCHES, 0)
    own_lens = lax.dynamic_slice(caption_lengths, (lane[0] * seqs,), (seqs,))
    lens = (image_lens, jnp.pad(own_lens, (0, 8 - seqs)).reshape(8, 1))
    gains, shifts = (image_gains, text_gains), (image_shifts, text_shifts)
    tokens = tuple(jnp.pad(v, ((0, t.padded - t.rows), (0, 0))) for t, v in zip(towers, (image_tokens, text_tokens)))

    corner = lax.axis_index(("x", "zb"))

    def then(v, *before):
        return lax.optimization_barrier((v,) + before)[0]

    def quarter_over_y(quarters):
        return lax.ppermute(lax.dynamic_index_in_dim(quarters, corner, 0, keepdims=False), "y", SWAP)

    def gather(quarters, over, before, late):
        wide = jnp.broadcast_to(then(over, *before)[None], quarters.shape)
        across = lax.all_to_all(wide, ("x", "zb"), split_axis=0, concat_axis=0, tiled=True)
        across = then(across, *late)
        return [quarters, across, lax.ppermute(quarters, "c", SWAP), lax.ppermute(across, "c", SWAP)]

    def pair_of(up, down):
        return jnp.stack([up.T, down])

    text_quarters = jnp.concatenate([jnp.transpose(text_qkv, (1, 0, 2)), text_out.T[None]], axis=0)
    image_quarters = jnp.concatenate([jnp.transpose(image_qkv, (1, 2, 0)), image_out[None]], axis=0)
    image_pair, text_pair = pair_of(image_up, image_down), pair_of(text_up, text_down)
    def with_core(slots):
        return slots + [lax.ppermute(v, "c", SWAP) for v in slots]

    fourths = image_pair.reshape(2, 4, image_pair.shape[1] // 4, image_pair.shape[2])
    fourth = lax.dynamic_index_in_dim(fourths, corner, 1, keepdims=False)
    image_over = quarter_over_y(image_quarters)
    text_over = lax.ppermute(then(text_quarters, image_over), "y", SWAP)
    pair_over = lax.ppermute(then(fourth, image_over), "y", SWAP)
    text_across = lax.ppermute(then(text_pair, pair_over), "y", SWAP)
    image_attn = gather(image_quarters, image_over, (text_pair, fourth) + tokens, (pair_over,))
    beside_x, beside_z = lax.ppermute(pair_over, "x", SWAP), lax.ppermute(pair_over, "zb", SWAP)
    beside_xz = lax.ppermute(pair_over, ("x", "zb"), [(i, i ^ 3) for i in range(4)])
    text_core = lax.ppermute(text_quarters, "c", SWAP)
    image_mlp = with_core([image_pair, pair_over, beside_x, beside_z, beside_xz])
    text_mlp = with_core([text_pair, text_across])
    attn, mlp = [image_attn, None], (image_mlp, text_mlp)
    names = ("image", "text")

    fronts = [None, None]
    for i in (0, 1):
        if i == 1:
            attn[1] = [text_quarters, text_over, text_core, lax.ppermute(then(text_over, fronts[0][0]), "c", SWAP)]
            tokens = (tokens[0], then(tokens[1], beside_x, beside_z))
        fronts[i] = call(
            "front_" + names[i],
            lambda ins, outs, tower=towers[i]: front_body(tower, groups, ins, outs),
            front_types(towers[i], groups),
            (tokens[i], gains[i], shifts[i], lens[i], lane, attn[i]),
            2 * 10**9,
            smem=(lane,),
            stream=attn[i],
        )

    def same_core(v):
        wide = jnp.broadcast_to(v[None], (devices // 2,) + v.shape)
        got = lax.all_to_all(wide, ("x", "zh", "zb", "y"), split_axis=0, concat_axis=0, tiled=True)
        return got.reshape(-1, v.shape[-1])

    def swap_all(v):
        flat = v.reshape((devices // 2,) + v.shape[2:])
        got = lax.all_to_all(flat, ("zh", "zb", "y", "c"), split_axis=0, concat_axis=0, tiled=True)
        got = got.reshape(-1, v.shape[-1])
        return got, lax.ppermute(got, "x", SWAP)

    mids = same_core(then(jnp.concatenate([fronts[0][0], fronts[1][0]], axis=1), beside_xz))
    def mix(i, *before):
        types = (shape_of(tokens[i].shape, F32), shape_of(tokens[i].shape, BF16))
        front = fronts[i]
        args = (tokens[i], gains[i], shifts[i], lens[i], then(front[1], *before), front[2], front[3], attn[i])
        return call("mix_" + names[i], lambda ins, outs: mix_body(towers[i], ins, outs), types, args, 4 * 10**9, stream=attn[i])

    mixed = [None, mix(1, text_across)]
    mids = then(mids, mixed[1][1], *image_mlp[5:], *text_mlp[2:])
    mids = (mids, lax.ppermute(mids, "c", SWAP))
    early_image = swap_all(then(fronts[0][6], mids[0]))

    projs = (image_proj, text_proj)
    pools = [(gains[i], shifts[i], mlp[i], projs[i]) for i in range(2)]
    scale = logit_scale.reshape(1, 1)
    after = (mixed[1][1],) if small else ()
    args = (me, mids, after, pools[0], pools[1], scale)
    if small:
        types = ()
        for i in range(2):
            types += pooled_types(towers[i], devices * 8, mlp[i], projs[i])
        types += (shape_of((1, 1), F32),) * 2
        pooled = fused("pooled", lambda *v: pooled_back(towers, devices, True, *v), types, args, 10**10, (me,), tuple(pltpu.VMEM((devices * seqs, t.width), F32) for t in towers), mlp[0] + mlp[1] + list(projs), after)
    else:
        pooled = pooled_back(towers, devices, False, *args)
    pools = (pooled[:8], pooled[8:16])
    loss, scale_grad = pooled[16:]

    early = [early_image, swap_all(then(fronts[1][6], early_image[0], pools[0][0]))]
    backs, late = [], []
    for i in range(2):
        front = fronts[i]
        ahead = pools[i][0] if i == 0 else then(pools[i][0], backs[0][0])
        args = (tokens[i], gains[i], lens[i], lane, ahead, front[1], front[2], front[3], front[4], front[5], attn[i])
        backs.append(call(
            "back_" + names[i],
            lambda ins, outs, tower=towers[i]: back_body(tower, groups, ins, outs),
            back_types(towers[i], groups), args, 10**9, smem=(lane,), stream=attn[i],
        ))
        late.append(swap_all(then(backs[i][1], early[1][0], *(v[0] for v in late))))

    mixed[0] = mix(0, backs[1][0])
    blocks = [None, None]
    for i in (1, 0):
        types = (shape_of((towers[i].rows, towers[i].width), BF16),)
        after = mixed[0][1] if i == 1 else late[1][0]
        middle = then(mixed[i][0], early[0][1], early[1][1]) if i == 1 else mixed[i][0]
        args = (middle, mixed[i][1], after, mlp[i])
        blocks[i] = call("mlp_" + names[i], lambda ins, outs, tower=towers[i]: mlp_body(tower, ins, outs), types, args, 8 * 10**9, stream=mlp[i], idle=(after,))[0]

    ends = []
    own_q = (attn[0][0], attn[1][0])
    for i, wo in enumerate((image_out, text_out)):
        tower = towers[i]
        args = (pools[i][1], pools[i][2], own_q[i], wo, early[i], late[i], pools[i][6], pools[i][7])
        if small:
            types = (shape_of((3,) + own_q[i].shape[1:], F32), shape_of(wo.shape, F32)) + (shape_of((3, tower.width), F32),) * 2
            ends.append(fused("last_" + names[i], lambda *v, tower=tower: last_step(tower, devices, True, *v), types, args, 10**9))
        else:
            grads, *rest = last_step(tower, devices, False, *args)
            ends.append((jnp.stack(grads), *rest))

    image_qkv_grad = jnp.transpose(jnp.asarray(ends[0][0]), (2, 0, 1))
    text_qkv_grad = jnp.transpose(jnp.asarray(ends[1][0]), (1, 0, 2))
    results = ()
    for i, qkv_grad in enumerate((image_qkv_grad, text_qkv_grad)):
        own, branch, first, up_grad, down_grad, proj_grad, _, _ = pools[i]
        results += (blocks[i], backs[i][0], qkv_grad, ends[i][1], up_grad, down_grad, ends[i][2], ends[i][3], proj_grad)
    return results + (scale_grad.reshape(1), loss.reshape(1))


def solution(mesh):
    towers, batches, tensors = (mesh.shape[a] for a in ("tower", "batch", "tensor"))
    fine = Mesh(mesh.devices.reshape(towers, batches // 2, 2, tensors // 2, 2), ("x", "zh", "zb", "y", "c"))
    rows = P(("x", "zh", "zb", "y", "c"), None)
    lanes = ("y", "c")
    weights = (P(None, None, lanes), P(lanes, None), P(None, lanes), P(lanes, None))
    tower_in = (rows, P(), P()) + weights + (P(),)
    tower_out = (rows, rows) + weights + (P(), P(), P())
    return jax.shard_map(
        per_device,
        mesh=fine,
        in_specs=tower_in + tower_in + (P(("x", "zh", "zb")), P()),
        out_specs=tower_out + tower_out + (P(), P()),
        check_vma=False,
    )
```

```python
import jax
import jax.numpy as jnp
from jax import lax
from jax.experimental import pallas as pl
from jax.experimental.pallas import tpu as pltpu
from jax.sharding import Mesh, PartitionSpec as P

HEAD = 64
PATCHES = 50
CTX = 77
EPS = 1e-05
F32 = jnp.float32
BF16 = jnp.bfloat16
HIGH = lax.Precision.HIGHEST
SCALE = HEAD**-0.5
SWAP = [(0, 1), (1, 0)]
ONE_KERNEL_ROWS = 256
SLOT_LANES = (0, 2, 1, 3)
VMEM_BYTES = 60 * 1024 * 1024


def nn(a, b):
    return lax.dot_general(a, b, (((1,), (0,)), ((), ())), preferred_element_type=F32)


def nt(a, b):
    return lax.dot_general(a, b, (((1,), (1,)), ((), ())), preferred_element_type=F32)


def tn(a, b):
    return lax.dot_general(a, b, (((0,), (0,)), ((), ())), preferred_element_type=F32)


def exact_nn(a, b):
    return lax.dot_general(
        a, b, (((1,), (0,)), ((), ())), precision=HIGH, preferred_element_type=F32
    )


def exact_tn(a, b):
    return lax.dot_general(
        a, b, (((0,), (0,)), ((), ())), precision=HIGH, preferred_element_type=F32
    )


def iota(shape, dim):
    return lax.broadcasted_iota(jnp.int32, shape, dim)


def norm_parts(v):
    mean = jnp.mean(v, axis=-1, keepdims=True)
    centred = v - mean
    inv = lax.rsqrt(jnp.mean(centred * centred, axis=-1, keepdims=True) + EPS)
    return centred * inv, inv


def norm_back(o, unit, inv, gain):
    scaled = o * gain
    mean_o = jnp.mean(scaled, axis=-1, keepdims=True)
    mean_u = jnp.mean(scaled * unit, axis=-1, keepdims=True)
    back = inv * (scaled - mean_o - unit * mean_u)
    return back, jnp.sum(o * unit, axis=0, keepdims=True), jnp.sum(o, axis=0, keepdims=True)


def sigmoid(v):
    return 0.5 + 0.5 * jnp.tanh(0.5 * v)


def shape_of(shape, dtype):
    return jax.ShapeDtypeStruct(shape, dtype)


class Streamed:
    def __init__(self, source, held, done):
        self.held, self.waiting = held, pltpu.make_async_copy(source, held, done)
        self.waiting.start()

    @property
    def shape(self):
        return self.held.shape

    def __getitem__(self, index):
        if self.waiting is not None:
            self.waiting.wait()
            self.waiting = None
        return self.held[index]


def call(name, body, out_types, args, flops, smem=(), scratch=(), stream=(), idle=()):
    flat, tree = jax.tree.flatten(args)
    count, total_outs = len(flat), len(out_types)
    moving = [i for i, v in enumerate(flat) if any(v is t for t in stream)]
    buffers = tuple(pltpu.VMEM(flat[i].shape, flat[i].dtype) for i in moving)

    def kernel(*refs):
        ins, outs, held = list(refs[:count]), refs[count : count + total_outs], refs[count + total_outs :]
        if moving:
            done = held[-1]
            for slot, i in enumerate(moving):
                ins[i] = Streamed(ins[i], held[slot], done.at[slot])
        body(jax.tree.unflatten(tree, ins), outs, *held[len(moving) : len(moving) + len(scratch)])

    moved = sum(v.size * v.dtype.itemsize for v in flat)
    spaces = [pltpu.SMEM if any(v is t for t in smem) else pltpu.VMEM for v in flat]
    for i, v in enumerate(flat):
        if i in moving or any(v is t for t in idle):
            spaces[i] = pl.ANY
    last = (pltpu.SemaphoreType.DMA((len(moving),)),) if moving else ()
    return pl.pallas_call(
        kernel,
        out_shape=out_types,
        in_specs=[pl.BlockSpec(memory_space=space) for space in spaces],
        scratch_shapes=buffers + tuple(scratch) + last,
        compiler_params=pltpu.CompilerParams(vmem_limit_bytes=VMEM_BYTES),
        cost_estimate=pl.CostEstimate(flops=flops, bytes_accessed=moved, transcendentals=0),
        name=name,
    )(*flat)


def fused(name, fn, out_types, args, flops, smem=(), scratch=(), stream=(), idle=()):
    def body(ins, outs, *held):
        for ref, value in zip(outs, fn(*ins, *held), strict=True):
            if isinstance(value, list):
                for i, part in enumerate(value):
                    ref[i] = part
            else:
                ref[...] = value

    return call(name, body, out_types, args, flops, smem, scratch, stream, idle)


def as_ones(mask):
    return jnp.where(mask, 1.0, 0.0)


def head_mask(heads):
    shape = (heads * 8, heads * HEAD)
    return (iota(shape, 0) >> 3) == (iota(shape, 1) >> 6)


def seq_mask(lens, heads, length, rows):
    lens_all = jnp.concatenate([lens[...]] * heads, axis=0)
    shape = (heads * 8, rows)
    low = (iota(shape, 0) & 7) * length
    col = iota(shape, 1)
    return (col >= low) & (col < low + lens_all)


def pick_rows(lens, length, rows):
    shape = (8, rows)
    held = lens[...]
    back = held - 1 if length == CTX else 0
    spot = jnp.where(held > 0, iota((8, 1), 0) * length + back, -1)
    return as_ones(iota(shape, 1) == spot)


def spread_heads(rows, mask, heads):
    return jnp.where(mask, jnp.concatenate([rows.astype(F32)] * heads, axis=0), 0.0)


def fold_heads(rows, mask, heads):
    kept = jnp.where(mask, rows, 0.0)
    total = kept[:8]
    for h in range(1, heads):
        total = total + kept[8 * h : 8 * h + 8]
    return total


class Tower:
    def __init__(self, length, heads, width, rows, seqs, flip):
        self.length, self.heads, self.width, self.rows, self.seqs, self.flip = length, heads, width, rows, seqs, flip
        self.part = heads * HEAD
        self.padded = -(-rows // 16) * 16
        self.piece = -(-self.part // 128) * 128
        self.per_row = width // self.piece

    def into(self, a, w):
        return nt(a, w) if self.flip else nn(a, w)

    def outof(self, a, w):
        return nn(a, w) if self.flip else nt(a, w)

    def through(self, a, w):
        return nn(a, w) if self.flip else nt(a, w)

    def through_back(self, a, w):
        return nt(a, w) if self.flip else nn(a, w)


def lane_rows(tower, small):
    shape = (tower.part, tower.piece)
    wide = nn(small, as_ones(iota(shape, 0) == iota(shape, 1)).astype(BF16))
    empty = jnp.zeros((1, tower.piece), F32)
    rows = []
    for first in (0, tower.per_row):
        ends = range(first, first + tower.per_row)
        rows.append(jnp.concatenate([wide[n : n + 1] if n < tower.seqs else empty for n in ends], axis=1))
    return rows


def fill_spare(rows, spare):
    row = iota(rows.shape, 0)
    for place, value in spare:
        rows = jnp.where(row == place, value, rows)
    return rows


def front_body(tower, groups, ins, outs):
    tokens, gains, shifts, lens, lane, slots = ins
    middle_out, normed_out, key_out, value_out, prob_out, query_out, early_out = outs
    heads = tower.heads
    low_tokens = tokens[...]
    unit, _ = norm_parts(low_tokens.astype(F32))
    normed = (unit * gains[0:1, :] + shifts[0:1, :]).astype(BF16)
    normed_out[...] = normed
    pick = pick_rows(lens, tower.length, tower.padded).astype(BF16)
    middle = nn(pick, low_tokens)
    normed_pick = nn(pick, normed).astype(BF16)
    allowed = seq_mask(lens, heads, tower.length, tower.padded)
    mask = head_mask(heads)
    for s in range(4):
        key = tower.into(normed, slots[s][1]).astype(BF16)
        value = tower.into(normed, slots[s][2]).astype(BF16)
        query = tower.into(normed_pick, slots[s][0]).astype(BF16)
        key_out[s] = key
        value_out[s] = value
        query_out[s] = query
        scores = nt(spread_heads(query, mask, heads).astype(BF16), key) * SCALE
        scores = jnp.where(allowed, scores, -1e9)
        weights = jnp.where(allowed, jnp.exp(scores - jnp.max(scores, axis=-1, keepdims=True)), 0.0)
        total = jnp.sum(weights, axis=-1, keepdims=True)
        prob = weights * (1.0 / jnp.where(total > 0.0, total, 1.0))
        prob_out[s] = prob
        low = prob.astype(BF16)
        mix = fold_heads(nn(low, value), mask, heads).astype(BF16)
        middle = middle + tower.through(mix, slots[s][3])
        halves = lane_rows(tower, mix)
        block = fill_spare(nn(low, normed), ((14, halves[0]), (15, halves[1]))).astype(BF16)
        early_out[:, lane[0] ^ SLOT_LANES[s]] = jnp.broadcast_to(block[None], (groups,) + block.shape)
    middle_out[...] = jnp.concatenate([middle, normed_pick.astype(F32)], axis=0).astype(BF16)


def front_types(tower, groups):
    return (
        shape_of((16, tower.width), BF16),
        shape_of((tower.padded, tower.width), BF16),
        shape_of((4, tower.padded, tower.part), BF16),
        shape_of((4, tower.padded, tower.part), BF16),
        shape_of((4, tower.heads * 8, tower.padded), F32),
        shape_of((4, 8, tower.part), BF16),
        shape_of((groups, 4, tower.heads * 8, tower.width), BF16),
    )


def window(first, last, tower):
    low = first // tower.length * tower.length // 16 * 16
    high = -(-(((last - 1) // tower.length + 1) * tower.length) // 16) * 16
    return low, min(high, tower.padded)


def mix_body(tower, ins, outs):
    tokens, gains, shifts, lens, normed, keys, values, slots = ins
    middle_out, normed_out = outs
    length, heads, rows = tower.length, tower.heads, tower.padded
    tile = 160 if length == CTX else 112
    row = iota((rows, 1), 0)
    low = jnp.zeros((rows, 1), jnp.int32)
    high = jnp.zeros((rows, 1), jnp.int32)
    for n in range(tower.seqs):
        here = (row >= n * length) & (row < (n + 1) * length)
        low = jnp.where(here, n * length, low)
        end = n * length + lens[n : n + 1, :]
        if length == CTX:
            end = jnp.minimum(end, row + 1)
        high = jnp.where(here, end, high)
    spans = [(first, min(first + tile, rows)) for first in range(0, rows, tile)]
    allowed = []
    for first, last in spans:
        start, stop = window(first, last, tower)
        col = iota((heads * (last - first), stop - start), 1) + start
        lows, highs = (jnp.concatenate([v[first:last]] * heads, axis=0) for v in (low, high))
        allowed.append((col >= lows) & (col < highs))
    held = normed[...]
    middle = tokens[...].astype(F32)
    lane_head = iota((1, tower.part), 1) >> 6
    for s in range(4):
        query = tower.into(held, slots[s][0]).astype(BF16)
        mixes = []
        for (first, last), mask in zip(spans, allowed, strict=True):
            start, stop = window(first, last, tower)
            mine = query[first:last].astype(F32) * SCALE
            stacked = jnp.concatenate([jnp.where(lane_head == h, mine, 0.0) for h in range(heads)], axis=0).astype(BF16)
            scores = jnp.where(mask, nt(stacked, keys[s, start:stop, :]), -1e9)
            weights = jnp.exp(scores - jnp.max(scores, axis=-1, keepdims=True))
            prob = (weights * (1.0 / jnp.sum(weights, axis=-1, keepdims=True))).astype(BF16)
            every = nn(prob, values[s, start:stop, :])
            size = last - first
            mix = jnp.where(lane_head == 0, every[:size], 0.0)
            for h in range(1, heads):
                mix = mix + jnp.where(lane_head == h, every[h * size : (h + 1) * size], 0.0)
            mixes.append(mix)
        middle = middle + tower.through(jnp.concatenate(mixes, axis=0).astype(BF16), slots[s][3])
    middle_out[...] = middle
    unit, _ = norm_parts(middle)
    normed_out[...] = (unit * gains[1:2, :] + shifts[1:2, :]).astype(BF16)


def mlp_body(tower, ins, outs):
    middle, normed, after, slots = ins
    final = middle[...]
    held = normed[...]
    for slot in slots:
        pre = nt(held, slot[0])
        final = final + nn((pre * sigmoid(1.702 * pre)).astype(BF16), slot[1])
    outs[0][...] = final[: tower.rows].astype(BF16)


def mlp_head_forward(tower, middle, gains, shifts, slots, proj, keep):
    unit_two, inv_two = norm_parts(middle)
    normed_two = (unit_two * gains[1:2, :] + shifts[1:2, :]).astype(BF16)
    final = middle
    pres, hids = [], []
    for slot in slots:
        pre = nt(normed_two, slot[0])
        hid = (pre * sigmoid(1.702 * pre)).astype(BF16)
        final = final + nn(hid, slot[1])
        pres.append(pre if keep else None)
        hids.append(hid)
    unit_head, inv_head = norm_parts(final)
    normed_head = (unit_head * gains[2:3, :] + shifts[2:3, :]).astype(BF16)
    embedding = nn(normed_head, proj[...])
    inv_len = lax.rsqrt(jnp.sum(embedding * embedding, axis=-1, keepdims=True) + 1e-06)
    unit = (embedding * inv_len).astype(BF16)
    return unit, (unit_two, inv_two, normed_two, pres, hids[0], unit_head, inv_head, normed_head, embedding, inv_len)


def mlp_head_backward(tower, grad_unit, kept, gains, slots, proj):
    unit_two, inv_two, normed_two, pres, hid, unit_head, inv_head, normed_head, embedding, inv_len = kept
    along = jnp.sum(embedding * grad_unit, axis=-1, keepdims=True)
    grad_emb = (inv_len * grad_unit - inv_len * inv_len * inv_len * embedding * along).astype(BF16)
    proj_grad = tn(normed_head, grad_emb)
    grad_final, gain_2, shift_2 = norm_back(nt(grad_emb, proj[...]), unit_head, inv_head, gains[2:3, :])
    grad_mlp = grad_final.astype(BF16)
    grad_two = None
    again = normed_two if pres[0] is not None else lax.optimization_barrier((normed_two, grad_mlp))[0]
    for slot, pre in zip(slots, pres, strict=True):
        if pre is None:
            pre = nt(again, slot[0])
        gate = sigmoid(1.702 * pre)
        slope = gate + 1.702 * pre * gate * (1.0 - gate)
        grad_pre = (nt(grad_mlp, slot[1]) * slope).astype(BF16)
        part = nn(grad_pre, slot[0])
        grad_two = part if grad_two is None else grad_two + part
        if slot is slots[0]:
            down_grad = tn(hid, grad_mlp)
            up_grad = tn(normed_two, grad_pre)
    back, gain_1, shift_1 = norm_back(grad_two, unit_two, inv_two, gains[1:2, :])
    grad_middle = grad_final + back
    gains_grad = jnp.concatenate([gain_1, gain_2], axis=0)
    shifts_grad = jnp.concatenate([shift_1, shift_2], axis=0)
    return grad_middle, up_grad, down_grad, proj_grad, gains_grad, shifts_grad


def total(v):
    return jnp.sum(jnp.sum(v, axis=1, keepdims=True), axis=0, keepdims=True)


def contrast(image_unit, text_unit, logit_scale):
    factor = jnp.exp(logit_scale[...])
    logits = factor * nt(image_unit, text_unit)
    count = logits.shape[0]
    row_top = jnp.max(logits, axis=1, keepdims=True)
    row_lse = row_top + jnp.log(jnp.sum(jnp.exp(logits - row_top), axis=1, keepdims=True))
    col_top = jnp.max(logits, axis=0, keepdims=True)
    col_lse = col_top + jnp.log(jnp.sum(jnp.exp(logits - col_top), axis=0, keepdims=True))
    eye = iota(logits.shape, 0) == iota(logits.shape, 1)
    diag = total(jnp.where(eye, logits, 0.0))
    loss = (0.5 * (total(row_lse) + total(col_lse)) - diag) / count
    grad = 0.5 * (jnp.exp(logits - row_lse) + jnp.exp(logits - col_lse))
    low = jnp.where(eye, grad - 1.0, grad).astype(BF16)
    scale_grad = total(low.astype(F32) * logits)
    grad_image = factor * nn(low, text_unit)
    grad_text = factor * tn(low, image_unit)
    return loss, scale_grad, grad_image, grad_text


def pooled_back(towers, devices, one_hot, place, mids, after, image, text, logit_scale, *held):
    seqs = towers[0].seqs
    pairs, spread = devices * seqs, devices * 8
    own_mids, other_mids = mids
    core = place[0] & 1
    if one_hot:
        pair = iota((pairs, 1), 0)
        device = ((2 * pair + 1) * (65536 // (2 * seqs) + 1)) >> 16
        spot = (device >> 1) * 16 + (pair - device * seqs)
        spot = jnp.where((device & 1) == core, spot, spot + spread)
        pick = as_ones(iota((pairs, 2 * spread), 1) == spot).astype(BF16)
        row = iota((spread, 1), 0)
        true_row = row + place[1] * (spread // 2)
        true_row = jnp.where(true_row >= spread, true_row - spread, true_row)
        spot = (true_row >> 4) * 16 + 8 + (row & 7)
        spot = jnp.where(((true_row >> 3) & 1) == core, spot, spot + spread)
        pick_first = as_ones(iota((spread, 2 * spread), 1) == spot).astype(BF16)
        split = towers[0].width
        both = [
            jnp.concatenate([own_mids[:, cut], other_mids[:, cut]], axis=0)
            for cut in (slice(0, split), slice(split, split + towers[1].width))
        ]
        rows = []
        for ref, v in zip(held, both, strict=True):
            ref[...] = jnp.maximum(nn(pick, v), -3.0e38)
            rows.append(ref[...])
        firsts = [nn(pick_first, v).astype(BF16) for v in both]
        back_shape = (spread, pairs)
        place_back = as_ones(iota(back_shape, 0) == widen(pairs, seqs, place[1]))
        own_shape = (8, pairs)
        own_row = iota((8, 1), 0)
        pick_mine = as_ones(iota(own_shape, 1) == jnp.where(own_row < seqs, place[0] * seqs + own_row, -1))
    else:
        both = jnp.stack([own_mids, other_mids]).reshape(2, devices // 2, 16, own_mids.shape[-1])
        both = jnp.where(core == 0, both, both[::-1])
        both = jnp.swapaxes(both, 0, 1).reshape(devices, 16, -1)
        rows = both[:, :seqs].reshape(pairs, -1).astype(F32)
        rows = [rows[:, : towers[0].width], rows[:, towers[0].width :]]
        firsts = own_half_first(both[:, 8:].reshape(spread, -1), place[1])
        firsts = [firsts[:, : towers[0].width], firsts[:, towers[0].width :]]
    units, kept = [], []
    for tower, middle, (gains, shifts, slots, proj) in zip(towers, rows, (image, text), strict=True):
        unit, state = mlp_head_forward(tower, middle, gains, shifts, slots, proj, one_hot)
        units.append(unit)
        kept.append(state)
    loss, scale_grad, grad_image, grad_text = contrast(units[0], units[1], logit_scale)
    results = ()
    for tower, grad, state, first, (gains, shifts, slots, proj) in zip(towers, (grad_image, grad_text), kept, firsts, (image, text), strict=True):
        grad_middle, *rest = mlp_head_backward(tower, grad, state, gains, slots, proj)
        low = grad_middle.astype(BF16)
        if one_hot:
            branch = nn(place_back.astype(BF16), low).astype(BF16)
            own = exact_nn(pick_mine, grad_middle)
        else:
            branch = jnp.pad(low.reshape(devices, seqs, -1), ((0, 0), (0, 8 - seqs), (0, 0))).reshape(spread, -1)
            branch = own_half_first(branch, place[1])
            own = jnp.pad(lax.dynamic_slice(grad_middle, (place[0] * seqs, 0), (seqs, tower.width)), ((0, 8 - seqs), (0, 0)))
        results += (own, branch, first) + tuple(rest)
    return results + (loss, scale_grad)


def own_half_first(rows, turn):
    half = rows.shape[0] // 2
    return jnp.where(turn == 0, rows, jnp.concatenate([rows[half:], rows[:half]], axis=0))


def widen(pairs, seqs, turn):
    pair = iota((1, pairs), 1)
    device = ((2 * pair + 1) * (65536 // (2 * seqs) + 1)) >> 16
    spread = pairs // seqs * 8
    row = device * 8 + (pair - device * seqs) + turn * (spread // 2)
    return jnp.where(row >= spread, row - spread, row)


def pooled_types(tower, spread, slots, proj):
    width = tower.width
    return (
        shape_of((8, width), F32),
        shape_of((spread, width), BF16),
        shape_of((spread, width), BF16),
        shape_of((width, slots[0].shape[1]), F32),
        shape_of((slots[0].shape[1], width), F32),
        shape_of(proj.shape, F32),
        shape_of((2, width), F32),
        shape_of((2, width), F32),
    )


def back_body(tower, groups, ins, outs):
    tokens, gains, lens, lane, grad_rows, normed, keys, values, probs, queries, slots = ins
    grad_out, late_out = outs
    heads = tower.heads
    unit, inv = norm_parts(tokens[...].astype(F32))
    mask = head_mask(heads)
    held = normed[...]
    grad_rows = grad_rows[...]
    branch = grad_rows.astype(BF16)
    left, right, y_keys, g_queries = [], [], [], []
    query_side = None
    for s in range(4):
        grad_mixed = tower.through_back(branch, slots[s][3]).astype(BF16)
        spread = spread_heads(grad_mixed, mask, heads).astype(BF16)
        grad_probs = nt(spread, values[s])
        prob = probs[s]
        grad_scores = (prob * (grad_probs - jnp.sum(prob * grad_probs, axis=-1, keepdims=True))).astype(BF16)
        grad_query = (fold_heads(nn(grad_scores, keys[s]), mask, heads) * SCALE).astype(BF16)
        part = tower.outof(grad_query, slots[s][0])
        query_side = part if query_side is None else query_side + part
        wide = (spread_heads(queries[s], mask, heads) * SCALE).astype(BF16)
        left += [grad_scores, prob.astype(BF16)]
        right += [tower.outof(wide, slots[s][1]).astype(BF16), tower.outof(spread, slots[s][2]).astype(BF16)]
        y_keys.append(nn(grad_scores, held))
        g_queries.append(grad_query)
    pick = pick_rows(lens, tower.length, tower.padded)
    grad_one = tn(jnp.concatenate(left, axis=0), jnp.concatenate(right, axis=0))
    grad_one = grad_one + tn(pick.astype(BF16), query_side.astype(BF16))
    back, gain_0, shift_0 = norm_back(grad_one, unit, inv, gains[0:1, :])
    grad_tokens = exact_tn(pick, grad_rows) + back
    grad_out[...] = grad_tokens[: tower.rows].astype(BF16)
    for s in range(4):
        halves = lane_rows(tower, g_queries[s])
        block = fill_spare(y_keys[s], ((6, gain_0), (7, shift_0), (14, halves[0]), (15, halves[1]))).astype(BF16)
        late_out[:, lane[0] ^ SLOT_LANES[s]] = jnp.broadcast_to(block[None], (groups,) + block.shape)


def back_types(tower, groups):
    return (
        shape_of((tower.rows, tower.width), BF16),
        shape_of((groups, 4, tower.heads * 8, tower.width), BF16),
    )


def last_step(tower, devices, one_hot, branch, first, wq, wo, early, late, gains, shifts):
    heads, part, piece = tower.heads, tower.part, tower.piece
    spread = devices * 8
    lane_head = iota((1, 1, 1, part), 3) >> 6

    def spare_rows(block, per, place):
        if not one_hot:
            return block.reshape(devices, per, -1)[:, place]
        shape = (devices, devices * per)
        return nn(as_ones(iota(shape, 1) == iota((devices, 1), 0) * per + place).astype(BF16), block).astype(BF16)

    def sum_rows(block, per, place):
        if not one_hot:
            return jnp.sum(block.reshape(devices, per, -1)[:, place].astype(F32), axis=0, keepdims=True)
        return jnp.sum(spare_rows(block, per, place).astype(F32), axis=0, keepdims=True)

    def small_rows(block, per):
        halves = (spare_rows(block, per, 14), spare_rows(block, per, 15))
        if not one_hot:
            both = jnp.concatenate(halves, axis=1).reshape(devices, -1, piece)[:, :8, :part]
            both = jnp.pad(both[:, : tower.seqs], ((0, 0), (0, 8 - tower.seqs), (0, 0)))
            return both.reshape(spread, part)
        row, col = iota((spread, devices), 0), iota((spread, devices), 1)
        rows = None
        for n in range(tower.seqs):
            here = n % tower.per_row * piece
            one = nn(as_ones((row >> 3 == col) & ((row & 7) == n)).astype(BF16), halves[n // tower.per_row][:, here : here + part])
            rows = one if rows is None else rows + one
        return rows.astype(BF16)

    def by_head(rows, per):
        blocks = per // 8
        wide = jnp.broadcast_to(rows.reshape(devices, 1, 8, part), (devices, blocks, 8, part))
        number = iota((1, blocks, 1, 1), 1)
        return jnp.where(lane_head == number, wide, 0.0).reshape(devices * per, part).astype(BF16)

    def pair(left, right):
        return tn(right, left) if tower.flip else tn(left, right)

    per = heads * 8
    branch, first = branch[...], first[...]
    early, late = (jnp.concatenate([v[0][...], v[1][...]], axis=0) for v in (early, late))
    queries = tower.into(first, wq[0]).astype(BF16).astype(F32) * SCALE
    grad_mixed = nt(branch, wo[...]).astype(BF16).astype(F32)
    mixes = small_rows(early, per)
    grad_queries = small_rows(late, per)
    q_part = pair(first, grad_queries)
    k_part = pair(late, by_head(queries, per))
    v_part = pair(early, by_head(grad_mixed, per))
    out_grad = tn(mixes, branch)
    gains_grad = jnp.concatenate([sum_rows(late, per, 6), gains[...]], axis=0)
    shifts_grad = jnp.concatenate([sum_rows(late, per, 7), shifts[...]], axis=0)
    return [q_part, k_part, v_part], out_grad, gains_grad, shifts_grad


def per_device(
    image_tokens, image_gains, image_shifts, image_qkv, image_out, image_up, image_down, image_proj,
    text_tokens, text_gains, text_shifts, text_qkv, text_out, text_up, text_down, text_proj,
    caption_lengths, logit_scale,
):
    every = ("x", "zh", "zb", "y", "c")
    devices = lax.axis_size(every)
    groups = devices // 8
    lane = lax.axis_index(("y", "c")).astype(jnp.int32).reshape(1)
    me = jnp.stack([lax.axis_index(every), lax.axis_index("x")]).astype(jnp.int32)
    seqs = image_tokens.shape[0] // PATCHES
    towers = (
        Tower(PATCHES, image_out.shape[0] // HEAD, image_tokens.shape[1], image_tokens.shape[0], seqs, True),
        Tower(CTX, text_out.shape[0] // HEAD, text_tokens.shape[1], text_tokens.shape[0], seqs, False),
    )
    small = devices * seqs <= ONE_KERNEL_ROWS
    image_lens = jnp.where(iota((8, 1), 0) < seqs, PATCHES, 0)
    own_lens = lax.dynamic_slice(caption_lengths, (lane[0] * seqs,), (seqs,))
    lens = (image_lens, jnp.pad(own_lens, (0, 8 - seqs)).reshape(8, 1))
    gains, shifts = (image_gains, text_gains), (image_shifts, text_shifts)
    tokens = tuple(jnp.pad(v, ((0, t.padded - t.rows), (0, 0))) for t, v in zip(towers, (image_tokens, text_tokens)))

    corner = lax.axis_index(("x", "zb"))

    def then(v, *before):
        return lax.optimization_barrier((v,) + before)[0]

    def quarter_over_y(quarters):
        return lax.ppermute(lax.dynamic_index_in_dim(quarters, corner, 0, keepdims=False), "y", SWAP)

    def gather(quarters, over, before, late):
        wide = jnp.broadcast_to(then(over, *before)[None], quarters.shape)
        across = lax.all_to_all(wide, ("x", "zb"), split_axis=0, concat_axis=0, tiled=True)
        across = then(across, *late)
        return [quarters, across, lax.ppermute(quarters, "c", SWAP), lax.ppermute(across, "c", SWAP)]

    def pair_of(up, down):
        return jnp.stack([up.T, down])

    text_quarters = jnp.concatenate([jnp.transpose(text_qkv, (1, 0, 2)), text_out.T[None]], axis=0)
    image_quarters = jnp.concatenate([jnp.transpose(image_qkv, (1, 2, 0)), image_out[None]], axis=0)
    image_pair, text_pair = pair_of(image_up, image_down), pair_of(text_up, text_down)
    def with_core(slots):
        return slots + [lax.ppermute(v, "c", SWAP) for v in slots]

    fourths = image_pair.reshape(2, 4, image_pair.shape[1] // 4, image_pair.shape[2])
    fourth = lax.dynamic_index_in_dim(fourths, corner, 1, keepdims=False)
    image_over = quarter_over_y(image_quarters)
    text_over = lax.ppermute(then(text_quarters, image_over), "y", SWAP)
    pair_over = lax.ppermute(then(fourth, image_over), "y", SWAP)
    text_across = lax.ppermute(then(text_pair, pair_over), "y", SWAP)
    image_attn = gather(image_quarters, image_over, (text_pair, fourth) + tokens, (pair_over,))
    beside_x, beside_z = lax.ppermute(pair_over, "x", SWAP), lax.ppermute(pair_over, "zb", SWAP)
    beside_xz = lax.ppermute(pair_over, ("x", "zb"), [(i, i ^ 3) for i in range(4)])
    text_core = lax.ppermute(text_quarters, "c", SWAP)
    image_mlp = with_core([image_pair, pair_over, beside_x, beside_z, beside_xz])
    text_mlp = with_core([text_pair, text_across])
    attn, mlp = [image_attn, None], (image_mlp, text_mlp)
    names = ("image", "text")

    fronts = [None, None]
    for i in (0, 1):
        if i == 1:
            attn[1] = [text_quarters, text_over, text_core, lax.ppermute(then(text_over, fronts[0][0]), "c", SWAP)]
            tokens = (tokens[0], then(tokens[1], beside_x, beside_z))
        fronts[i] = call(
            "front_" + names[i],
            lambda ins, outs, tower=towers[i]: front_body(tower, groups, ins, outs),
            front_types(towers[i], groups),
            (tokens[i], gains[i], shifts[i], lens[i], lane, attn[i]),
            2 * 10**9,
            smem=(lane,),
        )

    def same_core(v):
        wide = jnp.broadcast_to(v[None], (devices // 2,) + v.shape)
        got = lax.all_to_all(wide, ("x", "zh", "zb", "y"), split_axis=0, concat_axis=0, tiled=True)
        return got.reshape(-1, v.shape[-1])

    def swap_all(v):
        flat = v.reshape((devices // 2,) + v.shape[2:])
        got = lax.all_to_all(flat, ("zh", "zb", "y", "c"), split_axis=0, concat_axis=0, tiled=True)
        got = got.reshape(-1, v.shape[-1])
        return got, lax.ppermute(got, "x", SWAP)

    mids = same_core(then(jnp.concatenate([fronts[0][0], fronts[1][0]], axis=1), beside_xz))
    def mix(i, *before):
        types = (shape_of(tokens[i].shape, F32), shape_of(tokens[i].shape, BF16))
        front = fronts[i]
        args = (tokens[i], gains[i], shifts[i], lens[i], then(front[1], *before), front[2], front[3], attn[i])
        return call("mix_" + names[i], lambda ins, outs: mix_body(towers[i], ins, outs), types, args, 4 * 10**9)

    mixed = [None, mix(1, text_across)]
    mids = then(mids, mixed[1][1], *image_mlp[5:], *text_mlp[2:])
    mids = (mids, lax.ppermute(mids, "c", SWAP))
    early_image = swap_all(then(fronts[0][6], mids[0]))

    projs = (image_proj, text_proj)
    pools = [(gains[i], shifts[i], mlp[i], projs[i]) for i in range(2)]
    scale = logit_scale.reshape(1, 1)
    after = (mixed[1][1],) if small else ()
    args = (me, mids, after, pools[0], pools[1], scale)
    if small:
        types = ()
        for i in range(2):
            types += pooled_types(towers[i], devices * 8, mlp[i], projs[i])
        types += (shape_of((1, 1), F32),) * 2
        pooled = fused("pooled", lambda *v: pooled_back(towers, devices, True, *v), types, args, 10**10, (me,), tuple(pltpu.VMEM((devices * seqs, t.width), F32) for t in towers), mlp[0] + mlp[1] + list(projs), after)
    else:
        pooled = pooled_back(towers, devices, False, *args)
    pools = (pooled[:8], pooled[8:16])
    loss, scale_grad = pooled[16:]

    early = [early_image, swap_all(then(fronts[1][6], early_image[0], pools[0][0]))]
    backs, late = [], []
    for i in range(2):
        front = fronts[i]
        ahead = pools[i][0] if i == 0 else then(pools[i][0], backs[0][0])
        args = (tokens[i], gains[i], lens[i], lane, ahead, front[1], front[2], front[3], front[4], front[5], attn[i])
        backs.append(call(
            "back_" + names[i],
            lambda ins, outs, tower=towers[i]: back_body(tower, groups, ins, outs),
            back_types(towers[i], groups), args, 10**9, smem=(lane,),
        ))
        late.append(swap_all(then(backs[i][1], early[1][0], *(v[0] for v in late))))

    mixed[0] = mix(0, backs[1][0])
    blocks = [None, None]
    for i in (1, 0):
        types = (shape_of((towers[i].rows, towers[i].width), BF16),)
        after = mixed[0][1] if i == 1 else late[1][0]
        middle = then(mixed[i][0], early[0][1], early[1][1]) if i == 1 else mixed[i][0]
        args = (middle, mixed[i][1], after, mlp[i])
        blocks[i] = call("mlp_" + names[i], lambda ins, outs, tower=towers[i]: mlp_body(tower, ins, outs), types, args, 8 * 10**9, idle=(after,))[0]

    ends = []
    own_q = (attn[0][0], attn[1][0])
    for i, wo in enumerate((image_out, text_out)):
        tower = towers[i]
        args = (pools[i][1], pools[i][2], own_q[i], wo, early[i], late[i], pools[i][6], pools[i][7])
        if small:
            types = (shape_of((3,) + own_q[i].shape[1:], F32), shape_of(wo.shape, F32)) + (shape_of((3, tower.width), F32),) * 2
            ends.append(fused("last_" + names[i], lambda *v, tower=tower: last_step(tower, devices, True, *v), types, args, 10**9))
        else:
            grads, *rest = last_step(tower, devices, False, *args)
            ends.append((jnp.stack(grads), *rest))

    image_qkv_grad = jnp.transpose(jnp.asarray(ends[0][0]), (2, 0, 1))
    text_qkv_grad = jnp.transpose(jnp.asarray(ends[1][0]), (1, 0, 2))
    results = ()
    for i, qkv_grad in enumerate((image_qkv_grad, text_qkv_grad)):
        own, branch, first, up_grad, down_grad, proj_grad, _, _ = pools[i]
        results += (blocks[i], backs[i][0], qkv_grad, ends[i][1], up_grad, down_grad, ends[i][2], ends[i][3], proj_grad)
    return results + (scale_grad.reshape(1), loss.reshape(1))


def solution(mesh):
    towers, batches, tensors = (mesh.shape[a] for a in ("tower", "batch", "tensor"))
    fine = Mesh(mesh.devices.reshape(towers, batches // 2, 2, tensors // 2, 2), ("x", "zh", "zb", "y", "c"))
    rows = P(("x", "zh", "zb", "y", "c"), None)
    lanes = ("y", "c")
    weights = (P(None, None, lanes), P(lanes, None), P(None, lanes), P(lanes, None))
    tower_in = (rows, P(), P()) + weights + (P(),)
    tower_out = (rows, rows) + weights + (P(), P(), P())
    return jax.shard_map(
        per_device,
        mesh=fine,
        in_specs=tower_in + tower_in + (P(("x", "zh", "zb")), P()),
        out_specs=tower_out + tower_out + (P(), P()),
        check_vma=False,
    )
```
